512 devices in a mesh: dp: 32 (over y_hi, z), seqt: 16 (over y_lo, x, core).
Axes of the slice: x: 4, y: 8 (y_hi: 4, y_lo: 2; y = y_hi * 2 + y_lo), z: 8, core: 2. Of those that a mesh axis runs over, the one named last changes fastest.
Arguments:
- latent_tiles: bfloat16 [512, 64, 128], P(('dp', 'seqt')), may hold values from -6 to 6
- tile_route: int32 [512], P(('dp', 'seqt')), may hold values from 0 to 31, as said below
- image_tokens: int32 [32, 2], P('dp'), may hold values from 512 to 1024
- text_lengths: int32 [32, 2], P('dp'), may hold values from 1 to 128
- queries: bfloat16 [65536, 2048], P(('dp', 'seqt')), may hold values from -6 to 6
- key_rows: bfloat16 [65536, 2048], P(('dp', 'seqt')), may hold values from -6 to 6
- values: bfloat16 [65536, 2048], P(('dp', 'seqt')), may hold values from -48 to 48
- text_keys: bfloat16 [8192, 2048], P(('dp', 'seqt')), may hold values from -6 to 6
- text_values: bfloat16 [8192, 2048], P(('dp', 'seqt')), may hold values from -48 to 48
- query_gain: float32 [64], replicated, may hold values from 0.25 to 1.75
- key_gain: float32 [64], replicated, may hold values from 0.25 to 1.75
- residual: bfloat16 [65536, 2432], P(('dp', 'seqt')), may hold values from -6 to 6
- out_weight: bfloat16 [2048, 2432], P('seqt'), may hold values from -0.125 to 0.125
- modulation: float32 [64, 7296], P('dp'), may hold values from -3 to 3
- final_weight: bfloat16 [2432, 64], replicated, may hold values from -0.125 to 0.125
- noise_tiles: bfloat16 [512, 64, 128], P(('dp', 'seqt')), may hold values from -6 to 6
Outputs:
- velocity: float32 [512, 64, 128], P(('dp', 'seqt'))
- attention_grad: bfloat16 [65536, 2048], P(('dp', 'seqt'))
- final_grad: float32 [2432, 64], replicated
- loss_value: float32 [], replicated
The draws below stay inside these ranges and needn't reach their ends.
Inputs may be any that keep to these rules, and one draw needn't show every extreme that they name: `tile_route`: among the tiles of the encoder ranks of one seqt index, every group is named by exactly 1 tiles.
All inputs are finite; a program needn't handle non-finite values.
Results may differ from the reference program's by a relative error of at most 0.0075.
Values may be sent and summed in bfloat16 or wider, within the bound.
No kernel may reach another device: no remote copies, remote signals or barrier semaphores. Data moves between devices by JAX's collectives and lax.ppermute only.
A program may use at most 64 MiB of HBM per device.

```python
import jax
import jax.numpy as jnp
from jax import lax

D = 2432
HEADS = 32
HD = 64
LAT = 64
TILE = 128
IMGS = 2
TILES_DEV = 1
GROUPS = 32
TOK_GRP = 2048
TOKENS = 65536
TXT = 128
TILES_ALL = 512
N_DP = 32
N_SEQT = 16


def draw_tile_route(key, part):
    key = jax.random.fold_in(key, 11)
    column_keys = jax.random.split(key, N_SEQT)
    orders = jax.vmap(lambda single: jax.random.permutation(single, N_DP * TILES_DEV))(column_keys)
    orders = orders.reshape(N_SEQT, N_DP, TILES_DEV).transpose(1, 0, 2)
    return (orders // TILES_DEV).reshape(-1).astype(jnp.int32)


def draw_image_tokens(key, part):
    key = jax.random.fold_in(key, 12)
    first_key, second_key = jax.random.split(key)
    lowest = TOK_GRP // 4
    highest = TOK_GRP // 2
    counts = jax.random.randint(first_key, (GROUPS * IMGS,), lowest, highest + 1)
    chosen = jax.random.randint(second_key, (), 0, GROUPS * IMGS)
    counts = jnp.where(jnp.arange(GROUPS * IMGS) == chosen, highest, counts)
    return counts.reshape(GROUPS, IMGS).astype(jnp.int32)


def draw_text_lengths(key, part):
    key = jax.random.fold_in(key, 13)
    first_key, second_key = jax.random.split(key)
    counts = jax.random.randint(first_key, (GROUPS * IMGS,), 1, TXT + 1)
    chosen = jax.random.randint(second_key, (), 0, GROUPS * IMGS)
    counts = jnp.where(jnp.arange(GROUPS * IMGS) == chosen, TXT, counts)
    return counts.reshape(GROUPS, IMGS).astype(jnp.int32)


def steps_of(rng, dims, cuts, low, top_value):
    level, own = 1.0, jax.random.fold_in(rng, 6)
    for axis_at, shards_of in cuts:
        steps = jnp.exp(jax.random.uniform(jax.random.fold_in(own, axis_at), (shards_of,), jnp.float32, low / len(cuts), top_value / len(cuts)))
        level = level * jnp.repeat(steps, dims[axis_at] // shards_of).reshape([-1 if axis == axis_at else 1 for axis in range(len(dims))])
    return level


def gaussian(own_key, shape, width, bound, pieces=(), kind=jnp.bfloat16):
    loudness = steps_of(own_key, shape, pieces, -0.22, 0.18) if pieces else 1.0
    array = jax.random.normal(own_key, shape, jnp.float32) * width * loudness
    return jnp.minimum(jnp.maximum(array, -bound), bound).astype(kind)


def setup_inputs(seed: int = 0) -> dict:
    key_of = jax.random.split(jax.random.key(seed), 17)
    return {
        "latent_tiles": gaussian(key_of[0], (TILES_ALL, LAT, TILE), 1.0, 6.0, ((0, 512),)),
        "tile_route": draw_tile_route(jax.random.fold_in(key_of[16], 71), 0),
        "image_tokens": draw_image_tokens(jax.random.fold_in(key_of[16], 71), 0),
        "text_lengths": draw_text_lengths(jax.random.fold_in(key_of[16], 71), 0),
        "queries": gaussian(key_of[4], (TOKENS, HEADS * HD), 1.0, 6.0, ((0, 512),)),
        "key_rows": gaussian(key_of[5], (TOKENS, HEADS * HD), 1.0, 6.0, ((0, 512),)),
        "values": gaussian(key_of[6], (TOKENS, HEADS * HD), 8.0, 48.0, ((0, 512),)),
        "text_keys": gaussian(key_of[7], (GROUPS * IMGS * TXT, HEADS * HD), 1.0, 6.0, ((0, 512),)),
        "text_values": gaussian(key_of[8], (GROUPS * IMGS * TXT, HEADS * HD), 8.0, 48.0, ((0, 512),)),
        "query_gain": jnp.clip(1.0 + 0.15 * jax.random.normal(key_of[9], (HD,), jnp.float32), 0.25, 1.75),
        "key_gain": jnp.clip(1.0 + 0.15 * jax.random.normal(key_of[10], (HD,), jnp.float32), 0.25, 1.75),
        "residual": gaussian(key_of[11], (TOKENS, D), 1.0, 6.0, ((0, 512),)),
        "out_weight": gaussian(key_of[12], (HEADS * HD, D), (HEADS * HD) ** -0.5, 0.125, ((0, 16),)),
        "modulation": gaussian(key_of[13], (GROUPS * IMGS, 3 * D), 0.5, 3.0, ((0, 32),), jnp.float32),
        "final_weight": gaussian(key_of[14], (D, LAT), D ** -0.5, 0.125),
        "noise_tiles": gaussian(key_of[15], (TILES_ALL, LAT, TILE), 1.0, 6.0, ((0, 512),)),
    }


EPSILON = 1e-06

def head_norm(rows, gain):
    wide = rows.astype(jnp.float32)
    spread = lax.optimization_barrier(jnp.mean(wide * wide, axis=-1, keepdims=True))
    return (wide * lax.rsqrt(spread + EPSILON) * gain).astype(jnp.bfloat16)

def token_layout(counts, offset, length_rows):
    first_count = counts[0]
    second_count = counts[1]
    border = (first_count + TILE - 1) // TILE * TILE
    places = offset + jnp.arange(length_rows, dtype=jnp.int32)
    owner = (places >= border).astype(jnp.int32)
    usable = (places < first_count) | (places >= border) & (places < border + second_count)
    return (owner, usable)

def text_layout(lengths, text_slots):
    places = jnp.arange(IMGS * text_slots, dtype=jnp.int32)
    owner = places // text_slots
    limit = jnp.where(owner == 0, lengths[0], lengths[1])
    usable = places % text_slots < limit
    return (owner, usable)

def finish_rows(projected, owner, usable, residual_rows, modulate, final_weight, noise_rows, latent_rows, total_count):
    first_image = (owner == 0)[:, None]
    gate_rows = jnp.where(first_image, modulate[0, :D], modulate[1, :D])
    shift_rows = jnp.where(first_image, modulate[0, D:2 * D], modulate[1, D:2 * D])
    scale_rows = jnp.where(first_image, modulate[0, 2 * D:], modulate[1, 2 * D:])
    hidden = residual_rows.astype(jnp.float32) + gate_rows * projected
    average = lax.optimization_barrier(jnp.mean(hidden, axis=-1, keepdims=True))
    centered = hidden - average
    inverse = lax.rsqrt(lax.optimization_barrier(jnp.mean(centered * centered, axis=-1, keepdims=True)) + EPSILON)
    normed = centered * inverse
    mixed = (normed * (1.0 + scale_rows) + shift_rows).astype(jnp.bfloat16)
    velocity = jnp.dot(mixed, final_weight, preferred_element_type=jnp.float32)
    target = noise_rows.astype(jnp.float32) - latent_rows.astype(jnp.float32)
    row_weight = usable.astype(jnp.float32)[:, None]
    error_rows = (velocity - target) * row_weight
    loss_part = jnp.sum(error_rows * error_rows)
    grad_velocity = (error_rows * (2.0 / (total_count * LAT))).astype(jnp.bfloat16)
    final_part = jnp.dot(mixed.T, grad_velocity, preferred_element_type=jnp.float32)
    grad_mixed = jnp.dot(grad_velocity, final_weight.T, preferred_element_type=jnp.float32)
    grad_normed = grad_mixed * (1.0 + scale_rows)
    grad_hidden = inverse * (grad_normed - lax.optimization_barrier(jnp.mean(grad_normed, axis=-1, keepdims=True)) - normed * lax.optimization_barrier(jnp.mean(grad_normed * normed, axis=-1, keepdims=True)))
    grad_projected = (grad_hidden * gate_rows).astype(jnp.bfloat16)
    return (velocity, grad_projected, final_part, loss_part)

def group_attention(query_rows, key_part, value_rows, text_key_part, text_value_part, query_gain, key_gain, counts, lengths):
    query_heads = head_norm(query_rows.reshape(TOK_GRP, HEADS, HD), query_gain)
    key_heads = jnp.concatenate([head_norm(key_part.reshape(TOK_GRP, HEADS, HD), key_gain), head_norm(text_key_part.reshape(IMGS * TXT, HEADS, HD), key_gain)], axis=0)
    value_heads = jnp.concatenate([value_rows.reshape(TOK_GRP, HEADS, HD), text_value_part.reshape(IMGS * TXT, HEADS, HD)], axis=0)
    owner, usable = token_layout(counts, 0, TOK_GRP)
    text_owner, text_usable = text_layout(lengths, TXT)
    key_owner = jnp.concatenate([owner, text_owner])
    key_usable = jnp.concatenate([usable, text_usable])
    allowed = (owner[:, None] == key_owner[None, :]) & key_usable[None, :]

    def one_head(inputs):
        query_head, key_head, value_head = inputs
        scores = jnp.dot(query_head, key_head.T, preferred_element_type=jnp.float32) * HD ** (-0.5)
        scores = jnp.where(allowed, scores, -1e+30)
        largest = lax.optimization_barrier(jnp.max(scores, axis=-1, keepdims=True))
        exponent = jnp.exp(scores - largest)
        weights = (exponent / lax.optimization_barrier(jnp.sum(exponent, axis=-1, keepdims=True))).astype(jnp.bfloat16)
        return jnp.dot(weights, value_head, preferred_element_type=jnp.float32).astype(jnp.bfloat16)
    outputs = lax.map(one_head, (query_heads.transpose(1, 0, 2), key_heads.transpose(1, 0, 2), value_heads.transpose(1, 0, 2)))
    return (outputs.transpose(1, 0, 2).reshape(TOK_GRP, HEADS * HD), owner, usable)

def reference(latent_tiles, tile_route, image_tokens, text_lengths, queries, key_rows, values, text_keys, text_values, query_gain, key_gain, residual, out_weight, modulation, final_weight, noise_tiles):
    route_grid = tile_route.reshape(N_DP, N_SEQT, TILES_DEV).transpose(1, 0, 2).reshape(N_SEQT, N_DP * TILES_DEV)
    group_ids = jnp.arange(N_DP, dtype=jnp.int32)
    hits = (route_grid[:, :, None] == group_ids[None, None, :]).astype(jnp.int32)
    ranked = lax.optimization_barrier(jnp.sum((jnp.cumsum(hits, axis=1) - hits) * hits, axis=2)).astype(jnp.int32)
    column = jnp.arange(N_SEQT, dtype=jnp.int32)[:, None]
    target_tile = ((route_grid * N_SEQT + column) * TILES_DEV + ranked).astype(jnp.int32)
    source_tile = ((group_ids[None, :, None] * N_SEQT + column[:, :, None]) * TILES_DEV + jnp.arange(TILES_DEV, dtype=jnp.int32)[None, None, :]).reshape(N_SEQT, N_DP * TILES_DEV)
    landed = jnp.zeros_like(latent_tiles).at[target_tile.reshape(-1)].set(latent_tiles[source_tile.reshape(-1).astype(jnp.int32)])
    latent_rows = landed.transpose(0, 2, 1).reshape(N_DP, TOK_GRP, LAT)
    noise_rows = noise_tiles.transpose(0, 2, 1).reshape(N_DP, TOK_GRP, LAT)
    total_count = jnp.sum(image_tokens.astype(jnp.float32))

    def one_group(inputs):
        query_rows, key_part, value_rows, text_key_part, text_value_part, residual_rows, modulate, noise_part, latent_part, counts, lengths = inputs
        attention, owner, usable = group_attention(query_rows, key_part, value_rows, text_key_part, text_value_part, query_gain, key_gain, counts, lengths)
        projected = jnp.dot(attention, out_weight, preferred_element_type=jnp.float32)
        velocity, grad_projected, final_part, loss_part = finish_rows(projected, owner, usable, residual_rows, modulate, final_weight, noise_part, latent_part, total_count)
        attention_grad = jnp.dot(grad_projected, out_weight.T, preferred_element_type=jnp.float32).astype(jnp.bfloat16)
        return (velocity, attention_grad, final_part, loss_part)
    velocity, attention_grad, final_parts, loss_parts = lax.map(one_group, (queries.reshape(N_DP, TOK_GRP, HEADS * HD), key_rows.reshape(N_DP, TOK_GRP, HEADS * HD), values.reshape(N_DP, TOK_GRP, HEADS * HD), text_keys.reshape(N_DP, IMGS * TXT, HEADS * HD), text_values.reshape(N_DP, IMGS * TXT, HEADS * HD), residual.reshape(N_DP, TOK_GRP, D), modulation.reshape(N_DP, IMGS, 3 * D), noise_rows, latent_rows, image_tokens, text_lengths))
    velocity = velocity.reshape(TILES_ALL, TILE, LAT).transpose(0, 2, 1)
    attention_grad = attention_grad.reshape(TOKENS, HEADS * HD)
    final_grad = lax.optimization_barrier(jnp.sum(final_parts, axis=0))
    loss_value = jnp.sum(loss_parts) / (total_count * LAT)
    return (velocity, attention_grad, final_grad, loss_value)
```

```python
import functools

import jax
import jax.numpy as jnp
from jax import lax
from jax.experimental import pallas as pl
from jax.experimental.pallas import tpu as pltpu
from jax.sharding import PartitionSpec as P

HD = 64
IMGS = 2
LANES = 128
Q_ROWS = 256
EPSILON = 1e-06
VMEM = pl.BlockSpec(memory_space=pltpu.VMEM)
SMEM = pl.BlockSpec(memory_space=pltpu.SMEM)
NT = (((1,), (1,)), ((), ()))


def params(limit_mib, semantics=None):
    return pltpu.CompilerParams(
        vmem_limit_bytes=limit_mib * 2**20, dimension_semantics=semantics
    )


def pack_kernel(parts, *refs):
    ins, out_ref = refs[:-1], refs[-1]
    block_rows = sum(ref.shape[0] for ref in ins)
    for part in range(parts):
        row = part * block_rows
        for ref in ins:
            rows = ref.shape[0]
            out_ref[row : row + rows, :] = ref[:, part * LANES : (part + 1) * LANES]
            row += rows


def pack(arrays, parts):
    block_rows = sum(array.shape[0] for array in arrays)
    return pl.pallas_call(
        functools.partial(pack_kernel, parts),
        out_shape=jax.ShapeDtypeStruct((parts * block_rows, LANES), arrays[0].dtype),
        in_specs=[VMEM] * len(arrays),
        out_specs=VMEM,
        compiler_params=params(32),
    )(*arrays)


def head_norm(rows, gain, same_head):
    wide = rows.astype(jnp.float32)
    square = wide * wide
    high = square.astype(jnp.bfloat16)
    low = (square - high.astype(jnp.float32)).astype(jnp.bfloat16)
    total = jnp.dot(high, same_head, preferred_element_type=jnp.float32) + jnp.dot(
        low, same_head, preferred_element_type=jnp.float32
    )
    return (wide * lax.rsqrt(total * (1.0 / HD) + EPSILON) * gain).astype(jnp.bfloat16)


def attention_kernel(
    sources, tile, text_rows, counts_ref, lengths_ref, recv_ref, query_gain_ref, key_gain_ref,
    out_ref, query_ref, key_ref, value_ref, window_ref, weigh_ref,
):
    rows_all = sources * tile
    text_slots = sources * text_rows // IMGS
    window = rows_all // IMGS
    block = 3 * tile + 2 * text_rows
    per_image = sources // IMGS
    first_count = counts_ref[0, 0]
    second_count = counts_ref[0, 1]
    border = pl.multiple_of((first_count + tile - 1) // tile * tile, tile)
    head_row = lax.broadcasted_iota(jnp.int32, (LANES, LANES), 0) // HD
    head_column = lax.broadcasted_iota(jnp.int32, (LANES, LANES), 1) // HD
    same_head = (head_row == head_column).astype(jnp.float32).astype(jnp.bfloat16)
    query_gain = query_gain_ref[...]
    key_gain = key_gain_ref[...]
    for source in range(sources):
        at, row = source * block, source * tile
        key = head_norm(recv_ref[at + tile : at + 2 * tile, :], key_gain, same_head)
        key_ref[row : row + tile, :] = key
        if row < window:
            window_ref[0, row : row + tile, :] = key
        value_ref[row : row + tile, :] = recv_ref[at + 2 * tile : at + 3 * tile, :]
        query = head_norm(recv_ref[at : at + tile, :], query_gain, same_head)
        query_ref[row : row + tile, :] = query * jnp.bfloat16(HD**-0.5)
        image, place = source // per_image, window + source % per_image * text_rows
        text = recv_ref[at + 3 * tile : at + 3 * tile + text_rows, :]
        window_ref[image, place : place + text_rows, :] = head_norm(text, key_gain, same_head)
    window_ref[1, :window, :] = key_ref[pl.ds(border, window), :]

    def weighed(values, used, image, start, rows):
        low = lax.broadcasted_iota(jnp.int32, (rows, LANES), 1) < HD
        kept = lax.broadcasted_iota(jnp.int32, (rows, LANES), 0) < used
        wide = jnp.where(kept, values.astype(jnp.float32), 0.0)
        ones = kept.astype(jnp.float32)
        weigh_ref[image, 0, start : start + rows, :] = jnp.where(low, wide, ones).astype(jnp.bfloat16)
        weigh_ref[image, 1, start : start + rows, :] = jnp.where(low, ones, wide).astype(jnp.bfloat16)

    for image in range(IMGS):
        used = counts_ref[0, image]
        for start in range(0, window, tile):
            begin = start if image == 0 else pl.multiple_of(border + start, tile)
            weighed(value_ref[pl.ds(begin, tile), :], used - start, image, start, tile)
        text = jnp.concatenate(
            [
                recv_ref[s * block + 3 * tile + text_rows : (s + 1) * block, :]
                for s in range(image * per_image, (image + 1) * per_image)
            ],
            axis=0,
        )
        weighed(text, lengths_ref[0, image], image, window, text_slots)

    low = lax.broadcasted_iota(jnp.int32, (Q_ROWS, LANES), 1) < HD

    def rows_of(image, start):
        query = query_ref[pl.ds(start, Q_ROWS), :].astype(jnp.float32)
        sums = []
        for head in range(2):
            own = jnp.where(low == (head == 0), query, 0.0).astype(jnp.bfloat16)
            scores = lax.dot_general(own, window_ref[image], NT, preferred_element_type=jnp.float32)
            weights = jnp.exp(scores).astype(jnp.bfloat16)
            sums.append(jnp.dot(weights, weigh_ref[image, head], preferred_element_type=jnp.float32))
        above = jnp.where(low, sums[0], sums[1])
        below = pltpu.roll(jnp.where(low, sums[1], sums[0]), HD, 1)
        out_ref[pl.ds(start, Q_ROWS), :] = (above / below).astype(jnp.bfloat16)

    @pl.loop(0, (border + Q_ROWS - 1) // Q_ROWS)
    def _(step):
        rows_of(0, pl.multiple_of(step * Q_ROWS, tile))

    @pl.loop(0, (rows_all - border + Q_ROWS - 1) // Q_ROWS)
    def _(step):
        rows_of(1, pl.multiple_of(jnp.minimum(border + step * Q_ROWS, rows_all - Q_ROWS), tile))


def attention(recv, counts, lengths, query_gain, key_gain, sources, tile, text_rows):
    rows_all = sources * tile
    keys = rows_all // IMGS + sources * text_rows // IMGS
    twice = lambda gain: jnp.concatenate([gain, gain]).reshape(1, LANES)
    return pl.pallas_call(
        functools.partial(attention_kernel, sources, tile, text_rows),
        out_shape=jax.ShapeDtypeStruct((rows_all, LANES), jnp.bfloat16),
        in_specs=[SMEM, SMEM, VMEM, VMEM, VMEM],
        out_specs=VMEM,
        scratch_shapes=[
            pltpu.VMEM((rows_all, LANES), jnp.bfloat16),
            pltpu.VMEM((rows_all, LANES), jnp.bfloat16),
            pltpu.VMEM((rows_all, LANES), jnp.bfloat16),
            pltpu.VMEM((IMGS, keys, LANES), jnp.bfloat16),
            pltpu.VMEM((IMGS, 2, keys, LANES), jnp.bfloat16),
        ],
        compiler_params=params(48),
    )(counts, lengths, recv, twice(query_gain), twice(key_gain))


def head_kernel(
    steps, layout_ref, total_ref, rows_ref, weight_ref, residual_ref, modulate_ref, final_ref,
    noise_ref, landed_ref, velocity_ref, grad_ref, parts_ref, sum_ref,
):
    step = pl.program_id(0)
    tile, width = residual_ref.shape
    lat = final_ref.shape[0]
    rows = jnp.concatenate([rows_ref[:tile, :], rows_ref[tile:, :]], axis=1)
    product = jnp.dot(rows, weight_ref[...], preferred_element_type=jnp.float32)

    @pl.when(step == 0)
    def _():
        sum_ref[...] = product

    @pl.when(step > 0)
    def _():
        sum_ref[...] += product

    @pl.when(step == steps - 1)
    def _():
        first = layout_ref[0] == 0
        pick = lambda at: jnp.where(
            first,
            modulate_ref[0:1, at * width : (at + 1) * width],
            modulate_ref[1:2, at * width : (at + 1) * width],
        )
        gate, shift, scale = pick(0), pick(1), 1.0 + pick(2)
        mean = lambda array: jnp.sum(array, axis=-1, keepdims=True) * (1.0 / width)
        hidden = residual_ref[...].astype(jnp.float32) + gate * sum_ref[...]
        centered = hidden - mean(hidden)
        inverse = lax.rsqrt(mean(centered * centered) + EPSILON)
        normed = centered * inverse
        mixed = (normed * scale + shift).astype(jnp.bfloat16)
        velocity = lax.dot_general(final_ref[...], mixed, NT, preferred_element_type=jnp.float32)
        velocity_ref[...] = velocity
        target = noise_ref[...].astype(jnp.float32) - landed_ref[...].astype(jnp.float32)
        used = lax.broadcasted_iota(jnp.int32, (lat, tile), 1) < layout_ref[1]
        error = jnp.where(used, velocity - target, 0.0)
        grad_wide = error * (2.0 / (total_ref[0] * lat))
        grad_columns = grad_wide.astype(jnp.bfloat16)
        final_part = jnp.dot(grad_columns, mixed, preferred_element_type=jnp.float32)
        for at in range(width // LANES):
            parts_ref[at] = final_part[:, at * LANES : (at + 1) * LANES]
        parts_ref[width // LANES] = jnp.full((lat, LANES), jnp.sum(error * error))
        grad_rows = grad_wide.T.astype(jnp.bfloat16)
        grad_normed = jnp.dot(grad_rows, final_ref[...], preferred_element_type=jnp.float32) * scale
        grad_hidden = inverse * (
            grad_normed - mean(grad_normed) - normed * mean(grad_normed * normed)
        )
        grad_ref[...] = (grad_hidden * gate).astype(jnp.bfloat16)


def head(layout, total, recv, weight, residual, modulate, final_columns, noise, landed):
    tile, width = residual.shape
    lat = final_columns.shape[0]
    depth = 2 * LANES
    steps = weight.shape[0] // depth
    blocks = width // LANES + 1
    whole = lambda array: pl.BlockSpec(array.shape, lambda i: (0,) * array.ndim)
    return pl.pallas_call(
        functools.partial(head_kernel, steps),
        grid=(steps,),
        out_shape=(
            jax.ShapeDtypeStruct((lat, tile), jnp.float32),
            jax.ShapeDtypeStruct((tile, width), jnp.bfloat16),
            jax.ShapeDtypeStruct((blocks, lat, LANES), jnp.float32),
        ),
        in_specs=[
            SMEM,
            SMEM,
            pl.BlockSpec((2 * tile, LANES), lambda i: (i, 0)),
            pl.BlockSpec((depth, width), lambda i: (i, 0)),
            whole(residual),
            whole(modulate),
            whole(final_columns),
            whole(noise),
            whole(landed),
        ],
        out_specs=(
            pl.BlockSpec((lat, tile), lambda i: (0, 0)),
            pl.BlockSpec((tile, width), lambda i: (0, 0)),
            pl.BlockSpec((blocks, lat, LANES), lambda i: (0, 0, 0)),
        ),
        scratch_shapes=[pltpu.VMEM((tile, width), jnp.float32)],
        compiler_params=params(48, ("arbitrary",)),
    )(layout, total, recv, weight, residual, modulate, final_columns, noise, landed)


def back_kernel(grad_ref, weight_ref, out_ref):
    out_ref[...] = lax.dot_general(
        grad_ref[...], weight_ref[...], NT, preferred_element_type=jnp.float32
    ).astype(jnp.bfloat16)


def back(grad, weight):
    tile, width = grad.shape
    depth = 2 * LANES
    return pl.pallas_call(
        back_kernel,
        grid=(weight.shape[0] // depth,),
        out_shape=jax.ShapeDtypeStruct((tile, weight.shape[0]), jnp.bfloat16),
        in_specs=[
            pl.BlockSpec((tile, width), lambda i: (0, 0)),
            pl.BlockSpec((depth, width), lambda i: (i, 0)),
        ],
        out_specs=pl.BlockSpec((tile, depth), lambda i: (0, i)),
        compiler_params=params(32, ("arbitrary",)),
        cost_estimate=pl.CostEstimate(
            flops=2 * tile * width * weight.shape[0],
            bytes_accessed=2 * width * weight.shape[0],
            transcendentals=0,
        ),
    )(grad, weight)


def unpack_kernel(parts_ref, out_ref):
    for at in range(out_ref.shape[1] // LANES):
        out_ref[:, at * LANES : (at + 1) * LANES] = parts_ref[at]


def unpack(parts, width):
    return pl.pallas_call(
        unpack_kernel,
        out_shape=jax.ShapeDtypeStruct((parts.shape[1], width), jnp.float32),
        in_specs=[VMEM],
        out_specs=VMEM,
        compiler_params=params(32),
    )(parts)


def exchange(array, axis, groups=None):
    return lax.all_to_all(
        array, axis, split_axis=0, concat_axis=0, axis_index_groups=groups, tiled=True
    )


def digits(value, base, rows, lanes):
    places = lax.broadcasted_iota(jnp.int32, (rows, lanes), 0)
    return jnp.where(places == 1, value // base, jnp.where(places == 2, value % base, 0))


def route_near(tile, destination, count, near, groups):
    lat, lanes = tile.shape
    slots = jnp.arange(near, dtype=jnp.int32)[:, None, None]
    hit = destination % near == slots
    notes = digits(count, 16, 16, lanes)[None]
    first = lax.broadcasted_iota(jnp.int32, notes.shape, 1) == 0
    notes = jnp.where(first, jnp.where(hit, destination // near + 1, 0), notes)
    data = jnp.where(hit, tile[None], jnp.zeros_like(tile)[None])
    sent = jnp.concatenate([data, notes.astype(jnp.bfloat16)], axis=1)
    return exchange(sent, "dp", groups)


def route_far(recv, near, far, lat, groups):
    notes = recv[:, lat : lat + 3, 0].astype(jnp.float32).astype(jnp.int32)
    count = jnp.sum(notes[:, 1] * 16 + notes[:, 2])
    slots = jnp.arange(far, dtype=jnp.int32)[:, None]
    hit = (notes[:, 0][None, :] == slots + 1)[:, :, None, None]
    data = jnp.where(hit, recv[None, :, :lat].astype(jnp.float32), 0.0)
    data = jnp.sum(data, axis=1).astype(jnp.bfloat16)
    more = digits(count, 128, 16, recv.shape[2])[None].astype(jnp.bfloat16)
    sent = jnp.concatenate([data, jnp.broadcast_to(more, (far, *more.shape[1:]))], axis=1)
    recv = exchange(sent, "dp", groups)
    landed = jnp.sum(recv[:, :lat].astype(jnp.float32), axis=0).astype(jnp.bfloat16)
    notes = recv[:, lat : lat + 3, 0].astype(jnp.float32)
    return landed, jnp.sum(notes[:, 1] * 128.0 + notes[:, 2])


def sum_over(array, axis, count, groups=None):
    spread = jnp.broadcast_to(array[None], (count, *array.shape))
    return jnp.sum(exchange(spread, axis, groups), axis=0)


def per_device(
    near, latent_tiles, tile_route, image_tokens, text_lengths, queries, key_rows, values,
    text_keys, text_values, query_gain, key_gain, residual, out_weight, modulation, final_weight,
    noise_tiles,
):
    lat_width, tile = latent_tiles.shape[1:]
    rows_here, width = residual.shape
    text_rows = text_keys.shape[0]
    ranks, sources = lax.axis_size("dp"), lax.axis_size("seqt")
    far = ranks // near
    near_groups = [[row * near + at for at in range(near)] for row in range(far)]
    far_groups = [[row * near + at for row in range(far)] for at in range(near)]
    column_index = lax.axis_index("seqt")

    gathered = lax.all_gather(out_weight, "seqt", axis=0, tiled=True)
    sent = pack((queries, key_rows, values, text_keys, text_values), sources)
    recv = exchange(sent, "seqt")
    latent, route, counts, recv = lax.optimization_barrier(
        (latent_tiles, tile_route, image_tokens, recv)
    )
    near_recv = route_near(latent[0], route[0], jnp.sum(counts[0]), near, near_groups)
    heads = attention(
        recv, image_tokens, text_lengths, query_gain, key_gain, sources, tile, text_rows
    )
    heads, near_recv = lax.optimization_barrier((heads, near_recv))
    attended = exchange(heads, "seqt")
    attended, near_recv = lax.optimization_barrier((attended, near_recv))
    landed, total_count = route_far(near_recv, near, far, lat_width, far_groups)

    first_count, second_count = image_tokens[0, 0], image_tokens[0, 1]
    border = (first_count + tile - 1) // tile * tile
    place = column_index * rows_here
    owner = (place >= border).astype(jnp.int32)
    used = jnp.where(owner == 0, first_count, border + second_count) - place
    velocity, grad_projected, parts = head(
        jnp.stack([owner, used]).astype(jnp.int32), total_count.reshape(1), attended, gathered,
        residual, modulation, final_weight.T, noise_tiles[0], landed,
    )
    attention_grad = back(grad_projected, gathered)

    blocks = parts.shape[0]
    mine = exchange(parts.reshape(blocks * lat_width, LANES), "seqt")
    mine = jnp.sum(mine.reshape(sources, blocks * lat_width // sources, LANES), axis=0)
    mine = sum_over(mine, "dp", near, near_groups)
    mine = sum_over(mine, "dp", far, far_groups)
    spread = jnp.broadcast_to(mine[None], (sources, *mine.shape))
    sums = exchange(spread, "seqt").reshape(blocks, lat_width, LANES)
    final_grad = unpack(sums, width).T
    loss_value = sums[blocks - 1, 0, 0] / (total_count * lat_width)
    return velocity[None], attention_grad, final_grad, loss_value


def solution(mesh):
    both = P(("dp", "seqt"), None)
    tiles = P(("dp", "seqt"), None, None)
    placed = (
        tiles, P(("dp", "seqt")), P("dp", None), P("dp", None), both, both, both, both, both,
        P(), P(), both, P("seqt", None), P("dp", None), P(), tiles,
    )
    near = 8 if mesh.shape["dp"] % 8 == 0 else mesh.shape["dp"]
    return jax.shard_map(
        functools.partial(per_device, near),
        mesh=mesh,
        in_specs=placed,
        out_specs=(tiles, both, P(), P()),
        check_vma=False,
    )
```

```python
import functools

import jax
import jax.numpy as jnp
from jax import lax
from jax.experimental import pallas as pl
from jax.experimental.pallas import tpu as pltpu
from jax.sharding import PartitionSpec as P

HD = 64
IMGS = 2
LANES = 128
Q_ROWS = 256
NOTES = 16
EPSILON = 1e-06
HBM = pl.BlockSpec(memory_space=pltpu.HBM)
VMEM = pl.BlockSpec(memory_space=pltpu.VMEM)
SMEM = pl.BlockSpec(memory_space=pltpu.SMEM)
NT = (((1,), (1,)), ((), ()))


def params(limit_mib, semantics=None):
    return pltpu.CompilerParams(
        vmem_limit_bytes=limit_mib * 2**20, dimension_semantics=semantics
    )


def pack_kernel(parts, count, route_ref, counts_ref, tile_ref, *refs):
    ins, out_ref, tagged_ref, semaphore = refs[:count], refs[count], refs[count + 1], refs[count + 2]
    block_rows = sum(ref.shape[0] for ref in ins)
    for part in range(parts):
        row = part * block_rows
        for ref in ins:
            rows = ref.shape[0]
            pltpu.make_async_copy(
                ref.at[:, pl.ds(part * LANES, LANES)], out_ref.at[pl.ds(row, rows), :], semaphore
            ).start()
            row += rows
    lat = tile_ref.shape[1]
    tokens = counts_ref[0, 0] + counts_ref[0, 1]
    tagged_ref[:lat, :] = tile_ref[0]
    tagged_ref[lat:, :] = notes(route_ref[0], tokens // 16, tokens % 16)
    pltpu.make_async_copy(out_ref, out_ref, semaphore).wait()


def notes(first, second, third):
    places = lax.broadcasted_iota(jnp.int32, (NOTES, LANES), 0)
    third_or_none = jnp.where(places == 2, third, 0)
    numbers = jnp.where(places == 0, first, jnp.where(places == 1, second, third_or_none))
    return numbers.astype(jnp.float32).astype(jnp.bfloat16)


def pack(arrays, parts, tile, route, counts):
    block_rows = sum(array.shape[0] for array in arrays)
    return pl.pallas_call(
        functools.partial(pack_kernel, parts, len(arrays)),
        out_shape=(
            jax.ShapeDtypeStruct((parts * block_rows, LANES), arrays[0].dtype),
            jax.ShapeDtypeStruct((tile.shape[1] + NOTES, LANES), tile.dtype),
        ),
        in_specs=[SMEM, SMEM, VMEM] + [HBM] * len(arrays),
        out_specs=(HBM, VMEM),
        scratch_shapes=[pltpu.SemaphoreType.DMA],
        compiler_params=params(60),
    )(route, counts, tile, *arrays)


def select_kernel(me_ref, *refs):
    ins, out_ref = refs[:-1], refs[-1]
    rows = out_ref.shape[0] // 2
    lat = rows - NOTES
    tokens = jnp.zeros((1, 1), jnp.float32)
    mine = jnp.zeros((lat, LANES), jnp.float32)
    other = jnp.zeros((lat, LANES), jnp.float32)
    me = me_ref[0].astype(jnp.float32)
    beside = (me_ref[0] ^ 1).astype(jnp.float32)
    for ref in ins:
        for at in range(0, ref.shape[0], rows):
            tile = ref[at : at + lat, :].astype(jnp.float32)
            note = ref[at + lat : at + rows, :].astype(jnp.float32)
            route = note[0:1, 0:1]
            mine += jnp.where(route == me, tile, 0.0)
            other += jnp.where(route == beside, tile, 0.0)
            tokens += note[1:2, 0:1] * 16.0 + note[2:3, 0:1]
    high = jnp.floor(tokens * (1.0 / 128.0))
    places = lax.broadcasted_iota(jnp.int32, (NOTES, LANES), 0)
    number = jnp.where(places == 1, high, jnp.where(places == 2, tokens - high * 128.0, 0.0))
    for half, tile in enumerate((mine, other)):
        out_ref[half * rows : half * rows + lat, :] = tile.astype(jnp.bfloat16)
        out_ref[half * rows + lat : (half + 1) * rows, :] = number.astype(jnp.bfloat16)


def land(tagged, ranks):
    held = [tagged]
    step = ranks // 2
    while step > 1:
        have = held[0] if len(held) == 1 else jnp.concatenate(held, axis=0)
        held = [have, swap(have, ranks, step)]
        step //= 2
    rows = tagged.shape[0]
    chosen = pl.pallas_call(
        select_kernel,
        out_shape=jax.ShapeDtypeStruct((2 * rows, LANES), tagged.dtype),
        in_specs=[SMEM] + [VMEM] * len(held),
        out_specs=VMEM,
        compiler_params=params(32),
    )(lax.axis_index("dp").astype(jnp.int32).reshape(1), *held)
    mine, other = chosen[:rows], chosen[rows:]
    return mine, swap(other, ranks, 1) if ranks > 1 else jnp.zeros_like(other)


def swap(array, ranks, step):
    return lax.ppermute(array, "dp", [(rank, rank ^ step) for rank in range(ranks)])


def head_norm(rows, gain, same_head):
    wide = rows.astype(jnp.float32)
    square = wide * wide
    high = square.astype(jnp.bfloat16)
    low = (square - high.astype(jnp.float32)).astype(jnp.bfloat16)
    total = jnp.dot(high, same_head, preferred_element_type=jnp.float32) + jnp.dot(
        low, same_head, preferred_element_type=jnp.float32
    )
    return (wide * lax.rsqrt(total * (1.0 / HD) + EPSILON) * gain).astype(jnp.bfloat16)


def attention_kernel(
    sources, tile, text_rows, counts_ref, lengths_ref, recv_ref, query_gain_ref, key_gain_ref,
    out_ref, query_ref, key_ref, value_ref, window_ref, weigh_ref,
):
    rows_all = sources * tile
    text_slots = sources * text_rows // IMGS
    window = rows_all // IMGS
    block = 3 * tile + 2 * text_rows
    per_image = sources // IMGS
    first_count = counts_ref[0, 0]
    second_count = counts_ref[0, 1]
    border = pl.multiple_of((first_count + tile - 1) // tile * tile, tile)
    head_row = lax.broadcasted_iota(jnp.int32, (LANES, LANES), 0) // HD
    head_column = lax.broadcasted_iota(jnp.int32, (LANES, LANES), 1) // HD
    same_head = (head_row == head_column).astype(jnp.float32).astype(jnp.bfloat16)
    query_gain = query_gain_ref[...]
    key_gain = key_gain_ref[...]
    for source in range(sources):
        at, row = source * block, source * tile
        key = head_norm(recv_ref[at + tile : at + 2 * tile, :], key_gain, same_head)
        key_ref[row : row + tile, :] = key
        if row < window:
            window_ref[0, row : row + tile, :] = key
        value_ref[row : row + tile, :] = recv_ref[at + 2 * tile : at + 3 * tile, :]
        query = head_norm(recv_ref[at : at + tile, :], query_gain, same_head)
        query_ref[row : row + tile, :] = query * jnp.bfloat16(HD**-0.5)
        image, place = source // per_image, window + source % per_image * text_rows
        text = recv_ref[at + 3 * tile : at + 3 * tile + text_rows, :]
        window_ref[image, place : place + text_rows, :] = head_norm(text, key_gain, same_head)
    window_ref[1, :window, :] = key_ref[pl.ds(border, window), :]

    def weighed(values, used, image, start, rows):
        low = lax.broadcasted_iota(jnp.int32, (rows, LANES), 1) < HD
        kept = lax.broadcasted_iota(jnp.int32, (rows, LANES), 0) < used
        wide = jnp.where(kept, values.astype(jnp.float32), 0.0)
        ones = kept.astype(jnp.float32)
        weigh_ref[image, 0, start : start + rows, :] = jnp.where(low, wide, ones).astype(jnp.bfloat16)
        weigh_ref[image, 1, start : start + rows, :] = jnp.where(low, ones, wide).astype(jnp.bfloat16)

    for image in range(IMGS):
        used = counts_ref[0, image]
        for start in range(0, window, tile):
            begin = start if image == 0 else pl.multiple_of(border + start, tile)
            weighed(value_ref[pl.ds(begin, tile), :], used - start, image, start, tile)
        text = jnp.concatenate(
            [
                recv_ref[s * block + 3 * tile + text_rows : (s + 1) * block, :]
                for s in range(image * per_image, (image + 1) * per_image)
            ],
            axis=0,
        )
        weighed(text, lengths_ref[0, image], image, window, text_slots)

    low = lax.broadcasted_iota(jnp.int32, (Q_ROWS, LANES), 1) < HD

    def rows_of(image, start):
        query = query_ref[pl.ds(start, Q_ROWS), :].astype(jnp.float32)
        sums = []
        for head in range(2):
            own = jnp.where(low == (head == 0), query, 0.0).astype(jnp.bfloat16)
            scores = lax.dot_general(own, window_ref[image], NT, preferred_element_type=jnp.float32)
            weights = jnp.exp(scores).astype(jnp.bfloat16)
            sums.append(jnp.dot(weights, weigh_ref[image, head], preferred_element_type=jnp.float32))
        above = jnp.where(low, sums[0], sums[1])
        below = pltpu.roll(jnp.where(low, sums[1], sums[0]), HD, 1)
        out_ref[pl.ds(start, Q_ROWS), :] = (above / below).astype(jnp.bfloat16)

    @pl.loop(0, (border + Q_ROWS - 1) // Q_ROWS)
    def _(step):
        rows_of(0, pl.multiple_of(step * Q_ROWS, tile))

    @pl.loop(0, (rows_all - border + Q_ROWS - 1) // Q_ROWS)
    def _(step):
        rows_of(1, pl.multiple_of(jnp.minimum(border + step * Q_ROWS, rows_all - Q_ROWS), tile))


def attention(recv, counts, lengths, query_gain, key_gain, sources, tile, text_rows):
    rows_all = sources * tile
    keys = rows_all // IMGS + sources * text_rows // IMGS
    twice = lambda gain: jnp.concatenate([gain, gain]).reshape(1, LANES)
    return pl.pallas_call(
        functools.partial(attention_kernel, sources, tile, text_rows),
        out_shape=jax.ShapeDtypeStruct((rows_all, LANES), jnp.bfloat16),
        in_specs=[SMEM, SMEM, VMEM, VMEM, VMEM],
        out_specs=VMEM,
        scratch_shapes=[
            pltpu.VMEM((rows_all, LANES), jnp.bfloat16),
            pltpu.VMEM((rows_all, LANES), jnp.bfloat16),
            pltpu.VMEM((rows_all, LANES), jnp.bfloat16),
            pltpu.VMEM((IMGS, keys, LANES), jnp.bfloat16),
            pltpu.VMEM((IMGS, 2, keys, LANES), jnp.bfloat16),
        ],
        compiler_params=params(48),
    )(counts, lengths, recv, twice(query_gain), twice(key_gain))


def thirds(number, row):
    high = number.astype(jnp.bfloat16).astype(jnp.float32)
    middle = (number - high).astype(jnp.bfloat16).astype(jnp.float32)
    low = number - high - middle
    rest = jnp.where(row == 1, middle, jnp.where(row == 2, low, 0.0))
    return jnp.where(row == 0, high, rest).astype(jnp.bfloat16)


def head_kernel(
    steps, place_ref, counts_ref, rows_ref, weight_ref, residual_ref, modulate_ref, final_ref,
    noise_ref, near_ref, far_ref, velocity_ref, grad_ref, parts_ref, total_ref, sum_ref,
):
    step = pl.program_id(0)
    tile, width = residual_ref.shape
    lat = final_ref.shape[0]
    rows = jnp.concatenate([rows_ref[:tile, :], rows_ref[tile:, :]], axis=1)
    product = jnp.dot(rows, weight_ref[...], preferred_element_type=jnp.float32)

    @pl.when(step == 0)
    def _():
        sum_ref[...] = product

    @pl.when(step > 0)
    def _():
        sum_ref[...] += product

    @pl.when(step == steps - 1)
    def _():
        place = place_ref[0] * tile
        border = (counts_ref[0, 0] + tile - 1) // tile * tile
        first = place < border
        used_rows = jnp.where(first, counts_ref[0, 0], border + counts_ref[0, 1]) - place
        total = jnp.zeros((1, 1), jnp.float32)
        for ref in (near_ref, far_ref):
            note = ref[lat:, :].astype(jnp.float32)
            total += note[1:2, 0:1] * 128.0 + note[2:3, 0:1]
        total_ref[...] = jnp.broadcast_to(total, total_ref.shape)
        pick = lambda at: jnp.where(
            first,
            modulate_ref[0:1, at * width : (at + 1) * width],
            modulate_ref[1:2, at * width : (at + 1) * width],
        )
        gate, shift, scale = pick(0), pick(1), 1.0 + pick(2)
        mean = lambda array: jnp.sum(array, axis=-1, keepdims=True) * (1.0 / width)
        hidden = residual_ref[...].astype(jnp.float32) + gate * sum_ref[...]
        centered = hidden - mean(hidden)
        inverse = lax.rsqrt(mean(centered * centered) + EPSILON)
        normed = centered * inverse
        mixed = (normed * scale + shift).astype(jnp.bfloat16)
        velocity = lax.dot_general(final_ref[...], mixed, NT, preferred_element_type=jnp.float32)
        velocity_ref[...] = velocity
        landed = near_ref[:lat, :].astype(jnp.float32) + far_ref[:lat, :].astype(jnp.float32)
        target = noise_ref[...].astype(jnp.float32) - landed
        used = lax.broadcasted_iota(jnp.int32, (lat, tile), 1) < used_rows
        error = jnp.where(used, velocity - target, 0.0)
        grad_wide = error * (2.0 / (total * lat))
        grad_columns = grad_wide.astype(jnp.bfloat16)
        final_part = jnp.dot(grad_columns, mixed, preferred_element_type=jnp.float32)
        for at in range(width // LANES):
            parts_ref[at] = final_part[:, at * LANES : (at + 1) * LANES].astype(jnp.bfloat16)
        squares = jnp.sum(error * error, axis=(0, 1), keepdims=True)
        parts_ref[width // LANES] = thirds(squares, lax.broadcasted_iota(jnp.int32, (lat, LANES), 0))
        grad_rows = grad_wide.T.astype(jnp.bfloat16)
        grad_normed = jnp.dot(grad_rows, final_ref[...], preferred_element_type=jnp.float32) * scale
        grad_hidden = inverse * (
            grad_normed - mean(grad_normed) - normed * mean(grad_normed * normed)
        )
        grad_ref[...] = (grad_hidden * gate).astype(jnp.bfloat16)


def head(place, counts, recv, weight, residual, modulate, final_columns, noise, near, far):
    tile, width = residual.shape
    lat = final_columns.shape[0]
    depth = 2 * LANES
    steps = weight.shape[0] // depth
    blocks = width // LANES + 1
    whole = lambda array: pl.BlockSpec(array.shape, lambda i: (0,) * array.ndim)
    return pl.pallas_call(
        functools.partial(head_kernel, steps),
        grid=(steps,),
        out_shape=(
            jax.ShapeDtypeStruct((lat, tile), jnp.float32),
            jax.ShapeDtypeStruct((tile, width), jnp.bfloat16),
            jax.ShapeDtypeStruct((blocks, lat, LANES), jnp.bfloat16),
            jax.ShapeDtypeStruct((8, LANES), jnp.float32),
        ),
        in_specs=[
            SMEM,
            SMEM,
            pl.BlockSpec((2 * tile, LANES), lambda i: (i, 0)),
            pl.BlockSpec((depth, width), lambda i: (i, 0)),
            whole(residual),
            whole(modulate),
            whole(final_columns),
            whole(noise),
            whole(near),
            whole(far),
        ],
        out_specs=(
            pl.BlockSpec((lat, tile), lambda i: (0, 0)),
            pl.BlockSpec((tile, width), lambda i: (0, 0)),
            pl.BlockSpec((blocks, lat, LANES), lambda i: (0, 0, 0)),
            pl.BlockSpec((8, LANES), lambda i: (0, 0)),
        ),
        scratch_shapes=[pltpu.VMEM((tile, width), jnp.float32)],
        compiler_params=params(48, ("arbitrary",)),
    )(place, counts, recv, weight, residual, modulate, final_columns, noise, near, far)


def back_kernel(grad_ref, weight_ref, out_ref):
    out_ref[...] = lax.dot_general(
        grad_ref[...], weight_ref[...], NT, preferred_element_type=jnp.float32
    ).astype(jnp.bfloat16)


def back(grad, weight):
    tile, width = grad.shape
    depth = 2 * LANES
    return pl.pallas_call(
        back_kernel,
        grid=(weight.shape[0] // depth,),
        out_shape=jax.ShapeDtypeStruct((tile, weight.shape[0]), jnp.bfloat16),
        in_specs=[
            pl.BlockSpec((tile, width), lambda i: (0, 0)),
            pl.BlockSpec((depth, width), lambda i: (i, 0)),
        ],
        out_specs=pl.BlockSpec((tile, depth), lambda i: (0, i)),
        compiler_params=params(32, ("arbitrary",)),
        cost_estimate=pl.CostEstimate(
            flops=2 * tile * width * weight.shape[0],
            bytes_accessed=2 * width * weight.shape[0],
            transcendentals=0,
        ),
    )(grad, weight)


def sum_kernel(ranks, loss_row, last_ref, recv_ref, out_ref):
    rows = out_ref.shape[1]
    total = recv_ref[:rows, :].astype(jnp.float32)
    for rank in range(1, ranks):
        total += recv_ref[rank * rows : (rank + 1) * rows, :].astype(jnp.float32)
    loss = total[loss_row : loss_row + 1] + total[loss_row + 1 : loss_row + 2] + total[loss_row + 2 : loss_row + 3]
    row = lax.broadcasted_iota(jnp.int32, (rows, LANES), 0) - loss_row
    kept = thirds(loss, row)
    inside = jnp.logical_and(row >= 0, row < 3)
    changed = jnp.where(inside, kept.astype(jnp.float32), total)
    result = jnp.where(last_ref[0] == 1, changed, total).astype(jnp.bfloat16)
    for rank in range(out_ref.shape[0]):
        out_ref[rank] = result


def sum_out(recv, ranks, copies, loss_row, last):
    rows = recv.shape[0] // ranks
    result = pl.pallas_call(
        functools.partial(sum_kernel, ranks, loss_row),
        out_shape=jax.ShapeDtypeStruct((copies, rows, LANES), jnp.bfloat16),
        in_specs=[SMEM, VMEM],
        out_specs=VMEM,
        compiler_params=params(32),
    )(last, recv)
    return result.reshape(copies * rows, LANES)


def unpack_kernel(parts_ref, total_ref, out_ref, loss_ref):
    blocks, lat = parts_ref.shape[:2]
    for at in range(blocks - 1):
        out_ref[:, at * LANES : (at + 1) * LANES] = parts_ref[at].astype(jnp.float32)
    last = parts_ref[blocks - 1, :16, :].astype(jnp.float32)
    loss = last[0:1] + last[1:2] + last[2:3]
    loss_ref[...] = jnp.broadcast_to(loss, loss_ref.shape) / (total_ref[...] * lat)


def unpack(parts, total, width):
    return pl.pallas_call(
        unpack_kernel,
        out_shape=(
            jax.ShapeDtypeStruct((parts.shape[1], width), jnp.float32),
            jax.ShapeDtypeStruct((8, LANES), jnp.float32),
        ),
        in_specs=[VMEM, VMEM],
        out_specs=(VMEM, VMEM),
        compiler_params=params(32),
    )(parts, total)


def exchange(array, axis, groups=None):
    return lax.all_to_all(
        array, axis, split_axis=0, concat_axis=0, axis_index_groups=groups, tiled=True
    )


def per_device(
    near, latent_tiles, tile_route, image_tokens, text_lengths, queries, key_rows, values,
    text_keys, text_values, query_gain, key_gain, residual, out_weight, modulation, final_weight,
    noise_tiles,
):
    lat_width, tile = latent_tiles.shape[1:]
    rows_here, width = residual.shape
    text_rows = text_keys.shape[0]
    ranks, sources = lax.axis_size("dp"), lax.axis_size("seqt")
    far = ranks // near
    near_groups = [[row * near + at for at in range(near)] for row in range(far)]
    far_groups = [[row * near + at for row in range(far)] for at in range(near)]
    column_index = lax.axis_index("seqt").astype(jnp.int32)

    gathered = lax.all_gather(out_weight, "seqt", axis=0, tiled=True)
    sent, tagged = pack(
        (queries, key_rows, values, text_keys, text_values), sources, latent_tiles, tile_route, image_tokens
    )
    recv = exchange(sent, "seqt")
    mine, other = land(tagged, ranks)
    recv, mine, other = lax.optimization_barrier((recv, mine, other))
    heads = attention(
        recv, image_tokens, text_lengths, query_gain, key_gain, sources, tile, text_rows
    )
    attended = exchange(heads, "seqt")
    velocity, grad_projected, parts, total = head(
        column_index.reshape(1), image_tokens, attended, gathered, residual, modulation,
        final_weight.T, noise_tiles[0], mine, other,
    )
    attention_grad = back(grad_projected, gathered)

    blocks = parts.shape[0]
    share = blocks * lat_width // sources
    loss_row = (blocks - 1) * lat_width - (sources - 1) * share
    last = (column_index == sources - 1).astype(jnp.int32).reshape(1)
    sums = exchange(parts.reshape(blocks * lat_width, LANES), "seqt")
    sums = exchange(sum_out(sums, sources, near, loss_row, last), "dp", near_groups)
    sums = exchange(sum_out(sums, near, far, loss_row, last), "dp", far_groups)
    sums = exchange(sum_out(sums, far, sources, loss_row, last), "seqt")
    final_columns, loss = unpack(sums.reshape(blocks, lat_width, LANES), total, width)
    return velocity[None], attention_grad, final_columns.T, loss[0, 0]


def solution(mesh):
    both = P(("dp", "seqt"), None)
    tiles = P(("dp", "seqt"), None, None)
    placed = (
        tiles, P(("dp", "seqt")), P("dp", None), P("dp", None), both, both, both, both, both,
        P(), P(), both, P("seqt", None), P("dp", None), P(), tiles,
    )
    near = 8 if mesh.shape["dp"] % 8 == 0 else mesh.shape["dp"]
    return jax.shard_map(
        functools.partial(per_device, near),
        mesh=mesh,
        in_specs=placed,
        out_specs=(tiles, both, P(), P()),
        check_vma=False,
    )
```

```python
import functools

import jax
import jax.numpy as jnp
from jax import lax
from jax.experimental import pallas as pl
from jax.experimental.pallas import tpu as pltpu
from jax.sharding import PartitionSpec as P

HD = 64
IMGS = 2
LANES = 128
Q_ROWS = 256
NOTES = 16
EPSILON = 1e-06
HBM = pl.BlockSpec(memory_space=pltpu.HBM)
VMEM = pl.BlockSpec(memory_space=pltpu.VMEM)
SMEM = pl.BlockSpec(memory_space=pltpu.SMEM)
NT = (((1,), (1,)), ((), ()))


def params(limit_mib, semantics=None):
    return pltpu.CompilerParams(
        vmem_limit_bytes=limit_mib * 2**20, dimension_semantics=semantics
    )


def pack_kernel(parts, count, route_ref, counts_ref, tile_ref, *refs):
    ins, out_ref, tagged_ref, semaphore = refs[:count], refs[count], refs[count + 1], refs[count + 2]
    block_rows = sum(ref.shape[0] for ref in ins)
    for part in range(parts):
        row = part * block_rows
        for ref in ins:
            rows = ref.shape[0]
            pltpu.make_async_copy(
                ref.at[:, pl.ds(part * LANES, LANES)], out_ref.at[pl.ds(row, rows), :], semaphore
            ).start()
            row += rows
    lat = tile_ref.shape[1]
    tokens = counts_ref[0, 0] + counts_ref[0, 1]
    tagged_ref[:lat, :] = tile_ref[0]
    tagged_ref[lat:, :] = notes(route_ref[0], tokens // 16, tokens % 16)
    pltpu.make_async_copy(out_ref, out_ref, semaphore).wait()


def notes(first, second, third):
    places = lax.broadcasted_iota(jnp.int32, (NOTES, LANES), 0)
    third_or_none = jnp.where(places == 2, third, 0)
    numbers = jnp.where(places == 0, first, jnp.where(places == 1, second, third_or_none))
    return numbers.astype(jnp.float32).astype(jnp.bfloat16)


def pack(arrays, parts, tile, route, counts):
    block_rows = sum(array.shape[0] for array in arrays)
    return pl.pallas_call(
        functools.partial(pack_kernel, parts, len(arrays)),
        out_shape=(
            jax.ShapeDtypeStruct((parts * block_rows, LANES), arrays[0].dtype),
            jax.ShapeDtypeStruct((tile.shape[1] + NOTES, LANES), tile.dtype),
        ),
        in_specs=[SMEM, SMEM, VMEM] + [HBM] * len(arrays),
        out_specs=(VMEM, VMEM),
        scratch_shapes=[pltpu.SemaphoreType.DMA],
        compiler_params=params(60),
    )(route, counts, tile, *arrays)


def select_kernel(last, me_ref, *refs):
    ins, out_ref = refs[:-1], refs[-1]
    rows = out_ref.shape[1]
    lat = rows - NOTES
    tokens = jnp.zeros((1, 1), jnp.float32)
    mine = jnp.zeros((lat, LANES), jnp.float32)
    other = jnp.zeros((lat, LANES), jnp.float32)
    me = me_ref[0].astype(jnp.float32)
    beside = (me_ref[0] ^ last).astype(jnp.float32)
    for ref in ins:
        for at in range(0, ref.shape[0], rows):
            tile = ref[at : at + lat, :].astype(jnp.float32)
            note = ref[at + lat : at + rows, :].astype(jnp.float32)
            route = note[0:1, 0:1]
            mine += jnp.where(route == me, tile, 0.0)
            other += jnp.where(route == beside, tile, 0.0)
            tokens += note[1:2, 0:1] * 16.0 + note[2:3, 0:1]
    high = jnp.floor(tokens * (1.0 / 128.0))
    places = lax.broadcasted_iota(jnp.int32, (NOTES, LANES), 0)
    number = jnp.where(places == 1, high, jnp.where(places == 2, tokens - high * 128.0, 0.0))
    for half, tile in enumerate((mine, other)):
        out_ref[half, :lat, :] = tile.astype(jnp.bfloat16)
        out_ref[half, lat:, :] = number.astype(jnp.bfloat16)


def gather(held, ranks, bits):
    for bit in bits:
        held = jnp.concatenate([held, swap(held, ranks, bit)], axis=0)
    return held


def land(held, rows, ranks):
    bit = max(ranks // 2, 1)
    chosen = pl.pallas_call(
        functools.partial(select_kernel, bit),
        out_shape=jax.ShapeDtypeStruct((2, rows, LANES), held.dtype),
        in_specs=[SMEM, VMEM],
        out_specs=VMEM,
        compiler_params=params(32),
    )(lax.axis_index("dp").astype(jnp.int32).reshape(1), held)
    return chosen[0], swap(chosen[1], ranks, bit) if bit < ranks else jnp.zeros_like(chosen[1])


def swap(array, ranks, step):
    return lax.ppermute(array, "dp", [(rank, rank ^ step) for rank in range(ranks)])


def head_norm(rows, gain, same_head):
    wide = rows.astype(jnp.float32)
    square = wide * wide
    high = square.astype(jnp.bfloat16)
    low = (square - high.astype(jnp.float32)).astype(jnp.bfloat16)
    total = jnp.dot(high, same_head, preferred_element_type=jnp.float32) + jnp.dot(
        low, same_head, preferred_element_type=jnp.float32
    )
    return (wide * lax.rsqrt(total * (1.0 / HD) + EPSILON) * gain).astype(jnp.bfloat16)


def attention_kernel(
    sources, tile, text_rows, counts_ref, lengths_ref, recv_ref, query_gain_ref, key_gain_ref,
    out_ref, query_ref, key_ref, value_ref, window_ref, weigh_ref,
):
    rows_all = sources * tile
    text_slots = sources * text_rows // IMGS
    window = rows_all // IMGS
    block = 3 * tile + 2 * text_rows
    per_image = sources // IMGS
    first_count = counts_ref[0, 0]
    second_count = counts_ref[0, 1]
    border = pl.multiple_of((first_count + tile - 1) // tile * tile, tile)
    head_row = lax.broadcasted_iota(jnp.int32, (LANES, LANES), 0) // HD
    head_column = lax.broadcasted_iota(jnp.int32, (LANES, LANES), 1) // HD
    same_head = (head_row == head_column).astype(jnp.float32).astype(jnp.bfloat16)
    query_gain = query_gain_ref[...]
    key_gain = key_gain_ref[...]
    for source in range(sources):
        at, row = source * block, source * tile
        key = head_norm(recv_ref[at + tile : at + 2 * tile, :], key_gain, same_head)
        key_ref[row : row + tile, :] = key
        if row < window:
            window_ref[0, row : row + tile, :] = key
        value_ref[row : row + tile, :] = recv_ref[at + 2 * tile : at + 3 * tile, :]
        query = head_norm(recv_ref[at : at + tile, :], query_gain, same_head)
        query_ref[row : row + tile, :] = query * jnp.bfloat16(HD**-0.5)
        image, place = source // per_image, window + source % per_image * text_rows
        text = recv_ref[at + 3 * tile : at + 3 * tile + text_rows, :]
        window_ref[image, place : place + text_rows, :] = head_norm(text, key_gain, same_head)
    window_ref[1, :window, :] = key_ref[pl.ds(border, window), :]

    def weighed(values, used, image, start, rows):
        low = lax.broadcasted_iota(jnp.int32, (rows, LANES), 1) < HD
        kept = lax.broadcasted_iota(jnp.int32, (rows, LANES), 0) < used
        wide = jnp.where(kept, values.astype(jnp.float32), 0.0)
        ones = kept.astype(jnp.float32)
        weigh_ref[image, 0, start : start + rows, :] = jnp.where(low, wide, ones).astype(jnp.bfloat16)
        weigh_ref[image, 1, start : start + rows, :] = jnp.where(low, ones, wide).astype(jnp.bfloat16)

    for image in range(IMGS):
        used = counts_ref[0, image]
        for start in range(0, window, tile):
            begin = start if image == 0 else pl.multiple_of(border + start, tile)
            weighed(value_ref[pl.ds(begin, tile), :], used - start, image, start, tile)
        text = jnp.concatenate(
            [
                recv_ref[s * block + 3 * tile + text_rows : (s + 1) * block, :]
                for s in range(image * per_image, (image + 1) * per_image)
            ],
            axis=0,
        )
        weighed(text, lengths_ref[0, image], image, window, text_slots)

    low = lax.broadcasted_iota(jnp.int32, (Q_ROWS, LANES), 1) < HD

    def rows_of(image, start):
        query = query_ref[pl.ds(start, Q_ROWS), :].astype(jnp.float32)
        sums = []
        for head in range(2):
            own = jnp.where(low == (head == 0), query, 0.0).astype(jnp.bfloat16)
            scores = lax.dot_general(own, window_ref[image], NT, preferred_element_type=jnp.float32)
            weights = jnp.exp(scores).astype(jnp.bfloat16)
            sums.append(jnp.dot(weights, weigh_ref[image, head], preferred_element_type=jnp.float32))
        above = jnp.where(low, sums[0], sums[1])
        below = pltpu.roll(jnp.where(low, sums[1], sums[0]), HD, 1)
        out_ref[pl.ds(start, Q_ROWS), :] = (above / below).astype(jnp.bfloat16)

    @pl.loop(0, (border + Q_ROWS - 1) // Q_ROWS)
    def _(step):
        rows_of(0, pl.multiple_of(step * Q_ROWS, tile))

    @pl.loop(0, (rows_all - border + Q_ROWS - 1) // Q_ROWS)
    def _(step):
        rows_of(1, pl.multiple_of(jnp.minimum(border + step * Q_ROWS, rows_all - Q_ROWS), tile))


def attention(recv, counts, lengths, query_gain, key_gain, sources, tile, text_rows):
    rows_all = sources * tile
    keys = rows_all // IMGS + sources * text_rows // IMGS
    twice = lambda gain: jnp.concatenate([gain, gain]).reshape(1, LANES)
    return pl.pallas_call(
        functools.partial(attention_kernel, sources, tile, text_rows),
        out_shape=jax.ShapeDtypeStruct((rows_all, LANES), jnp.bfloat16),
        in_specs=[SMEM, SMEM, VMEM, VMEM, VMEM],
        out_specs=VMEM,
        scratch_shapes=[
            pltpu.VMEM((rows_all, LANES), jnp.bfloat16),
            pltpu.VMEM((rows_all, LANES), jnp.bfloat16),
            pltpu.VMEM((rows_all, LANES), jnp.bfloat16),
            pltpu.VMEM((IMGS, keys, LANES), jnp.bfloat16),
            pltpu.VMEM((IMGS, 2, keys, LANES), jnp.bfloat16),
        ],
        compiler_params=params(48),
        cost_estimate=pl.CostEstimate(
            flops=16 * rows_all * keys * LANES,
            bytes_accessed=4 * rows_all * LANES * 4,
            transcendentals=2 * rows_all * keys,
        ),
    )(counts, lengths, recv, twice(query_gain), twice(key_gain))


def thirds(number, row):
    high = number.astype(jnp.bfloat16).astype(jnp.float32)
    middle = (number - high).astype(jnp.bfloat16).astype(jnp.float32)
    low = number - high - middle
    rest = jnp.where(row == 1, middle, jnp.where(row == 2, low, 0.0))
    return jnp.where(row == 0, high, rest).astype(jnp.bfloat16)


def head_kernel(
    steps, place_ref, counts_ref, rows_ref, weight_ref, residual_ref, modulate_ref, final_ref,
    noise_ref, near_ref, far_ref, velocity_ref, grad_ref, parts_ref, total_ref, sum_ref,
):
    step = pl.program_id(0)
    tile, width = residual_ref.shape
    lat = final_ref.shape[0]
    rows = jnp.concatenate([rows_ref[:tile, :], rows_ref[tile:, :]], axis=1)
    product = jnp.dot(rows, weight_ref[...], preferred_element_type=jnp.float32)

    @pl.when(step == 0)
    def _():
        sum_ref[...] = product

    @pl.when(step > 0)
    def _():
        sum_ref[...] += product

    @pl.when(step == steps - 1)
    def _():
        place = place_ref[0] * tile
        border = (counts_ref[0, 0] + tile - 1) // tile * tile
        first = place < border
        used_rows = jnp.where(first, counts_ref[0, 0], border + counts_ref[0, 1]) - place
        total = jnp.zeros((1, 1), jnp.float32)
        for ref in (near_ref, far_ref):
            note = ref[lat:, :].astype(jnp.float32)
            total += note[1:2, 0:1] * 128.0 + note[2:3, 0:1]
        total_ref[...] = jnp.broadcast_to(total, total_ref.shape)
        pick = lambda at: jnp.where(
            first,
            modulate_ref[0:1, at * width : (at + 1) * width],
            modulate_ref[1:2, at * width : (at + 1) * width],
        )
        gate, shift, scale = pick(0), pick(1), 1.0 + pick(2)
        mean = lambda array: jnp.sum(array, axis=-1, keepdims=True) * (1.0 / width)
        hidden = residual_ref[...].astype(jnp.float32) + gate * sum_ref[...]
        centered = hidden - mean(hidden)
        inverse = lax.rsqrt(mean(centered * centered) + EPSILON)
        normed = centered * inverse
        mixed = (normed * scale + shift).astype(jnp.bfloat16)
        velocity = lax.dot_general(final_ref[...], mixed, NT, preferred_element_type=jnp.float32)
        velocity_ref[...] = velocity
        landed = near_ref[:lat, :].astype(jnp.float32) + far_ref[:lat, :].astype(jnp.float32)
        target = noise_ref[...].astype(jnp.float32) - landed
        used = lax.broadcasted_iota(jnp.int32, (lat, tile), 1) < used_rows
        error = jnp.where(used, velocity - target, 0.0)
        grad_wide = error * (2.0 / (total * lat))
        grad_columns = grad_wide.astype(jnp.bfloat16)
        final_part = jnp.dot(grad_columns, mixed, preferred_element_type=jnp.float32)
        for at in range(width // LANES):
            parts_ref[at] = final_part[:, at * LANES : (at + 1) * LANES].astype(jnp.bfloat16)
        squares = jnp.sum(error * error, axis=(0, 1), keepdims=True)
        parts_ref[width // LANES] = thirds(squares, lax.broadcasted_iota(jnp.int32, (lat, LANES), 0))
        grad_rows = grad_wide.T.astype(jnp.bfloat16)
        grad_normed = jnp.dot(grad_rows, final_ref[...], preferred_element_type=jnp.float32) * scale
        grad_hidden = inverse * (
            grad_normed - mean(grad_normed) - normed * mean(grad_normed * normed)
        )
        grad_ref[...] = (grad_hidden * gate).astype(jnp.bfloat16)


def head(place, counts, recv, weight, residual, modulate, final_columns, noise, near, far):
    tile, width = residual.shape
    lat = final_columns.shape[0]
    depth = 2 * LANES
    steps = weight.shape[0] // depth
    blocks = width // LANES + 1
    whole = lambda array: pl.BlockSpec(array.shape, lambda i: (0,) * array.ndim)
    return pl.pallas_call(
        functools.partial(head_kernel, steps),
        grid=(steps,),
        out_shape=(
            jax.ShapeDtypeStruct((lat, tile), jnp.float32),
            jax.ShapeDtypeStruct((tile, width), jnp.bfloat16),
            jax.ShapeDtypeStruct((blocks, lat, LANES), jnp.bfloat16),
            jax.ShapeDtypeStruct((8, LANES), jnp.float32),
        ),
        in_specs=[
            SMEM,
            SMEM,
            pl.BlockSpec((2 * tile, LANES), lambda i: (i, 0)),
            pl.BlockSpec((depth, width), lambda i: (i, 0)),
            whole(residual),
            whole(modulate),
            whole(final_columns),
            whole(noise),
            whole(near),
            whole(far),
        ],
        out_specs=(
            pl.BlockSpec((lat, tile), lambda i: (0, 0)),
            pl.BlockSpec((tile, width), lambda i: (0, 0)),
            pl.BlockSpec((blocks, lat, LANES), lambda i: (0, 0, 0)),
            pl.BlockSpec((8, LANES), lambda i: (0, 0)),
        ),
        scratch_shapes=[pltpu.VMEM((tile, width), jnp.float32)],
        compiler_params=params(48, ("arbitrary",)),
    )(place, counts, recv, weight, residual, modulate, final_columns, noise, near, far)


def back_kernel(grad_ref, weight_ref, out_ref):
    out_ref[...] = lax.dot_general(
        grad_ref[...], weight_ref[...], NT, preferred_element_type=jnp.float32
    ).astype(jnp.bfloat16)


def back(grad, weight):
    tile, width = grad.shape
    depth = 2 * LANES
    return pl.pallas_call(
        back_kernel,
        grid=(weight.shape[0] // depth,),
        out_shape=jax.ShapeDtypeStruct((tile, weight.shape[0]), jnp.bfloat16),
        in_specs=[
            pl.BlockSpec((tile, width), lambda i: (0, 0)),
            pl.BlockSpec((depth, width), lambda i: (i, 0)),
        ],
        out_specs=pl.BlockSpec((tile, depth), lambda i: (0, i)),
        compiler_params=params(32, ("arbitrary",)),
        cost_estimate=pl.CostEstimate(
            flops=2 * tile * width * weight.shape[0],
            bytes_accessed=2 * width * weight.shape[0],
            transcendentals=0,
        ),
    )(grad, weight)


def sum_kernel(ranks, loss_row, last_ref, recv_ref, out_ref):
    rows = out_ref.shape[1]
    total = recv_ref[:rows, :].astype(jnp.float32)
    for rank in range(1, ranks):
        total += recv_ref[rank * rows : (rank + 1) * rows, :].astype(jnp.float32)
    loss = total[loss_row : loss_row + 1] + total[loss_row + 1 : loss_row + 2] + total[loss_row + 2 : loss_row + 3]
    row = lax.broadcasted_iota(jnp.int32, (rows, LANES), 0) - loss_row
    kept = thirds(loss, row)
    inside = jnp.logical_and(row >= 0, row < 3)
    changed = jnp.where(inside, kept.astype(jnp.float32), total)
    result = jnp.where(last_ref[0] == 1, changed, total).astype(jnp.bfloat16)
    for rank in range(out_ref.shape[0]):
        out_ref[rank] = result


def sum_out(recv, ranks, copies, loss_row, last):
    rows = recv.shape[0] // ranks
    result = pl.pallas_call(
        functools.partial(sum_kernel, ranks, loss_row),
        out_shape=jax.ShapeDtypeStruct((copies, rows, LANES), jnp.bfloat16),
        in_specs=[SMEM, VMEM],
        out_specs=VMEM,
        compiler_params=params(32),
    )(last, recv)
    return result.reshape(copies * rows, LANES)


def unpack_kernel(parts_ref, total_ref, out_ref, loss_ref):
    blocks, lat = parts_ref.shape[:2]
    for at in range(blocks - 1):
        out_ref[:, at * LANES : (at + 1) * LANES] = parts_ref[at].astype(jnp.float32)
    last = parts_ref[blocks - 1, :16, :].astype(jnp.float32)
    loss = last[0:1] + last[1:2] + last[2:3]
    loss_ref[...] = jnp.broadcast_to(loss, loss_ref.shape) / (total_ref[...] * lat)


def unpack(parts, total, width):
    return pl.pallas_call(
        unpack_kernel,
        out_shape=(
            jax.ShapeDtypeStruct((parts.shape[1], width), jnp.float32),
            jax.ShapeDtypeStruct((8, LANES), jnp.float32),
        ),
        in_specs=[VMEM, VMEM],
        out_specs=(VMEM, VMEM),
        compiler_params=params(32),
    )(parts, total)


def exchange(array, axis, groups=None):
    return lax.all_to_all(
        array, axis, split_axis=0, concat_axis=0, axis_index_groups=groups, tiled=True
    )


def per_device(
    near, latent_tiles, tile_route, image_tokens, text_lengths, queries, key_rows, values,
    text_keys, text_values, query_gain, key_gain, residual, out_weight, modulation, final_weight,
    noise_tiles,
):
    lat_width, tile = latent_tiles.shape[1:]
    rows_here, width = residual.shape
    text_rows = text_keys.shape[0]
    ranks, sources = lax.axis_size("dp"), lax.axis_size("seqt")
    far = ranks // near
    near_groups = [[row * near + at for at in range(near)] for row in range(far)]
    far_groups = [[row * near + at for row in range(far)] for at in range(near)]
    column_index = lax.axis_index("seqt").astype(jnp.int32)

    gathered = lax.all_gather(out_weight, "seqt", axis=0, tiled=True)
    sent, tagged = pack(
        (queries, key_rows, values, text_keys, text_values), sources, latent_tiles, tile_route, image_tokens
    )
    recv = exchange(sent, "seqt")
    bits = [1 << at for at in range(ranks.bit_length() - 1)]
    held = gather(tagged, ranks, [bit for bit in reversed(bits) if bit < near])
    recv, held = lax.optimization_barrier((recv, held))
    held = gather(held, ranks, [bit for bit in bits[:-1] if bit >= near])
    heads = attention(
        recv, image_tokens, text_lengths, query_gain, key_gain, sources, tile, text_rows
    )
    heads, held = lax.optimization_barrier((heads, held))
    attended = exchange(heads, "seqt")
    mine, other = land(held, tagged.shape[0], ranks)
    velocity, grad_projected, parts, total = head(
        column_index.reshape(1), image_tokens, attended, gathered, residual, modulation,
        final_weight.T, noise_tiles[0], mine, other,
    )
    attention_grad = back(grad_projected, gathered)

    blocks = parts.shape[0]
    share = blocks * lat_width // sources
    loss_row = (blocks - 1) * lat_width - (sources - 1) * share
    last = (column_index == sources - 1).astype(jnp.int32).reshape(1)
    sums = exchange(parts.reshape(blocks * lat_width, LANES), "seqt")
    sums = exchange(sum_out(sums, sources, near, loss_row, last), "dp", near_groups)
    sums = exchange(sum_out(sums, near, far, loss_row, last), "dp", far_groups)
    sums = exchange(sum_out(sums, far, sources, loss_row, last), "seqt")
    final_columns, loss = unpack(sums.reshape(blocks, lat_width, LANES), total, width)
    return velocity[None], attention_grad, final_columns.T, loss[0, 0]


def solution(mesh):
    both = P(("dp", "seqt"), None)
    tiles = P(("dp", "seqt"), None, None)
    placed = (
        tiles, P(("dp", "seqt")), P("dp", None), P("dp", None), both, both, both, both, both,
        P(), P(), both, P("seqt", None), P("dp", None), P(), tiles,
    )
    near = 8 if mesh.shape["dp"] % 8 == 0 else mesh.shape["dp"]
    return jax.shard_map(
        functools.partial(per_device, near),
        mesh=mesh,
        in_specs=placed,
        out_specs=(tiles, both, P(), P()),
        check_vma=False,
    )
```

```python
import functools

import jax
import jax.numpy as jnp
from jax import lax
from jax.experimental import pallas as pl
from jax.experimental.pallas import tpu as pltpu
from jax.sharding import PartitionSpec as P

HD = 64
IMGS = 2
LANES = 128
Q_ROWS = 256
NOTES = 16
EPSILON = 1e-06
HBM = pl.BlockSpec(memory_space=pltpu.HBM)
VMEM = pl.BlockSpec(memory_space=pltpu.VMEM)
SMEM = pl.BlockSpec(memory_space=pltpu.SMEM)
NT = (((1,), (1,)), ((), ()))


def params(limit_mib, semantics=None):
    return pltpu.CompilerParams(
        vmem_limit_bytes=limit_mib * 2**20, dimension_semantics=semantics
    )


def pack_kernel(parts, count, route_ref, counts_ref, tile_ref, *refs):
    ins, out_ref, tagged_ref, semaphore = refs[:count], refs[count], refs[count + 1], refs[count + 2]
    block_rows = sum(ref.shape[0] for ref in ins)
    for part in range(parts):
        row = part * block_rows
        for ref in ins:
            rows = ref.shape[0]
            pltpu.make_async_copy(
                ref.at[:, pl.ds(part * LANES, LANES)], out_ref.at[pl.ds(row, rows), :], semaphore
            ).start()
            row += rows
    lat = tile_ref.shape[1]
    tokens = counts_ref[0, 0] + counts_ref[0, 1]
    tagged_ref[:lat, :] = tile_ref[0]
    tagged_ref[lat:, :] = notes(route_ref[0], tokens // 16, tokens % 16)
    pltpu.make_async_copy(out_ref, out_ref, semaphore).wait()


def notes(first, second, third):
    places = lax.broadcasted_iota(jnp.int32, (NOTES, LANES), 0)
    third_or_none = jnp.where(places == 2, third, 0)
    numbers = jnp.where(places == 0, first, jnp.where(places == 1, second, third_or_none))
    return numbers.astype(jnp.float32).astype(jnp.bfloat16)


def pack(arrays, parts, tile, route, counts):
    block_rows = sum(array.shape[0] for array in arrays)
    return pl.pallas_call(
        functools.partial(pack_kernel, parts, len(arrays)),
        out_shape=(
            jax.ShapeDtypeStruct((parts * block_rows, LANES), arrays[0].dtype),
            jax.ShapeDtypeStruct((tile.shape[1] + NOTES, LANES), tile.dtype),
        ),
        in_specs=[SMEM, SMEM, VMEM] + [HBM] * len(arrays),
        out_specs=(VMEM, VMEM),
        scratch_shapes=[pltpu.SemaphoreType.DMA],
        compiler_params=params(60),
    )(route, counts, tile, *arrays)


def select_kernel(last, me_ref, *refs):
    ins, out_ref = refs[:-1], refs[-1]
    rows = out_ref.shape[1]
    lat = rows - NOTES
    tokens = jnp.zeros((1, 1), jnp.float32)
    mine = jnp.zeros((lat, LANES), jnp.float32)
    other = jnp.zeros((lat, LANES), jnp.float32)
    me = me_ref[0].astype(jnp.float32)
    beside = (me_ref[0] ^ last).astype(jnp.float32)
    for ref in ins:
        for at in range(0, ref.shape[0], rows):
            tile = ref[at : at + lat, :].astype(jnp.float32)
            note = ref[at + lat : at + rows, :].astype(jnp.float32)
            route = note[0:1, 0:1]
            mine += jnp.where(route == me, tile, 0.0)
            other += jnp.where(route == beside, tile, 0.0)
            tokens += note[1:2, 0:1] * 16.0 + note[2:3, 0:1]
    high = jnp.floor(tokens * (1.0 / 128.0))
    places = lax.broadcasted_iota(jnp.int32, (NOTES, LANES), 0)
    number = jnp.where(places == 1, high, jnp.where(places == 2, tokens - high * 128.0, 0.0))
    for half, tile in enumerate((mine, other)):
        out_ref[half, :lat, :] = tile.astype(jnp.bfloat16)
        out_ref[half, lat:, :] = number.astype(jnp.bfloat16)


def gather(held, ranks, bits):
    for bit in bits:
        held = jnp.concatenate([held, swap(held, ranks, bit)], axis=0)
    return held


def land(held, rows, ranks):
    bit = max(ranks // 2, 1)
    chosen = pl.pallas_call(
        functools.partial(select_kernel, bit),
        out_shape=jax.ShapeDtypeStruct((2, rows, LANES), held.dtype),
        in_specs=[SMEM, VMEM],
        out_specs=VMEM,
        compiler_params=params(16),
    )(lax.axis_index("dp").astype(jnp.int32).reshape(1), held)
    return chosen[0], swap(chosen[1], ranks, bit) if bit < ranks else jnp.zeros_like(chosen[1])


def swap(array, ranks, step, axis="dp"):
    return lax.ppermute(array, axis, [(rank, rank ^ step) for rank in range(ranks)])


def head_norm(rows, gain, same_head):
    wide = rows.astype(jnp.float32)
    square = wide * wide
    high = square.astype(jnp.bfloat16)
    low = (square - high.astype(jnp.float32)).astype(jnp.bfloat16)
    total = jnp.dot(high, same_head, preferred_element_type=jnp.float32) + jnp.dot(
        low, same_head, preferred_element_type=jnp.float32
    )
    return (wide * lax.rsqrt(total * (1.0 / HD) + EPSILON) * gain).astype(jnp.bfloat16)


def attention_kernel(
    sources, tile, text_rows, counts_ref, lengths_ref, recv_ref, query_gain_ref, key_gain_ref,
    out_ref, query_ref, key_ref, value_ref, window_ref, weigh_ref,
):
    rows_all = sources * tile
    text_slots = sources * text_rows // IMGS
    window = rows_all // IMGS
    block = 3 * tile + 2 * text_rows
    per_image = sources // IMGS
    first_count = counts_ref[0, 0]
    second_count = counts_ref[0, 1]
    border = pl.multiple_of((first_count + tile - 1) // tile * tile, tile)
    head_row = lax.broadcasted_iota(jnp.int32, (LANES, LANES), 0) // HD
    head_column = lax.broadcasted_iota(jnp.int32, (LANES, LANES), 1) // HD
    same_head = (head_row == head_column).astype(jnp.float32).astype(jnp.bfloat16)
    query_gain = query_gain_ref[...]
    key_gain = key_gain_ref[...]
    for source in range(sources):
        at, row = source * block, source * tile
        key = head_norm(recv_ref[at + tile : at + 2 * tile, :], key_gain, same_head)
        key_ref[row : row + tile, :] = key
        if row < window:
            window_ref[0, row : row + tile, :] = key
        value_ref[row : row + tile, :] = recv_ref[at + 2 * tile : at + 3 * tile, :]
        query = head_norm(recv_ref[at : at + tile, :], query_gain, same_head)
        query_ref[row : row + tile, :] = query * jnp.bfloat16(HD**-0.5)
        image, place = source // per_image, window + source % per_image * text_rows
        text = recv_ref[at + 3 * tile : at + 3 * tile + text_rows, :]
        window_ref[image, place : place + text_rows, :] = head_norm(text, key_gain, same_head)
    window_ref[1, :window, :] = key_ref[pl.ds(border, window), :]

    def weighed(values, used, image, start, rows):
        low = lax.broadcasted_iota(jnp.int32, (rows, LANES), 1) < HD
        kept = lax.broadcasted_iota(jnp.int32, (rows, LANES), 0) < used
        wide = jnp.where(kept, values.astype(jnp.float32), 0.0)
        ones = kept.astype(jnp.float32)
        weigh_ref[image, 0, start : start + rows, :] = jnp.where(low, wide, ones).astype(jnp.bfloat16)
        weigh_ref[image, 1, start : start + rows, :] = jnp.where(low, ones, wide).astype(jnp.bfloat16)

    for image in range(IMGS):
        used = counts_ref[0, image]
        for start in range(0, window, tile):
            begin = start if image == 0 else pl.multiple_of(border + start, tile)
            weighed(value_ref[pl.ds(begin, tile), :], used - start, image, start, tile)
        text = jnp.concatenate(
            [
                recv_ref[s * block + 3 * tile + text_rows : (s + 1) * block, :]
                for s in range(image * per_image, (image + 1) * per_image)
            ],
            axis=0,
        )
        weighed(text, lengths_ref[0, image], image, window, text_slots)

    low = lax.broadcasted_iota(jnp.int32, (Q_ROWS, LANES), 1) < HD

    def rows_of(image, start):
        query = query_ref[pl.ds(start, Q_ROWS), :].astype(jnp.float32)
        sums = []
        for head in range(2):
            own = jnp.where(low == (head == 0), query, 0.0).astype(jnp.bfloat16)
            scores = lax.dot_general(own, window_ref[image], NT, preferred_element_type=jnp.float32)
            weights = jnp.exp(scores).astype(jnp.bfloat16)
            sums.append(jnp.dot(weights, weigh_ref[image, head], preferred_element_type=jnp.float32))
        above = jnp.where(low, sums[0], sums[1])
        below = pltpu.roll(jnp.where(low, sums[1], sums[0]), HD, 1)
        result = (above / below).astype(jnp.bfloat16)
        for part in range(Q_ROWS // tile):
            at = start // tile + part
            place = (lax.rem(at, per_image) * IMGS + lax.div(at, per_image)) * tile
            out_ref[pl.ds(pl.multiple_of(place, tile), tile), :] = result[part * tile : (part + 1) * tile]

    @pl.loop(0, (border + Q_ROWS - 1) // Q_ROWS)
    def _(step):
        rows_of(0, pl.multiple_of(step * Q_ROWS, tile))

    @pl.loop(0, (rows_all - border + Q_ROWS - 1) // Q_ROWS)
    def _(step):
        rows_of(1, pl.multiple_of(jnp.minimum(border + step * Q_ROWS, rows_all - Q_ROWS), tile))


def attention(recv, counts, lengths, query_gain, key_gain, sources, tile, text_rows):
    rows_all = sources * tile
    keys = rows_all // IMGS + sources * text_rows // IMGS
    twice = lambda gain: jnp.concatenate([gain, gain]).reshape(1, LANES)
    return pl.pallas_call(
        functools.partial(attention_kernel, sources, tile, text_rows),
        out_shape=jax.ShapeDtypeStruct((rows_all, LANES), jnp.bfloat16),
        in_specs=[SMEM, SMEM, VMEM, VMEM, VMEM],
        out_specs=VMEM,
        scratch_shapes=[
            pltpu.VMEM((rows_all, LANES), jnp.bfloat16),
            pltpu.VMEM((rows_all, LANES), jnp.bfloat16),
            pltpu.VMEM((rows_all, LANES), jnp.bfloat16),
            pltpu.VMEM((IMGS, keys, LANES), jnp.bfloat16),
            pltpu.VMEM((IMGS, 2, keys, LANES), jnp.bfloat16),
        ],
        compiler_params=params(32),
        cost_estimate=pl.CostEstimate(
            flops=16 * rows_all * keys * LANES,
            bytes_accessed=4 * rows_all * LANES * 4,
            transcendentals=2 * rows_all * keys,
        ),
    )(counts, lengths, recv, twice(query_gain), twice(key_gain))


def thirds(number, row):
    high = number.astype(jnp.bfloat16).astype(jnp.float32)
    middle = (number - high).astype(jnp.bfloat16).astype(jnp.float32)
    low = number - high - middle
    rest = jnp.where(row == 1, middle, jnp.where(row == 2, low, 0.0))
    return jnp.where(row == 0, high, rest).astype(jnp.bfloat16)


def pick_rows(first, modulate_ref, at, width):
    columns = pl.ds(at * width, width)
    return jnp.where(first, modulate_ref[0:1, columns], modulate_ref[1:2, columns])


def row_mean(array):
    return jnp.sum(array, axis=-1, keepdims=True) * (1.0 / array.shape[1])


def layout(place_ref, counts_ref, tile):
    place = place_ref[0] * tile
    border = (counts_ref[0, 0] + tile - 1) // tile * tile
    first = place < border
    return first, jnp.where(first, counts_ref[0, 0], border + counts_ref[0, 1]) - place


def project_kernel(steps, half_ref, rows_ref, weight_ref, own_ref, other_ref, sum_ref):
    step = pl.program_id(0)
    tile = own_ref.shape[0]
    rows = jnp.concatenate([rows_ref[: 2 * tile, :], rows_ref[2 * tile :, :]], axis=1)
    product = jnp.dot(rows, weight_ref[...], preferred_element_type=jnp.float32)

    @pl.when(step == 0)
    def _():
        sum_ref[...] = product

    @pl.when(step > 0)
    def _():
        sum_ref[...] += product

    @pl.when(step == steps - 1)
    def _():
        for half in range(2):

            @pl.when(half_ref[0] == half)
            def _():
                own_ref[...] = sum_ref[half * tile : (half + 1) * tile, :]
                other = sum_ref[(1 - half) * tile : (2 - half) * tile, :]
                other_ref[...] = other.astype(jnp.bfloat16)


def project(half, recv, weight, tile):
    depth = 2 * LANES
    steps = weight.shape[0] // depth
    width = weight.shape[1]
    return pl.pallas_call(
        functools.partial(project_kernel, steps),
        grid=(steps,),
        out_shape=(
            jax.ShapeDtypeStruct((tile, width), jnp.float32),
            jax.ShapeDtypeStruct((tile, width), jnp.bfloat16),
        ),
        in_specs=[
            SMEM,
            pl.BlockSpec((4 * tile, LANES), lambda i: (i, 0)),
            pl.BlockSpec((depth, width), lambda i: (i, 0)),
        ],
        out_specs=(VMEM, VMEM),
        scratch_shapes=[pltpu.VMEM((2 * tile, width), jnp.float32)],
        compiler_params=params(52, ("arbitrary",)),
    )(half, recv, weight)


def head_kernel(
    place_ref, counts_ref, own_ref, other_ref, residual_ref, modulate_ref, final_ref, noise_ref,
    near_ref, far_ref, velocity_ref, parts_ref, total_ref, normed_ref, inverse_ref, grad_ref,
):
    tile, width = residual_ref.shape
    lat = final_ref.shape[0]
    first, used_rows = layout(place_ref, counts_ref, tile)
    total = jnp.zeros((1, 1), jnp.float32)
    for ref in (near_ref, far_ref):
        note = ref[lat:, :].astype(jnp.float32)
        total += note[1:2, 0:1] * 128.0 + note[2:3, 0:1]
    total_ref[...] = jnp.broadcast_to(total, total_ref.shape)
    gate, shift, scale = (pick_rows(first, modulate_ref, at, width) for at in range(3))
    projected = own_ref[...] + other_ref[...].astype(jnp.float32)
    hidden = residual_ref[...].astype(jnp.float32) + gate * projected
    centered = hidden - row_mean(hidden)
    inverse = lax.rsqrt(row_mean(centered * centered) + EPSILON)
    normed = centered * inverse
    normed_ref[...] = normed
    inverse_ref[...] = jnp.broadcast_to(inverse, inverse_ref.shape)
    mixed = (normed * (1.0 + scale) + shift).astype(jnp.bfloat16)
    velocity = lax.dot_general(final_ref[...], mixed, NT, preferred_element_type=jnp.float32)
    velocity_ref[...] = velocity
    landed = near_ref[:lat, :].astype(jnp.float32) + far_ref[:lat, :].astype(jnp.float32)
    target = noise_ref[...].astype(jnp.float32) - landed
    used = lax.broadcasted_iota(jnp.int32, (lat, tile), 1) < used_rows
    error = jnp.where(used, velocity - target, 0.0)
    grad_wide = error * (2.0 / (total * lat))
    grad_columns = grad_wide.astype(jnp.bfloat16)
    grad_ref[...] = grad_wide
    final_part = jnp.dot(grad_columns, mixed, preferred_element_type=jnp.float32)
    for at in range(width // LANES):
        parts_ref[at] = final_part[:, at * LANES : (at + 1) * LANES].astype(jnp.bfloat16)
    squares = jnp.sum(error * error, axis=(0, 1), keepdims=True)
    parts_ref[width // LANES] = thirds(squares, lax.broadcasted_iota(jnp.int32, (lat, LANES), 0))


def head(place, counts, own, other, residual, modulate, final_columns, noise, near, far):
    tile, width = residual.shape
    lat = final_columns.shape[0]
    blocks = width // LANES + 1
    return pl.pallas_call(
        head_kernel,
        out_shape=(
            jax.ShapeDtypeStruct((lat, tile), jnp.float32),
            jax.ShapeDtypeStruct((blocks, lat, LANES), jnp.bfloat16),
            jax.ShapeDtypeStruct((8, LANES), jnp.float32),
            jax.ShapeDtypeStruct((tile, width), jnp.float32),
            jax.ShapeDtypeStruct((tile, LANES), jnp.float32),
            jax.ShapeDtypeStruct((lat, tile), jnp.float32),
        ),
        in_specs=[SMEM] * 2 + [VMEM] * 8,
        out_specs=(VMEM,) * 6,
        compiler_params=params(20),
    )(place, counts, own, other, residual, modulate, final_columns, noise, near, far)


def grad_kernel(
    place_ref, counts_ref, grad_columns_ref, normed_ref, inverse_ref, modulate_ref, final_ref, out_ref
):
    tile, width = normed_ref.shape
    first, _ = layout(place_ref, counts_ref, tile)
    gate, scale = (pick_rows(first, modulate_ref, at, width) for at in (0, 2))
    normed = normed_ref[...]
    grad_rows = grad_columns_ref[...].T.astype(jnp.bfloat16)
    grad_mixed = jnp.dot(grad_rows, final_ref[...], preferred_element_type=jnp.float32)
    grad_normed = grad_mixed * (1.0 + scale)
    across = normed * row_mean(grad_normed * normed)
    grad_hidden = inverse_ref[:, 0:1] * (grad_normed - row_mean(grad_normed) - across)
    out_ref[...] = (grad_hidden * gate).astype(jnp.bfloat16)


def grad_projected_of(place, counts, grad_columns, normed, inverse, modulate, final_columns):
    return pl.pallas_call(
        grad_kernel,
        out_shape=jax.ShapeDtypeStruct(normed.shape, jnp.bfloat16),
        in_specs=[SMEM] * 2 + [VMEM] * 5,
        out_specs=VMEM,
        compiler_params=params(20),
    )(place, counts, grad_columns, normed, inverse, modulate, final_columns)


def back_kernel(own_ref, other_ref, weight_ref, own_out_ref, other_out_ref, both_ref):
    tile = own_ref.shape[0]

    @pl.when(pl.program_id(0) == 0)
    def _():
        both_ref[:tile, :] = own_ref[...]
        both_ref[tile:, :] = other_ref[...]

    product = lax.dot_general(both_ref[...], weight_ref[...], NT, preferred_element_type=jnp.float32)
    own_out_ref[...] = product[:tile].astype(jnp.bfloat16)
    other_out_ref[...] = product[tile:].astype(jnp.bfloat16)


def back(own, other, weight):
    tile, width = own.shape
    depth = 2 * LANES
    out = jax.ShapeDtypeStruct((tile, weight.shape[0]), jnp.bfloat16)
    out_spec = pl.BlockSpec((tile, depth), lambda i: (0, i))
    return pl.pallas_call(
        back_kernel,
        grid=(weight.shape[0] // depth,),
        out_shape=(out, out),
        in_specs=[VMEM, VMEM, pl.BlockSpec((depth, width), lambda i: (i, 0))],
        out_specs=(out_spec, out_spec),
        scratch_shapes=[pltpu.VMEM((2 * tile, width), jnp.bfloat16)],
        compiler_params=params(24, ("arbitrary",)),
        cost_estimate=pl.CostEstimate(
            flops=4 * tile * width * weight.shape[0],
            bytes_accessed=2 * width * weight.shape[0],
            transcendentals=0,
        ),
    )(own, other, weight)


def join_kernel(half_ref, own_ref, other_ref, out_ref):
    depth = own_ref.shape[1]
    for half in range(2):

        @pl.when(half_ref[0] == half)
        def _():
            out_ref[:, half * depth : (half + 1) * depth] = own_ref[...]
            out_ref[:, (1 - half) * depth : (2 - half) * depth] = other_ref[...]


def join(half, own, other):
    return pl.pallas_call(
        join_kernel,
        out_shape=jax.ShapeDtypeStruct((own.shape[0], 2 * own.shape[1]), own.dtype),
        in_specs=[SMEM, VMEM, VMEM],
        out_specs=VMEM,
        compiler_params=params(16),
    )(half, own, other)


def sum_kernel(ranks, loss_row, last_ref, recv_ref, out_ref):
    rows = out_ref.shape[1]
    total = recv_ref[:rows, :].astype(jnp.float32)
    for rank in range(1, ranks):
        total += recv_ref[rank * rows : (rank + 1) * rows, :].astype(jnp.float32)
    loss = total[loss_row : loss_row + 1] + total[loss_row + 1 : loss_row + 2] + total[loss_row + 2 : loss_row + 3]
    row = lax.broadcasted_iota(jnp.int32, (rows, LANES), 0) - loss_row
    kept = thirds(loss, row)
    inside = jnp.logical_and(row >= 0, row < 3)
    changed = jnp.where(inside, kept.astype(jnp.float32), total)
    result = jnp.where(last_ref[0] == 1, changed, total).astype(jnp.bfloat16)
    for rank in range(out_ref.shape[0]):
        out_ref[rank] = result


def sum_out(recv, ranks, copies, loss_row, last):
    rows = recv.shape[0] // ranks
    result = pl.pallas_call(
        functools.partial(sum_kernel, ranks, loss_row),
        out_shape=jax.ShapeDtypeStruct((copies, rows, LANES), jnp.bfloat16),
        in_specs=[SMEM, VMEM],
        out_specs=VMEM,
        compiler_params=params(16),
    )(last, recv)
    return result.reshape(copies * rows, LANES)


def unpack_kernel(parts_ref, total_ref, out_ref, loss_ref):
    blocks, lat = parts_ref.shape[:2]
    for at in range(blocks - 1):
        out_ref[:, at * LANES : (at + 1) * LANES] = parts_ref[at].astype(jnp.float32)
    last = parts_ref[blocks - 1, :16, :].astype(jnp.float32)
    loss = last[0:1] + last[1:2] + last[2:3]
    loss_ref[...] = jnp.broadcast_to(loss, loss_ref.shape) / (total_ref[...] * lat)


def unpack(parts, total, width):
    return pl.pallas_call(
        unpack_kernel,
        out_shape=(
            jax.ShapeDtypeStruct((parts.shape[1], width), jnp.float32),
            jax.ShapeDtypeStruct((8, LANES), jnp.float32),
        ),
        in_specs=[VMEM, VMEM],
        out_specs=(VMEM, VMEM),
        compiler_params=params(16),
    )(parts, total)


def exchange(array, axis, groups=None):
    return lax.all_to_all(
        array, axis, split_axis=0, concat_axis=0, axis_index_groups=groups, tiled=True
    )


def per_device(
    near, latent_tiles, tile_route, image_tokens, text_lengths, queries, key_rows, values,
    text_keys, text_values, query_gain, key_gain, residual, out_weight, modulation, final_weight,
    noise_tiles,
):
    lat_width, tile = latent_tiles.shape[1:]
    rows_here, width = residual.shape
    text_rows = text_keys.shape[0]
    ranks, sources = lax.axis_size("dp"), lax.axis_size("seqt")
    far = ranks // near
    near_groups = [[row * near + at for at in range(near)] for row in range(far)]
    far_groups = [[row * near + at for row in range(far)] for at in range(near)]
    column_index = lax.axis_index("seqt").astype(jnp.int32)

    per_half = sources // 2
    halves = [[half * per_half + at for at in range(per_half)] for half in range(2)]
    place = column_index.reshape(1)
    half = (column_index // per_half).reshape(1)

    gathered = lax.all_gather(out_weight, "seqt", axis=0, axis_index_groups=halves, tiled=True)
    sent, tagged = pack(
        (queries, key_rows, values, text_keys, text_values), sources, latent_tiles, tile_route, image_tokens
    )
    recv = exchange(sent, "seqt")
    bits = [1 << at for at in range(ranks.bit_length() - 1)]
    held = gather(tagged, ranks, [bit for bit in reversed(bits) if bit < near])
    recv, held = lax.optimization_barrier((recv, held))
    held = gather(held, ranks, [bit for bit in bits[:-1] if bit >= near])
    heads = attention(
        recv, image_tokens, text_lengths, query_gain, key_gain, sources, tile, text_rows
    )
    heads, held = lax.optimization_barrier((heads, held))
    attended = exchange(heads, "seqt", halves)
    mine, other = land(held, tagged.shape[0], ranks)
    final_columns = final_weight.T
    own, across = project(half, attended, gathered, tile)
    across = swap(across, sources, per_half, "seqt")
    velocity, parts, total, normed, inverse, grad_columns = head(
        place, image_tokens, own, across, residual, modulation, final_columns, noise_tiles[0],
        mine, other,
    )
    grad_projected = grad_projected_of(
        place, image_tokens, grad_columns, normed, inverse, modulation, final_columns
    )
    blocks = parts.shape[0]
    share = blocks * lat_width // sources
    loss_row = (blocks - 1) * lat_width - (sources - 1) * share
    last = (column_index == sources - 1).astype(jnp.int32).reshape(1)
    sums = exchange(parts.reshape(blocks * lat_width, LANES), "seqt")
    sums, grad_projected = lax.optimization_barrier((sums, grad_projected))
    partner_grad = swap(grad_projected, sources, per_half, "seqt")
    sums = exchange(sum_out(sums, sources, near, loss_row, last), "dp", near_groups)
    sums, partner_grad = lax.optimization_barrier((sums, partner_grad))
    own_grad, across_grad = back(grad_projected, partner_grad, gathered)
    sums = exchange(sum_out(sums, near, far, loss_row, last), "dp", far_groups)
    sums, own_grad, across_grad = lax.optimization_barrier((sums, own_grad, across_grad))
    attention_grad = join(half, own_grad, swap(across_grad, sources, per_half, "seqt"))
    sums = exchange(sum_out(sums, far, sources, loss_row, last), "seqt")
    final_sums, loss = unpack(sums.reshape(blocks, lat_width, LANES), total, width)
    return velocity[None], attention_grad, final_sums.T, loss[0, 0]


def solution(mesh):
    both = P(("dp", "seqt"), None)
    tiles = P(("dp", "seqt"), None, None)
    placed = (
        tiles, P(("dp", "seqt")), P("dp", None), P("dp", None), both, both, both, both, both,
        P(), P(), both, P("seqt", None), P("dp", None), P(), tiles,
    )
    near = 8 if mesh.shape["dp"] % 8 == 0 else mesh.shape["dp"]
    return jax.shard_map(
        functools.partial(per_device, near),
        mesh=mesh,
        in_specs=placed,
        out_specs=(tiles, both, P(), P()),
        check_vma=False,
    )
```

```python
import functools

import jax
import jax.numpy as jnp
from jax import lax
from jax.experimental import pallas as pl
from jax.experimental.pallas import tpu as pltpu
from jax.sharding import PartitionSpec as P

HD = 64
IMGS = 2
LANES = 128
Q_ROWS = 256
NOTES = 16
EPSILON = 1e-06
HBM = pl.BlockSpec(memory_space=pltpu.HBM)
VMEM = pl.BlockSpec(memory_space=pltpu.VMEM)
SMEM = pl.BlockSpec(memory_space=pltpu.SMEM)
NT = (((1,), (1,)), ((), ()))


def params(limit_mib, semantics=None):
    return pltpu.CompilerParams(
        vmem_limit_bytes=limit_mib * 2**20, dimension_semantics=semantics
    )


def pack_kernel(parts, count, route_ref, counts_ref, tile_ref, *refs):
    ins, (out_ref, tagged_ref, lined_ref, in_semaphores, out_semaphore) = refs[:count], refs[count:]
    block_rows = sum(ref.shape[0] for ref in ins)
    for part in range(parts):
        row = part * block_rows
        for ref in ins:
            rows = ref.shape[0]
            pltpu.make_async_copy(
                ref.at[:, pl.ds(part * LANES, LANES)],
                lined_ref.at[pl.ds(row, rows), :],
                in_semaphores.at[part],
            ).start()
            row += rows
    lat = tile_ref.shape[1]
    tokens = counts_ref[0, 0] + counts_ref[0, 1]
    tagged_ref[:lat, :] = tile_ref[0]
    tagged_ref[lat:, :] = notes(route_ref[0], tokens // 16, tokens % 16)
    for part in range(parts):
        here = lined_ref.at[pl.ds(part * block_rows, block_rows), :]
        pltpu.make_async_copy(here, here, in_semaphores.at[part]).wait()
        there = out_ref.at[pl.ds(part * block_rows, block_rows), :]
        pltpu.make_async_copy(here, there, out_semaphore).start()
    pltpu.make_async_copy(lined_ref, out_ref, out_semaphore).wait()


def notes(first, second, third):
    places = lax.broadcasted_iota(jnp.int32, (NOTES, LANES), 0)
    third_or_none = jnp.where(places == 2, third, 0)
    numbers = jnp.where(places == 0, first, jnp.where(places == 1, second, third_or_none))
    return numbers.astype(jnp.float32).astype(jnp.bfloat16)


def pack(arrays, parts, tile, route, counts):
    block_rows = sum(array.shape[0] for array in arrays)
    return pl.pallas_call(
        functools.partial(pack_kernel, parts, len(arrays)),
        out_shape=(
            jax.ShapeDtypeStruct((parts * block_rows, LANES), arrays[0].dtype),
            jax.ShapeDtypeStruct((tile.shape[1] + NOTES, LANES), tile.dtype),
        ),
        in_specs=[SMEM, SMEM, VMEM] + [HBM] * len(arrays),
        out_specs=(HBM, VMEM),
        scratch_shapes=[
            pltpu.VMEM((parts * block_rows, LANES), arrays[0].dtype),
            pltpu.SemaphoreType.DMA((parts,)),
            pltpu.SemaphoreType.DMA,
        ],
        compiler_params=params(60),
    )(route, counts, tile, *arrays)


def select_kernel(last, me_ref, *refs):
    ins, out_ref = refs[:-1], refs[-1]
    rows = out_ref.shape[1]
    lat = rows - NOTES
    tokens = jnp.zeros((1, 1), jnp.float32)
    mine = jnp.zeros((lat, LANES), jnp.float32)
    other = jnp.zeros((lat, LANES), jnp.float32)
    me = me_ref[0].astype(jnp.float32)
    beside = (me_ref[0] ^ last).astype(jnp.float32)
    for ref in ins:
        for at in range(0, ref.shape[0], rows):
            tile = ref[at : at + lat, :].astype(jnp.float32)
            note = ref[at + lat : at + rows, :].astype(jnp.float32)
            route = note[0:1, 0:1]
            mine += jnp.where(route == me, tile, 0.0)
            other += jnp.where(route == beside, tile, 0.0)
            tokens += note[1:2, 0:1] * 16.0 + note[2:3, 0:1]
    high = jnp.floor(tokens * (1.0 / 128.0))
    places = lax.broadcasted_iota(jnp.int32, (NOTES, LANES), 0)
    number = jnp.where(places == 1, high, jnp.where(places == 2, tokens - high * 128.0, 0.0))
    for half, tile in enumerate((mine, other)):
        out_ref[half, :lat, :] = tile.astype(jnp.bfloat16)
        out_ref[half, lat:, :] = number.astype(jnp.bfloat16)


def gather(held, ranks, bits):
    for bit in bits:
        held = jnp.concatenate([held, swap(held, ranks, bit)], axis=0)
    return held


def land(held, rows, ranks):
    bit = max(ranks // 2, 1)
    chosen = pl.pallas_call(
        functools.partial(select_kernel, bit),
        out_shape=jax.ShapeDtypeStruct((2, rows, LANES), held.dtype),
        in_specs=[SMEM, VMEM],
        out_specs=VMEM,
        compiler_params=params(16),
    )(lax.axis_index("dp").astype(jnp.int32).reshape(1), held)
    return chosen[0], swap(chosen[1], ranks, bit) if bit < ranks else jnp.zeros_like(chosen[1])


def swap(array, ranks, step, axis="dp"):
    return lax.ppermute(array, axis, [(rank, rank ^ step) for rank in range(ranks)])


def head_norm(rows, gain, same_head):
    wide = rows.astype(jnp.float32)
    square = wide * wide
    high = square.astype(jnp.bfloat16)
    low = (square - high.astype(jnp.float32)).astype(jnp.bfloat16)
    total = jnp.dot(high, same_head, preferred_element_type=jnp.float32) + jnp.dot(
        low, same_head, preferred_element_type=jnp.float32
    )
    return (wide * lax.rsqrt(total * (1.0 / HD) + EPSILON) * gain).astype(jnp.bfloat16)


def attention_kernel(
    sources, tile, text_rows, counts_ref, lengths_ref, recv_ref, query_gain_ref, key_gain_ref,
    out_ref, query_ref, key_ref, value_ref, window_ref, weigh_ref,
):
    rows_all = sources * tile
    text_slots = sources * text_rows // IMGS
    window = rows_all // IMGS
    block = 3 * tile + 2 * text_rows
    per_image = sources // IMGS
    first_count = counts_ref[0, 0]
    second_count = counts_ref[0, 1]
    border = pl.multiple_of((first_count + tile - 1) // tile * tile, tile)
    head_row = lax.broadcasted_iota(jnp.int32, (LANES, LANES), 0) // HD
    head_column = lax.broadcasted_iota(jnp.int32, (LANES, LANES), 1) // HD
    same_head = (head_row == head_column).astype(jnp.float32).astype(jnp.bfloat16)
    query_gain = query_gain_ref[...]
    key_gain = key_gain_ref[...]
    for source in range(sources):
        at, row = source * block, source * tile
        key = head_norm(recv_ref[at + tile : at + 2 * tile, :], key_gain, same_head)
        key_ref[row : row + tile, :] = key
        if row < window:
            window_ref[0, row : row + tile, :] = key
        value_ref[row : row + tile, :] = recv_ref[at + 2 * tile : at + 3 * tile, :]
        query = head_norm(recv_ref[at : at + tile, :], query_gain, same_head)
        query_ref[row : row + tile, :] = query * jnp.bfloat16(HD**-0.5)
        image, place = source // per_image, window + source % per_image * text_rows
        text = recv_ref[at + 3 * tile : at + 3 * tile + text_rows, :]
        window_ref[image, place : place + text_rows, :] = head_norm(text, key_gain, same_head)
    window_ref[1, :window, :] = key_ref[pl.ds(border, window), :]

    def weighed(values, used, image, start, rows):
        low = lax.broadcasted_iota(jnp.int32, (rows, LANES), 1) < HD
        kept = lax.broadcasted_iota(jnp.int32, (rows, LANES), 0) < used
        wide = jnp.where(kept, values.astype(jnp.float32), 0.0)
        ones = kept.astype(jnp.float32)
        weigh_ref[image, 0, start : start + rows, :] = jnp.where(low, wide, ones).astype(jnp.bfloat16)
        weigh_ref[image, 1, start : start + rows, :] = jnp.where(low, ones, wide).astype(jnp.bfloat16)

    for image in range(IMGS):
        used = counts_ref[0, image]
        for start in range(0, window, tile):
            begin = start if image == 0 else pl.multiple_of(border + start, tile)
            weighed(value_ref[pl.ds(begin, tile), :], used - start, image, start, tile)
        text = jnp.concatenate(
            [
                recv_ref[s * block + 3 * tile + text_rows : (s + 1) * block, :]
                for s in range(image * per_image, (image + 1) * per_image)
            ],
            axis=0,
        )
        weighed(text, lengths_ref[0, image], image, window, text_slots)

    low = lax.broadcasted_iota(jnp.int32, (Q_ROWS, LANES), 1) < HD

    def rows_of(image, start):
        query = query_ref[pl.ds(start, Q_ROWS), :].astype(jnp.float32)
        sums = []
        for head in range(2):
            own = jnp.where(low == (head == 0), query, 0.0).astype(jnp.bfloat16)
            scores = lax.dot_general(own, window_ref[image], NT, preferred_element_type=jnp.float32)
            weights = jnp.exp(scores).astype(jnp.bfloat16)
            sums.append(jnp.dot(weights, weigh_ref[image, head], preferred_element_type=jnp.float32))
        above = jnp.where(low, sums[0], sums[1])
        below = pltpu.roll(jnp.where(low, sums[1], sums[0]), HD, 1)
        result = (above / below).astype(jnp.bfloat16)
        for part in range(Q_ROWS // tile):
            at = start // tile + part
            place = (lax.rem(at, per_image) * IMGS + lax.div(at, per_image)) * tile
            out_ref[pl.ds(pl.multiple_of(place, tile), tile), :] = result[part * tile : (part + 1) * tile]

    @pl.loop(0, (border + Q_ROWS - 1) // Q_ROWS)
    def _(step):
        rows_of(0, pl.multiple_of(step * Q_ROWS, tile))

    @pl.loop(0, (rows_all - border + Q_ROWS - 1) // Q_ROWS)
    def _(step):
        rows_of(1, pl.multiple_of(jnp.minimum(border + step * Q_ROWS, rows_all - Q_ROWS), tile))


def attention(recv, counts, lengths, query_gain, key_gain, sources, tile, text_rows):
    rows_all = sources * tile
    keys = rows_all // IMGS + sources * text_rows // IMGS
    twice = lambda gain: jnp.concatenate([gain, gain]).reshape(1, LANES)
    return pl.pallas_call(
        functools.partial(attention_kernel, sources, tile, text_rows),
        out_shape=jax.ShapeDtypeStruct((rows_all, LANES), jnp.bfloat16),
        in_specs=[SMEM, SMEM, VMEM, VMEM, VMEM],
        out_specs=VMEM,
        scratch_shapes=[
            pltpu.VMEM((rows_all, LANES), jnp.bfloat16),
            pltpu.VMEM((rows_all, LANES), jnp.bfloat16),
            pltpu.VMEM((rows_all, LANES), jnp.bfloat16),
            pltpu.VMEM((IMGS, keys, LANES), jnp.bfloat16),
            pltpu.VMEM((IMGS, 2, keys, LANES), jnp.bfloat16),
        ],
        compiler_params=params(32),
        cost_estimate=pl.CostEstimate(
            flops=16 * rows_all * keys * LANES,
            bytes_accessed=4 * rows_all * LANES * 4,
            transcendentals=2 * rows_all * keys,
        ),
    )(counts, lengths, recv, twice(query_gain), twice(key_gain))


def thirds(number, row):
    high = number.astype(jnp.bfloat16).astype(jnp.float32)
    middle = (number - high).astype(jnp.bfloat16).astype(jnp.float32)
    low = number - high - middle
    rest = jnp.where(row == 1, middle, jnp.where(row == 2, low, 0.0))
    return jnp.where(row == 0, high, rest).astype(jnp.bfloat16)


def pick_rows(first, modulate_ref, at, width):
    columns = pl.ds(at * width, width)
    return jnp.where(first, modulate_ref[0:1, columns], modulate_ref[1:2, columns])


def row_mean(array):
    return jnp.sum(array, axis=-1, keepdims=True) * (1.0 / array.shape[1])


def layout(place_ref, counts_ref, tile):
    place = place_ref[0] * tile
    border = (counts_ref[0, 0] + tile - 1) // tile * tile
    first = place < border
    return first, jnp.where(first, counts_ref[0, 0], border + counts_ref[0, 1]) - place


def project_kernel(half_ref, rows_ref, weight_ref, own_ref, other_ref, lined_ref):
    tile = own_ref.shape[0]

    @pl.when(pl.program_id(0) == 0)
    def _():
        for at in range(lined_ref.shape[1] // LANES):
            rows = rows_ref[at * 2 * tile : (at + 1) * 2 * tile, :]
            lined_ref[:, at * LANES : (at + 1) * LANES] = rows

    product = jnp.dot(lined_ref[...], weight_ref[...], preferred_element_type=jnp.float32)
    first = half_ref[0] == 0
    own_ref[...] = jnp.where(first, product[:tile], product[tile:])
    other_ref[...] = jnp.where(first, product[tile:], product[:tile]).astype(jnp.bfloat16)


def project(half, recv, weight, tile):
    depth, width = weight.shape
    block = 4 * LANES
    out_spec = pl.BlockSpec((tile, block), lambda i: (0, i))
    return pl.pallas_call(
        project_kernel,
        grid=(pl.cdiv(width, block),),
        out_shape=(
            jax.ShapeDtypeStruct((tile, width), jnp.float32),
            jax.ShapeDtypeStruct((tile, width), jnp.bfloat16),
        ),
        in_specs=[SMEM, VMEM, pl.BlockSpec((depth, block), lambda i: (0, i))],
        out_specs=(out_spec, out_spec),
        scratch_shapes=[pltpu.VMEM((2 * tile, depth), jnp.bfloat16)],
        compiler_params=params(52, ("arbitrary",)),
    )(half, recv, weight)


def head_kernel(
    place_ref, counts_ref, own_ref, other_ref, residual_ref, modulate_ref, final_ref, noise_ref,
    near_ref, far_ref, velocity_ref, parts_ref, total_ref, normed_ref, inverse_ref, grad_ref,
    own_here, other_here, semaphores,
):
    copies = [
        pltpu.make_async_copy(own_ref, own_here, semaphores.at[0]),
        pltpu.make_async_copy(other_ref, other_here, semaphores.at[1]),
    ]
    for copy in copies:
        copy.start()
    tile, width = residual_ref.shape
    lat = final_ref.shape[0]
    first, used_rows = layout(place_ref, counts_ref, tile)
    total = jnp.zeros((1, 1), jnp.float32)
    for ref in (near_ref, far_ref):
        note = ref[lat:, :].astype(jnp.float32)
        total += note[1:2, 0:1] * 128.0 + note[2:3, 0:1]
    total_ref[...] = jnp.broadcast_to(total, total_ref.shape)
    gate, shift, scale = (pick_rows(first, modulate_ref, at, width) for at in range(3))
    for copy in copies:
        copy.wait()
    projected = own_here[...] + other_here[...].astype(jnp.float32)
    hidden = residual_ref[...].astype(jnp.float32) + gate * projected
    centered = hidden - row_mean(hidden)
    inverse = lax.rsqrt(row_mean(centered * centered) + EPSILON)
    normed = centered * inverse
    normed_ref[...] = normed
    inverse_ref[...] = jnp.broadcast_to(inverse, inverse_ref.shape)
    mixed = (normed * (1.0 + scale) + shift).astype(jnp.bfloat16)
    velocity = lax.dot_general(final_ref[...], mixed, NT, preferred_element_type=jnp.float32)
    velocity_ref[...] = velocity
    landed = near_ref[:lat, :].astype(jnp.float32) + far_ref[:lat, :].astype(jnp.float32)
    target = noise_ref[...].astype(jnp.float32) - landed
    used = lax.broadcasted_iota(jnp.int32, (lat, tile), 1) < used_rows
    error = jnp.where(used, velocity - target, 0.0)
    grad_wide = error * (2.0 / (total * lat))
    grad_columns = grad_wide.astype(jnp.bfloat16)
    grad_ref[...] = grad_wide
    final_part = jnp.dot(grad_columns, mixed, preferred_element_type=jnp.float32)
    for at in range(width // LANES):
        parts_ref[at] = final_part[:, at * LANES : (at + 1) * LANES].astype(jnp.bfloat16)
    squares = jnp.sum(error * error, axis=(0, 1), keepdims=True)
    parts_ref[width // LANES] = thirds(squares, lax.broadcasted_iota(jnp.int32, (lat, LANES), 0))


def head(place, counts, own, other, residual, modulate, final_columns, noise, near, far):
    tile, width = residual.shape
    lat = final_columns.shape[0]
    blocks = width // LANES + 1
    return pl.pallas_call(
        head_kernel,
        out_shape=(
            jax.ShapeDtypeStruct((lat, tile), jnp.float32),
            jax.ShapeDtypeStruct((blocks, lat, LANES), jnp.bfloat16),
            jax.ShapeDtypeStruct((8, LANES), jnp.float32),
            jax.ShapeDtypeStruct((tile, width), jnp.float32),
            jax.ShapeDtypeStruct((tile, LANES), jnp.float32),
            jax.ShapeDtypeStruct((lat, tile), jnp.float32),
        ),
        in_specs=[SMEM] * 2 + [HBM] * 2 + [VMEM] * 6,
        out_specs=(VMEM,) * 6,
        scratch_shapes=[
            pltpu.VMEM(own.shape, own.dtype),
            pltpu.VMEM(other.shape, other.dtype),
            pltpu.SemaphoreType.DMA((2,)),
        ],
        compiler_params=params(52),
    )(place, counts, own, other, residual, modulate, final_columns, noise, near, far)


def grad_kernel(
    place_ref, counts_ref, grad_columns_ref, normed_ref, inverse_ref, modulate_ref, final_ref, out_ref
):
    tile, width = normed_ref.shape
    first, _ = layout(place_ref, counts_ref, tile)
    gate, scale = (pick_rows(first, modulate_ref, at, width) for at in (0, 2))
    normed = normed_ref[...]
    grad_rows = grad_columns_ref[...].T.astype(jnp.bfloat16)
    grad_mixed = jnp.dot(grad_rows, final_ref[...], preferred_element_type=jnp.float32)
    grad_normed = grad_mixed * (1.0 + scale)
    across = normed * row_mean(grad_normed * normed)
    grad_hidden = inverse_ref[:, 0:1] * (grad_normed - row_mean(grad_normed) - across)
    out_ref[...] = (grad_hidden * gate).astype(jnp.bfloat16)


def grad_projected_of(place, counts, grad_columns, normed, inverse, modulate, final_columns):
    return pl.pallas_call(
        grad_kernel,
        out_shape=jax.ShapeDtypeStruct(normed.shape, jnp.bfloat16),
        in_specs=[SMEM] * 2 + [VMEM] * 5,
        out_specs=VMEM,
        compiler_params=params(20),
    )(place, counts, grad_columns, normed, inverse, modulate, final_columns)


def back_kernel(own_ref, other_ref, weight_ref, own_out_ref, other_out_ref, both_ref):
    tile = own_ref.shape[0]

    @pl.when(pl.program_id(0) == 0)
    def _():
        both_ref[:tile, :] = own_ref[...]
        both_ref[tile:, :] = other_ref[...]

    product = lax.dot_general(both_ref[...], weight_ref[...], NT, preferred_element_type=jnp.float32)
    own_out_ref[...] = product[:tile].astype(jnp.bfloat16)
    other_out_ref[...] = product[tile:].astype(jnp.bfloat16)


def back(own, other, weight):
    tile, width = own.shape
    depth = 2 * LANES
    out = jax.ShapeDtypeStruct((tile, weight.shape[0]), jnp.bfloat16)
    out_spec = pl.BlockSpec((tile, depth), lambda i: (0, i))
    return pl.pallas_call(
        back_kernel,
        grid=(weight.shape[0] // depth,),
        out_shape=(out, out),
        in_specs=[VMEM, VMEM, pl.BlockSpec((depth, width), lambda i: (i, 0))],
        out_specs=(out_spec, out_spec),
        scratch_shapes=[pltpu.VMEM((2 * tile, width), jnp.bfloat16)],
        compiler_params=params(24, ("arbitrary",)),
        cost_estimate=pl.CostEstimate(
            flops=4 * tile * width * weight.shape[0],
            bytes_accessed=2 * width * weight.shape[0],
            transcendentals=0,
        ),
    )(own, other, weight)


def join_kernel(half_ref, own_ref, other_ref, out_ref):
    depth = own_ref.shape[1]
    for half in range(2):

        @pl.when(half_ref[0] == half)
        def _():
            out_ref[:, half * depth : (half + 1) * depth] = own_ref[...]
            out_ref[:, (1 - half) * depth : (2 - half) * depth] = other_ref[...]


def join(half, own, other):
    return pl.pallas_call(
        join_kernel,
        out_shape=jax.ShapeDtypeStruct((own.shape[0], 2 * own.shape[1]), own.dtype),
        in_specs=[SMEM, VMEM, VMEM],
        out_specs=VMEM,
        compiler_params=params(16),
    )(half, own, other)


def sum_kernel(ranks, loss_row, last_ref, recv_ref, out_ref):
    rows = out_ref.shape[1]
    total = recv_ref[:rows, :].astype(jnp.float32)
    for rank in range(1, ranks):
        total += recv_ref[rank * rows : (rank + 1) * rows, :].astype(jnp.float32)
    loss = total[loss_row : loss_row + 1] + total[loss_row + 1 : loss_row + 2] + total[loss_row + 2 : loss_row + 3]
    row = lax.broadcasted_iota(jnp.int32, (rows, LANES), 0) - loss_row
    kept = thirds(loss, row)
    inside = jnp.logical_and(row >= 0, row < 3)
    changed = jnp.where(inside, kept.astype(jnp.float32), total)
    result = jnp.where(last_ref[0] == 1, changed, total).astype(jnp.bfloat16)
    for rank in range(out_ref.shape[0]):
        out_ref[rank] = result


def sum_out(recv, ranks, copies, loss_row, last):
    rows = recv.shape[0] // ranks
    result = pl.pallas_call(
        functools.partial(sum_kernel, ranks, loss_row),
        out_shape=jax.ShapeDtypeStruct((copies, rows, LANES), jnp.bfloat16),
        in_specs=[SMEM, VMEM],
        out_specs=VMEM,
        compiler_params=params(16),
    )(last, recv)
    return result.reshape(copies * rows, LANES)


def unpack_kernel(parts_ref, total_ref, out_ref, loss_ref):
    blocks, lat = parts_ref.shape[:2]
    for at in range(blocks - 1):
        out_ref[:, at * LANES : (at + 1) * LANES] = parts_ref[at].astype(jnp.float32)
    last = parts_ref[blocks - 1, :16, :].astype(jnp.float32)
    loss = last[0:1] + last[1:2] + last[2:3]
    loss_ref[...] = jnp.broadcast_to(loss, loss_ref.shape) / (total_ref[...] * lat)


def unpack(parts, total, width):
    return pl.pallas_call(
        unpack_kernel,
        out_shape=(
            jax.ShapeDtypeStruct((parts.shape[1], width), jnp.float32),
            jax.ShapeDtypeStruct((8, LANES), jnp.float32),
        ),
        in_specs=[VMEM, VMEM],
        out_specs=(VMEM, VMEM),
        compiler_params=params(16),
    )(parts, total)


def exchange(array, axis, groups=None):
    return lax.all_to_all(
        array, axis, split_axis=0, concat_axis=0, axis_index_groups=groups, tiled=True
    )


def per_device(
    near, latent_tiles, tile_route, image_tokens, text_lengths, queries, key_rows, values,
    text_keys, text_values, query_gain, key_gain, residual, out_weight, modulation, final_weight,
    noise_tiles,
):
    lat_width, tile = latent_tiles.shape[1:]
    rows_here, width = residual.shape
    text_rows = text_keys.shape[0]
    ranks, sources = lax.axis_size("dp"), lax.axis_size("seqt")
    far = ranks // near
    near_groups = [[row * near + at for at in range(near)] for row in range(far)]
    far_groups = [[row * near + at for row in range(far)] for at in range(near)]
    column_index = lax.axis_index("seqt").astype(jnp.int32)

    per_half = sources // 2
    halves = [[half * per_half + at for at in range(per_half)] for half in range(2)]
    place = column_index.reshape(1)
    half = (column_index // per_half).reshape(1)

    gathered = lax.all_gather(out_weight, "seqt", axis=0, axis_index_groups=halves, tiled=True)
    sent, tagged = pack(
        (queries, key_rows, values, text_keys, text_values), sources, latent_tiles, tile_route, image_tokens
    )
    recv = exchange(sent, "seqt")
    bits = [1 << at for at in range(ranks.bit_length() - 1)]
    held = gather(tagged, ranks, [bit for bit in reversed(bits) if bit < near])
    recv, held = lax.optimization_barrier((recv, held))
    held = gather(held, ranks, [bit for bit in bits[:-1] if bit >= near])
    heads = attention(
        recv, image_tokens, text_lengths, query_gain, key_gain, sources, tile, text_rows
    )
    heads, held = lax.optimization_barrier((heads, held))
    attended = exchange(heads, "seqt", halves)
    mine, other = land(held, tagged.shape[0], ranks)
    attended, mine, other = lax.optimization_barrier((attended, mine, other))
    final_columns = final_weight.T
    own, across = project(half, attended, gathered, tile)
    across = swap(across, sources, per_half, "seqt")
    velocity, parts, total, normed, inverse, grad_columns = head(
        place, image_tokens, own, across, residual, modulation, final_columns, noise_tiles[0],
        mine, other,
    )
    grad_projected = grad_projected_of(
        place, image_tokens, grad_columns, normed, inverse, modulation, final_columns
    )
    blocks = parts.shape[0]
    share = blocks * lat_width // sources
    loss_row = (blocks - 1) * lat_width - (sources - 1) * share
    last = (column_index == sources - 1).astype(jnp.int32).reshape(1)
    partner_grad = swap(grad_projected, sources, per_half, "seqt")
    own_grad, across_grad = back(grad_projected, partner_grad, gathered)
    swapped_grad = swap(across_grad, sources, per_half, "seqt")
    sums = exchange(parts.reshape(blocks * lat_width, LANES), "seqt")
    sums, _ = lax.optimization_barrier((sums, grad_projected))
    sums = exchange(sum_out(sums, sources, near, loss_row, last), "dp", near_groups)
    sums, _ = lax.optimization_barrier((sums, partner_grad))
    sums = exchange(sum_out(sums, near, far, loss_row, last), "dp", far_groups)
    sums, _ = lax.optimization_barrier((sums, across_grad))
    sums = exchange(sum_out(sums, far, sources, loss_row, last), "seqt")
    attention_grad = join(half, own_grad, swapped_grad)
    final_sums, loss = unpack(sums.reshape(blocks, lat_width, LANES), total, width)
    return velocity[None], attention_grad, final_sums.T, loss[0, 0]


def solution(mesh):
    both = P(("dp", "seqt"), None)
    tiles = P(("dp", "seqt"), None, None)
    placed = (
        tiles, P(("dp", "seqt")), P("dp", None), P("dp", None), both, both, both, both, both,
        P(), P(), both, P("seqt", None), P("dp", None), P(), tiles,
    )
    near = 8 if mesh.shape["dp"] % 8 == 0 else mesh.shape["dp"]
    return jax.shard_map(
        functools.partial(per_device, near),
        mesh=mesh,
        in_specs=placed,
        out_specs=(tiles, both, P(), P()),
        check_vma=False,
    )
```

```python
import functools

import jax
import jax.numpy as jnp
from jax import lax
from jax.experimental import pallas as pl
from jax.experimental.pallas import tpu as pltpu
from jax.sharding import PartitionSpec as P

HD = 64
IMGS = 2
LANES = 128
Q_ROWS = 256
NOTES = 16
EPSILON = 1e-06
HBM = pl.BlockSpec(memory_space=pltpu.HBM)
VMEM = pl.BlockSpec(memory_space=pltpu.VMEM)
SMEM = pl.BlockSpec(memory_space=pltpu.SMEM)
NT = (((1,), (1,)), ((), ()))


def params(limit_mib, semantics=None):
    return pltpu.CompilerParams(
        vmem_limit_bytes=limit_mib * 2**20, dimension_semantics=semantics
    )


def pack_kernel(parts, count, route_ref, counts_ref, tile_ref, *refs):
    ins, (out_ref, tagged_ref, lined_ref, in_semaphores, out_semaphore) = refs[:count], refs[count:]
    block_rows = sum(ref.shape[0] for ref in ins)
    for part in range(parts):
        row = part * block_rows
        for ref in ins:
            rows = ref.shape[0]
            pltpu.make_async_copy(
                ref.at[:, pl.ds(part * LANES, LANES)],
                lined_ref.at[pl.ds(row, rows), :],
                in_semaphores.at[part],
            ).start()
            row += rows
    lat = tile_ref.shape[1]
    tokens = counts_ref[0, 0] + counts_ref[0, 1]
    tagged_ref[:lat, :] = tile_ref[0]
    tagged_ref[lat:, :] = notes(route_ref[0], tokens // 16, tokens % 16)
    for part in range(parts):
        here = lined_ref.at[pl.ds(part * block_rows, block_rows), :]
        pltpu.make_async_copy(here, here, in_semaphores.at[part]).wait()
        there = out_ref.at[pl.ds(part * block_rows, block_rows), :]
        pltpu.make_async_copy(here, there, out_semaphore).start()
    pltpu.make_async_copy(lined_ref, out_ref, out_semaphore).wait()


def notes(first, second, third):
    places = lax.broadcasted_iota(jnp.int32, (NOTES, LANES), 0)
    third_or_none = jnp.where(places == 2, third, 0)
    numbers = jnp.where(places == 0, first, jnp.where(places == 1, second, third_or_none))
    return numbers.astype(jnp.float32).astype(jnp.bfloat16)


def pack(arrays, parts, tile, route, counts):
    block_rows = sum(array.shape[0] for array in arrays)
    return pl.pallas_call(
        functools.partial(pack_kernel, parts, len(arrays)),
        out_shape=(
            jax.ShapeDtypeStruct((parts * block_rows, LANES), arrays[0].dtype),
            jax.ShapeDtypeStruct((tile.shape[1] + NOTES, LANES), tile.dtype),
        ),
        in_specs=[SMEM, SMEM, VMEM] + [HBM] * len(arrays),
        out_specs=(HBM, VMEM),
        scratch_shapes=[
            pltpu.VMEM((parts * block_rows, LANES), arrays[0].dtype),
            pltpu.SemaphoreType.DMA((parts,)),
            pltpu.SemaphoreType.DMA,
        ],
        compiler_params=params(60),
    )(route, counts, tile, *arrays)


def select_kernel(last, me_ref, *refs):
    ins, out_ref = refs[:-1], refs[-1]
    rows = out_ref.shape[1]
    lat = rows - NOTES
    tokens = jnp.zeros((1, 1), jnp.float32)
    mine = jnp.zeros((lat, LANES), jnp.float32)
    other = jnp.zeros((lat, LANES), jnp.float32)
    me = me_ref[0].astype(jnp.float32)
    beside = (me_ref[0] ^ last).astype(jnp.float32)
    for ref in ins:
        for at in range(0, ref.shape[0], rows):
            tile = ref[at : at + lat, :].astype(jnp.float32)
            note = ref[at + lat : at + rows, :].astype(jnp.float32)
            route = note[0:1, 0:1]
            mine += jnp.where(route == me, tile, 0.0)
            other += jnp.where(route == beside, tile, 0.0)
            tokens += note[1:2, 0:1] * 16.0 + note[2:3, 0:1]
    high = jnp.floor(tokens * (1.0 / 128.0))
    places = lax.broadcasted_iota(jnp.int32, (NOTES, LANES), 0)
    number = jnp.where(places == 1, high, jnp.where(places == 2, tokens - high * 128.0, 0.0))
    for half, tile in enumerate((mine, other)):
        out_ref[half, :lat, :] = tile.astype(jnp.bfloat16)
        out_ref[half, lat:, :] = number.astype(jnp.bfloat16)


def gather(held, ranks, bits):
    for bit in bits:
        held = jnp.concatenate([held, swap(held, ranks, bit)], axis=0)
    return held


def land(held, rows, ranks):
    bit = max(ranks // 2, 1)
    chosen = pl.pallas_call(
        functools.partial(select_kernel, bit),
        out_shape=jax.ShapeDtypeStruct((2, rows, LANES), held.dtype),
        in_specs=[SMEM, VMEM],
        out_specs=VMEM,
        compiler_params=params(16),
    )(lax.axis_index("dp").astype(jnp.int32).reshape(1), held)
    return chosen[0], swap(chosen[1], ranks, bit) if bit < ranks else jnp.zeros_like(chosen[1])


def swap(array, ranks, step, axis="dp"):
    return lax.ppermute(array, axis, [(rank, rank ^ step) for rank in range(ranks)])


def head_norm(rows, gain, same_head):
    wide = rows.astype(jnp.float32)
    square = wide * wide
    high = square.astype(jnp.bfloat16)
    low = (square - high.astype(jnp.float32)).astype(jnp.bfloat16)
    total = jnp.dot(high, same_head, preferred_element_type=jnp.float32) + jnp.dot(
        low, same_head, preferred_element_type=jnp.float32
    )
    return (wide * lax.rsqrt(total * (1.0 / HD) + EPSILON) * gain).astype(jnp.bfloat16)


def attention_kernel(
    sources, tile, text_rows, counts_ref, lengths_ref, recv_ref, query_gain_ref, key_gain_ref,
    out_ref, query_ref, key_ref, value_ref, window_ref, weigh_ref,
):
    rows_all = sources * tile
    text_slots = sources * text_rows // IMGS
    window = rows_all // IMGS
    block = 3 * tile + 2 * text_rows
    per_image = sources // IMGS
    first_count = counts_ref[0, 0]
    second_count = counts_ref[0, 1]
    border = pl.multiple_of((first_count + tile - 1) // tile * tile, tile)
    head_row = lax.broadcasted_iota(jnp.int32, (LANES, LANES), 0) // HD
    head_column = lax.broadcasted_iota(jnp.int32, (LANES, LANES), 1) // HD
    same_head = (head_row == head_column).astype(jnp.float32).astype(jnp.bfloat16)
    query_gain = query_gain_ref[...]
    key_gain = key_gain_ref[...]
    for source in range(sources):
        at, row = source * block, source * tile
        key = head_norm(recv_ref[at + tile : at + 2 * tile, :], key_gain, same_head)
        key_ref[row : row + tile, :] = key
        if row < window:
            window_ref[0, row : row + tile, :] = key
        value_ref[row : row + tile, :] = recv_ref[at + 2 * tile : at + 3 * tile, :]
        query = head_norm(recv_ref[at : at + tile, :], query_gain, same_head)
        query_ref[row : row + tile, :] = query * jnp.bfloat16(HD**-0.5)
        image, place = source // per_image, window + source % per_image * text_rows
        text = recv_ref[at + 3 * tile : at + 3 * tile + text_rows, :]
        window_ref[image, place : place + text_rows, :] = head_norm(text, key_gain, same_head)
    window_ref[1, :window, :] = key_ref[pl.ds(border, window), :]

    def weighed(values, used, image, start, rows):
        low = lax.broadcasted_iota(jnp.int32, (rows, LANES), 1) < HD
        kept = lax.broadcasted_iota(jnp.int32, (rows, LANES), 0) < used
        wide = jnp.where(kept, values.astype(jnp.float32), 0.0)
        ones = kept.astype(jnp.float32)
        weigh_ref[image, 0, start : start + rows, :] = jnp.where(low, wide, ones).astype(jnp.bfloat16)
        weigh_ref[image, 1, start : start + rows, :] = jnp.where(low, ones, wide).astype(jnp.bfloat16)

    for image in range(IMGS):
        used = counts_ref[0, image]
        for start in range(0, window, tile):
            begin = start if image == 0 else pl.multiple_of(border + start, tile)
            weighed(value_ref[pl.ds(begin, tile), :], used - start, image, start, tile)
        text = jnp.concatenate(
            [
                recv_ref[s * block + 3 * tile + text_rows : (s + 1) * block, :]
                for s in range(image * per_image, (image + 1) * per_image)
            ],
            axis=0,
        )
        weighed(text, lengths_ref[0, image], image, window, text_slots)

    low = lax.broadcasted_iota(jnp.int32, (Q_ROWS, LANES), 1) < HD

    def rows_of(image, start):
        query = query_ref[pl.ds(start, Q_ROWS), :].astype(jnp.float32)
        sums = []
        for head in range(2):
            own = jnp.where(low == (head == 0), query, 0.0).astype(jnp.bfloat16)
            scores = lax.dot_general(own, window_ref[image], NT, preferred_element_type=jnp.float32)
            weights = jnp.exp(scores).astype(jnp.bfloat16)
            sums.append(jnp.dot(weights, weigh_ref[image, head], preferred_element_type=jnp.float32))
        above = jnp.where(low, sums[0], sums[1])
        below = pltpu.roll(jnp.where(low, sums[1], sums[0]), HD, 1)
        result = (above / below).astype(jnp.bfloat16)
        for part in range(Q_ROWS // tile):
            at = start // tile + part
            place = (lax.rem(at, per_image) * IMGS + lax.div(at, per_image)) * tile
            out_ref[pl.ds(pl.multiple_of(place, tile), tile), :] = result[part * tile : (part + 1) * tile]

    @pl.loop(0, (border + Q_ROWS - 1) // Q_ROWS)
    def _(step):
        rows_of(0, pl.multiple_of(step * Q_ROWS, tile))

    @pl.loop(0, (rows_all - border + Q_ROWS - 1) // Q_ROWS)
    def _(step):
        rows_of(1, pl.multiple_of(jnp.minimum(border + step * Q_ROWS, rows_all - Q_ROWS), tile))


def attention(recv, counts, lengths, query_gain, key_gain, sources, tile, text_rows):
    rows_all = sources * tile
    keys = rows_all // IMGS + sources * text_rows // IMGS
    twice = lambda gain: jnp.concatenate([gain, gain]).reshape(1, LANES)
    return pl.pallas_call(
        functools.partial(attention_kernel, sources, tile, text_rows),
        out_shape=jax.ShapeDtypeStruct((rows_all, LANES), jnp.bfloat16),
        in_specs=[SMEM, SMEM, VMEM, VMEM, VMEM],
        out_specs=VMEM,
        scratch_shapes=[
            pltpu.VMEM((rows_all, LANES), jnp.bfloat16),
            pltpu.VMEM((rows_all, LANES), jnp.bfloat16),
            pltpu.VMEM((rows_all, LANES), jnp.bfloat16),
            pltpu.VMEM((IMGS, keys, LANES), jnp.bfloat16),
            pltpu.VMEM((IMGS, 2, keys, LANES), jnp.bfloat16),
        ],
        compiler_params=params(32),
        cost_estimate=pl.CostEstimate(
            flops=16 * rows_all * keys * LANES,
            bytes_accessed=4 * rows_all * LANES * 4,
            transcendentals=2 * rows_all * keys,
        ),
    )(counts, lengths, recv, twice(query_gain), twice(key_gain))


def thirds(number, row):
    high = number.astype(jnp.bfloat16).astype(jnp.float32)
    middle = (number - high).astype(jnp.bfloat16).astype(jnp.float32)
    low = number - high - middle
    rest = jnp.where(row == 1, middle, jnp.where(row == 2, low, 0.0))
    return jnp.where(row == 0, high, rest).astype(jnp.bfloat16)


def pick_rows(first, modulate_ref, at, width):
    columns = pl.ds(at * width, width)
    return jnp.where(first, modulate_ref[0:1, columns], modulate_ref[1:2, columns])


def row_mean(array):
    return jnp.sum(array, axis=-1, keepdims=True) * (1.0 / array.shape[1])


def layout(place_ref, counts_ref, tile):
    place = place_ref[0] * tile
    border = (counts_ref[0, 0] + tile - 1) // tile * tile
    first = place < border
    return first, jnp.where(first, counts_ref[0, 0], border + counts_ref[0, 1]) - place


def project_kernel(
    block, half_ref, rows_ref, weight_ref, own_ref, other_ref, lined_ref, here_ref, semaphores
):
    tile, width = own_ref.shape
    whole = width // block

    def landing(at, size):
        columns = pl.ds(pl.multiple_of(at * block, block), size)
        return pltpu.make_async_copy(
            weight_ref.at[:, columns], here_ref.at[:, columns], semaphores.at[at]
        )

    sizes = [block] * whole + ([width % block] if width % block else [])
    for at, size in enumerate(sizes):
        landing(at, size).start()
    for at in range(lined_ref.shape[1] // LANES):
        rows = rows_ref[at * 2 * tile : (at + 1) * 2 * tile, :]
        lined_ref[:, at * LANES : (at + 1) * LANES] = rows
    first = half_ref[0] == 0

    def multiply(at, size):
        landing(at, size).wait()
        columns = pl.ds(pl.multiple_of(at * block, block), size)
        product = jnp.dot(lined_ref[...], here_ref[:, columns], preferred_element_type=jnp.float32)
        own_ref[:, columns] = jnp.where(first, product[:tile], product[tile:])
        other = jnp.where(first, product[tile:], product[:tile])
        other_ref[:, columns] = other.astype(jnp.bfloat16)

    @pl.loop(0, whole)
    def _(at):
        multiply(at, block)

    if width % block:
        multiply(whole, width % block)


def project(half, recv, weight, tile):
    depth, width = weight.shape
    block = 4 * LANES
    return pl.pallas_call(
        functools.partial(project_kernel, block),
        out_shape=(
            jax.ShapeDtypeStruct((tile, width), jnp.float32),
            jax.ShapeDtypeStruct((tile, width), jnp.bfloat16),
        ),
        in_specs=[SMEM, VMEM, HBM],
        out_specs=(VMEM, VMEM),
        scratch_shapes=[
            pltpu.VMEM((2 * tile, depth), jnp.bfloat16),
            pltpu.VMEM((depth, width), jnp.bfloat16),
            pltpu.SemaphoreType.DMA((pl.cdiv(width, block),)),
        ],
        compiler_params=params(52),
    )(half, recv, weight)


def head_kernel(
    place_ref, counts_ref, own_ref, other_ref, residual_ref, modulate_ref, final_ref, noise_ref,
    near_ref, far_ref, velocity_ref, parts_ref, total_ref, normed_ref, inverse_ref, grad_ref,
    own_here, other_here, residual_here, semaphores,
):
    pairs = ((own_ref, own_here), (residual_ref, residual_here), (other_ref, other_here))
    copies = [
        pltpu.make_async_copy(there, here, semaphores.at[at]) for at, (there, here) in enumerate(pairs)
    ]
    for copy in copies:
        copy.start()
    tile, width = residual_ref.shape
    lat = final_ref.shape[0]
    first, used_rows = layout(place_ref, counts_ref, tile)
    total = jnp.zeros((1, 1), jnp.float32)
    for ref in (near_ref, far_ref):
        note = ref[lat:, :].astype(jnp.float32)
        total += note[1:2, 0:1] * 128.0 + note[2:3, 0:1]
    total_ref[...] = jnp.broadcast_to(total, total_ref.shape)
    gate, shift, scale = (pick_rows(first, modulate_ref, at, width) for at in range(3))
    for copy in copies:
        copy.wait()
    projected = own_here[...] + other_here[...].astype(jnp.float32)
    hidden = residual_here[...].astype(jnp.float32) + gate * projected
    centered = hidden - row_mean(hidden)
    inverse = lax.rsqrt(row_mean(centered * centered) + EPSILON)
    normed = centered * inverse
    normed_ref[...] = normed
    inverse_ref[...] = jnp.broadcast_to(inverse, inverse_ref.shape)
    mixed = (normed * (1.0 + scale) + shift).astype(jnp.bfloat16)
    velocity = lax.dot_general(final_ref[...], mixed, NT, preferred_element_type=jnp.float32)
    velocity_ref[...] = velocity
    landed = near_ref[:lat, :].astype(jnp.float32) + far_ref[:lat, :].astype(jnp.float32)
    target = noise_ref[...].astype(jnp.float32) - landed
    used = lax.broadcasted_iota(jnp.int32, (lat, tile), 1) < used_rows
    error = jnp.where(used, velocity - target, 0.0)
    grad_wide = error * (2.0 / (total * lat))
    grad_columns = grad_wide.astype(jnp.bfloat16)
    grad_ref[...] = grad_wide
    final_part = jnp.dot(grad_columns, mixed, preferred_element_type=jnp.float32)
    for at in range(width // LANES):
        parts_ref[at] = final_part[:, at * LANES : (at + 1) * LANES].astype(jnp.bfloat16)
    squares = jnp.sum(error * error, axis=(0, 1), keepdims=True)
    parts_ref[width // LANES] = thirds(squares, lax.broadcasted_iota(jnp.int32, (lat, LANES), 0))


def head(place, counts, own, other, residual, modulate, final_columns, noise, near, far):
    tile, width = residual.shape
    lat = final_columns.shape[0]
    blocks = width // LANES + 1
    return pl.pallas_call(
        head_kernel,
        out_shape=(
            jax.ShapeDtypeStruct((lat, tile), jnp.float32),
            jax.ShapeDtypeStruct((blocks, lat, LANES), jnp.bfloat16),
            jax.ShapeDtypeStruct((8, LANES), jnp.float32),
            jax.ShapeDtypeStruct((tile, width), jnp.float32),
            jax.ShapeDtypeStruct((tile, LANES), jnp.float32),
            jax.ShapeDtypeStruct((lat, tile), jnp.float32),
        ),
        in_specs=[SMEM] * 2 + [HBM] * 3 + [VMEM] * 5,
        out_specs=(VMEM,) * 6,
        scratch_shapes=[
            pltpu.VMEM(own.shape, own.dtype),
            pltpu.VMEM(other.shape, other.dtype),
            pltpu.VMEM(residual.shape, residual.dtype),
            pltpu.SemaphoreType.DMA((3,)),
        ],
        compiler_params=params(52),
    )(place, counts, own, other, residual, modulate, final_columns, noise, near, far)


def grad_kernel(
    place_ref, counts_ref, grad_columns_ref, normed_ref, inverse_ref, modulate_ref, final_ref, out_ref
):
    tile, width = normed_ref.shape
    first, _ = layout(place_ref, counts_ref, tile)
    gate, scale = (pick_rows(first, modulate_ref, at, width) for at in (0, 2))
    normed = normed_ref[...]
    grad_rows = grad_columns_ref[...].T.astype(jnp.bfloat16)
    grad_mixed = jnp.dot(grad_rows, final_ref[...], preferred_element_type=jnp.float32)
    grad_normed = grad_mixed * (1.0 + scale)
    across = normed * row_mean(grad_normed * normed)
    grad_hidden = inverse_ref[:, 0:1] * (grad_normed - row_mean(grad_normed) - across)
    out_ref[...] = (grad_hidden * gate).astype(jnp.bfloat16)


def grad_projected_of(place, counts, grad_columns, normed, inverse, modulate, final_columns):
    return pl.pallas_call(
        grad_kernel,
        out_shape=jax.ShapeDtypeStruct(normed.shape, jnp.bfloat16),
        in_specs=[SMEM] * 2 + [VMEM] * 5,
        out_specs=VMEM,
        compiler_params=params(20),
    )(place, counts, grad_columns, normed, inverse, modulate, final_columns)


def back_kernel(own_ref, other_ref, weight_ref, own_out_ref, other_out_ref, both_ref):
    tile = own_ref.shape[0]

    @pl.when(pl.program_id(0) == 0)
    def _():
        both_ref[:tile, :] = own_ref[...]
        both_ref[tile:, :] = other_ref[...]

    product = lax.dot_general(both_ref[...], weight_ref[...], NT, preferred_element_type=jnp.float32)
    own_out_ref[...] = product[:tile].astype(jnp.bfloat16)
    other_out_ref[...] = product[tile:].astype(jnp.bfloat16)


def back(own, other, weight):
    tile, width = own.shape
    depth = 2 * LANES
    out = jax.ShapeDtypeStruct((tile, weight.shape[0]), jnp.bfloat16)
    out_spec = pl.BlockSpec((tile, depth), lambda i: (0, i))
    return pl.pallas_call(
        back_kernel,
        grid=(weight.shape[0] // depth,),
        out_shape=(out, out),
        in_specs=[VMEM, VMEM, pl.BlockSpec((depth, width), lambda i: (i, 0))],
        out_specs=(out_spec, out_spec),
        scratch_shapes=[pltpu.VMEM((2 * tile, width), jnp.bfloat16)],
        compiler_params=params(24, ("arbitrary",)),
        cost_estimate=pl.CostEstimate(
            flops=4 * tile * width * weight.shape[0],
            bytes_accessed=2 * width * weight.shape[0],
            transcendentals=0,
        ),
    )(own, other, weight)


def join_kernel(half_ref, own_ref, other_ref, out_ref):
    depth = own_ref.shape[1]
    for half in range(2):

        @pl.when(half_ref[0] == half)
        def _():
            out_ref[:, half * depth : (half + 1) * depth] = own_ref[...]
            out_ref[:, (1 - half) * depth : (2 - half) * depth] = other_ref[...]


def join(half, own, other):
    return pl.pallas_call(
        join_kernel,
        out_shape=jax.ShapeDtypeStruct((own.shape[0], 2 * own.shape[1]), own.dtype),
        in_specs=[SMEM, VMEM, VMEM],
        out_specs=VMEM,
        compiler_params=params(16),
    )(half, own, other)


def sum_kernel(ranks, loss_row, last_ref, recv_ref, out_ref):
    rows = out_ref.shape[1]
    total = recv_ref[:rows, :].astype(jnp.float32)
    for rank in range(1, ranks):
        total += recv_ref[rank * rows : (rank + 1) * rows, :].astype(jnp.float32)
    loss = total[loss_row : loss_row + 1] + total[loss_row + 1 : loss_row + 2] + total[loss_row + 2 : loss_row + 3]
    row = lax.broadcasted_iota(jnp.int32, (rows, LANES), 0) - loss_row
    kept = thirds(loss, row)
    inside = jnp.logical_and(row >= 0, row < 3)
    changed = jnp.where(inside, kept.astype(jnp.float32), total)
    result = jnp.where(last_ref[0] == 1, changed, total).astype(jnp.bfloat16)
    for rank in range(out_ref.shape[0]):
        out_ref[rank] = result


def sum_out(recv, ranks, copies, loss_row, last):
    rows = recv.shape[0] // ranks
    result = pl.pallas_call(
        functools.partial(sum_kernel, ranks, loss_row),
        out_shape=jax.ShapeDtypeStruct((copies, rows, LANES), jnp.bfloat16),
        in_specs=[SMEM, VMEM],
        out_specs=VMEM,
        compiler_params=params(16),
    )(last, recv)
    return result.reshape(copies * rows, LANES)


def unpack_kernel(parts_ref, total_ref, out_ref, loss_ref):
    blocks, lat = parts_ref.shape[:2]
    for at in range(blocks - 1):
        out_ref[:, at * LANES : (at + 1) * LANES] = parts_ref[at].astype(jnp.float32)
    last = parts_ref[blocks - 1, :16, :].astype(jnp.float32)
    loss = last[0:1] + last[1:2] + last[2:3]
    loss_ref[...] = jnp.broadcast_to(loss, loss_ref.shape) / (total_ref[...] * lat)


def unpack(parts, total, width):
    return pl.pallas_call(
        unpack_kernel,
        out_shape=(
            jax.ShapeDtypeStruct((parts.shape[1], width), jnp.float32),
            jax.ShapeDtypeStruct((8, LANES), jnp.float32),
        ),
        in_specs=[VMEM, VMEM],
        out_specs=(VMEM, VMEM),
        compiler_params=params(16),
    )(parts, total)


def exchange(array, axis, groups=None):
    return lax.all_to_all(
        array, axis, split_axis=0, concat_axis=0, axis_index_groups=groups, tiled=True
    )


def per_device(
    near, latent_tiles, tile_route, image_tokens, text_lengths, queries, key_rows, values,
    text_keys, text_values, query_gain, key_gain, residual, out_weight, modulation, final_weight,
    noise_tiles,
):
    lat_width, tile = latent_tiles.shape[1:]
    rows_here, width = residual.shape
    text_rows = text_keys.shape[0]
    ranks, sources = lax.axis_size("dp"), lax.axis_size("seqt")
    far = ranks // near
    near_groups = [[row * near + at for at in range(near)] for row in range(far)]
    far_groups = [[row * near + at for row in range(far)] for at in range(near)]
    column_index = lax.axis_index("seqt").astype(jnp.int32)

    per_half = sources // 2
    halves = [[half * per_half + at for at in range(per_half)] for half in range(2)]
    place = column_index.reshape(1)
    half = (column_index // per_half).reshape(1)

    gathered = lax.all_gather(out_weight, "seqt", axis=0, axis_index_groups=halves, tiled=True)
    sent, tagged = pack(
        (queries, key_rows, values, text_keys, text_values), sources, latent_tiles, tile_route, image_tokens
    )
    recv = exchange(sent, "seqt")
    bits = [1 << at for at in range(ranks.bit_length() - 1)]
    held = gather(tagged, ranks, [bit for bit in reversed(bits) if bit < near])
    recv, _ = lax.optimization_barrier((recv, held))
    held = gather(held, ranks, [bit for bit in bits[:-1] if bit >= near])
    heads = attention(
        recv, image_tokens, text_lengths, query_gain, key_gain, sources, tile, text_rows
    )
    heads, held = lax.optimization_barrier((heads, held))
    attended = exchange(heads, "seqt", halves)
    mine, other = land(held, tagged.shape[0], ranks)
    attended, mine, other = lax.optimization_barrier((attended, mine, other))
    final_columns = final_weight.T
    own, across = project(half, attended, gathered, tile)
    across = swap(across, sources, per_half, "seqt")
    velocity, parts, total, normed, inverse, grad_columns = head(
        place, image_tokens, own, across, residual, modulation, final_columns, noise_tiles[0],
        mine, other,
    )
    grad_projected = grad_projected_of(
        place, image_tokens, grad_columns, normed, inverse, modulation, final_columns
    )
    blocks = parts.shape[0]
    share = blocks * lat_width // sources
    loss_row = (blocks - 1) * lat_width - (sources - 1) * share
    last = (column_index == sources - 1).astype(jnp.int32).reshape(1)
    partner_grad = swap(grad_projected, sources, per_half, "seqt")
    own_grad, across_grad = back(grad_projected, partner_grad, gathered)
    swapped_grad = swap(across_grad, sources, per_half, "seqt")
    sums = exchange(parts.reshape(blocks * lat_width, LANES), "seqt")
    sums, _ = lax.optimization_barrier((sums, grad_projected))
    sums = exchange(sum_out(sums, sources, near, loss_row, last), "dp", near_groups)
    sums = exchange(sum_out(sums, near, far, loss_row, last), "dp", far_groups)
    sums, _ = lax.optimization_barrier((sums, across_grad))
    sums = exchange(sum_out(sums, far, sources, loss_row, last), "seqt")
    attention_grad = join(half, own_grad, swapped_grad)
    final_sums, loss = unpack(sums.reshape(blocks, lat_width, LANES), total, width)
    return velocity[None], attention_grad, final_sums.T, loss[0, 0]


def solution(mesh):
    both = P(("dp", "seqt"), None)
    tiles = P(("dp", "seqt"), None, None)
    placed = (
        tiles, P(("dp", "seqt")), P("dp", None), P("dp", None), both, both, both, both, both,
        P(), P(), both, P("seqt", None), P("dp", None), P(), tiles,
    )
    near = 8 if mesh.shape["dp"] % 8 == 0 else mesh.shape["dp"]
    return jax.shard_map(
        functools.partial(per_device, near),
        mesh=mesh,
        in_specs=placed,
        out_specs=(tiles, both, P(), P()),
        check_vma=False,
    )
```

```python
import functools

import jax
import jax.numpy as jnp
from jax import lax
from jax.experimental import pallas as pl
from jax.experimental.pallas import tpu as pltpu
from jax.sharding import PartitionSpec as P

HD = 64
IMGS = 2
LANES = 128
Q_ROWS = 256
NOTES = 16
EPSILON = 1e-06
HBM = pl.BlockSpec(memory_space=pltpu.HBM)
VMEM = pl.BlockSpec(memory_space=pltpu.VMEM)
SMEM = pl.BlockSpec(memory_space=pltpu.SMEM)
NT = (((1,), (1,)), ((), ()))


def params(limit_mib, semantics=None):
    return pltpu.CompilerParams(
        vmem_limit_bytes=limit_mib * 2**20, dimension_semantics=semantics
    )


def pack_kernel(parts, count, route_ref, counts_ref, tile_ref, *refs):
    ins, (out_ref, tagged_ref, lined_ref, in_semaphores, out_semaphore) = refs[:count], refs[count:]
    block_rows = sum(ref.shape[0] for ref in ins)
    for part in range(parts):
        row = part * block_rows
        for ref in ins:
            rows = ref.shape[0]
            pltpu.make_async_copy(
                ref.at[:, pl.ds(part * LANES, LANES)],
                lined_ref.at[pl.ds(row, rows), :],
                in_semaphores.at[part],
            ).start()
            row += rows
    lat = tile_ref.shape[1]
    tokens = counts_ref[0, 0] + counts_ref[0, 1]
    tagged_ref[:lat, :] = tile_ref[0]
    tagged_ref[lat:, :] = notes(route_ref[0], tokens // 16, tokens % 16)
    for part in range(parts):
        here = lined_ref.at[pl.ds(part * block_rows, block_rows), :]
        pltpu.make_async_copy(here, here, in_semaphores.at[part]).wait()
        there = out_ref.at[pl.ds(part * block_rows, block_rows), :]
        pltpu.make_async_copy(here, there, out_semaphore).start()
    pltpu.make_async_copy(lined_ref, out_ref, out_semaphore).wait()


def notes(first, second, third):
    places = lax.broadcasted_iota(jnp.int32, (NOTES, LANES), 0)
    third_or_none = jnp.where(places == 2, third, 0)
    numbers = jnp.where(places == 0, first, jnp.where(places == 1, second, third_or_none))
    return numbers.astype(jnp.float32).astype(jnp.bfloat16)


def pack(arrays, parts, tile, route, counts):
    block_rows = sum(array.shape[0] for array in arrays)
    return pl.pallas_call(
        functools.partial(pack_kernel, parts, len(arrays)),
        out_shape=(
            jax.ShapeDtypeStruct((parts * block_rows, LANES), arrays[0].dtype),
            jax.ShapeDtypeStruct((tile.shape[1] + NOTES, LANES), tile.dtype),
        ),
        in_specs=[SMEM, SMEM, VMEM] + [HBM] * len(arrays),
        out_specs=(HBM, VMEM),
        scratch_shapes=[
            pltpu.VMEM((parts * block_rows, LANES), arrays[0].dtype),
            pltpu.SemaphoreType.DMA((parts,)),
            pltpu.SemaphoreType.DMA,
        ],
        compiler_params=params(60),
    )(route, counts, tile, *arrays)


def select_kernel(last, me_ref, *refs):
    ins, out_ref = refs[:-1], refs[-1]
    rows = out_ref.shape[1]
    lat = rows - NOTES
    tokens = jnp.zeros((1, 1), jnp.float32)
    mine = jnp.zeros((lat, LANES), jnp.float32)
    other = jnp.zeros((lat, LANES), jnp.float32)
    me = me_ref[0].astype(jnp.float32)
    beside = (me_ref[0] ^ last).astype(jnp.float32)
    for ref in ins:
        for at in range(0, ref.shape[0], rows):
            tile = ref[at : at + lat, :].astype(jnp.float32)
            note = ref[at + lat : at + rows, :].astype(jnp.float32)
            route = note[0:1, 0:1]
            mine += jnp.where(route == me, tile, 0.0)
            other += jnp.where(route == beside, tile, 0.0)
            tokens += note[1:2, 0:1] * 16.0 + note[2:3, 0:1]
    high = jnp.floor(tokens * (1.0 / 128.0))
    places = lax.broadcasted_iota(jnp.int32, (NOTES, LANES), 0)
    number = jnp.where(places == 1, high, jnp.where(places == 2, tokens - high * 128.0, 0.0))
    for half, tile in enumerate((mine, other)):
        out_ref[half, :lat, :] = tile.astype(jnp.bfloat16)
        out_ref[half, lat:, :] = number.astype(jnp.bfloat16)


def gather(held, ranks, bits):
    for bit in bits:
        held = jnp.concatenate([held, swap(held, ranks, bit)], axis=0)
    return held


def land(held, rows, ranks):
    bit = max(ranks // 2, 1)
    chosen = pl.pallas_call(
        functools.partial(select_kernel, bit),
        out_shape=jax.ShapeDtypeStruct((2, rows, LANES), held.dtype),
        in_specs=[SMEM, VMEM],
        out_specs=VMEM,
        compiler_params=params(16),
    )(lax.axis_index("dp").astype(jnp.int32).reshape(1), held)
    return chosen[0], swap(chosen[1], ranks, bit) if bit < ranks else jnp.zeros_like(chosen[1])


def swap(array, ranks, step, axis="dp"):
    return lax.ppermute(array, axis, [(rank, rank ^ step) for rank in range(ranks)])


def head_norm(rows, gain, same_head):
    wide = rows.astype(jnp.float32)
    square = wide * wide
    high = square.astype(jnp.bfloat16)
    low = (square - high.astype(jnp.float32)).astype(jnp.bfloat16)
    total = jnp.dot(high, same_head, preferred_element_type=jnp.float32) + jnp.dot(
        low, same_head, preferred_element_type=jnp.float32
    )
    return (wide * lax.rsqrt(total * (1.0 / HD) + EPSILON) * gain).astype(jnp.bfloat16)


def attention_kernel(
    sources, tile, text_rows, counts_ref, lengths_ref, recv_ref, query_gain_ref, key_gain_ref,
    out_ref, query_ref, key_ref, value_ref, window_ref, weigh_ref,
):
    rows_all = sources * tile
    text_slots = sources * text_rows // IMGS
    window = rows_all // IMGS
    block = 3 * tile + 2 * text_rows
    per_image = sources // IMGS
    first_count = counts_ref[0, 0]
    second_count = counts_ref[0, 1]
    border = pl.multiple_of((first_count + tile - 1) // tile * tile, tile)
    head_row = lax.broadcasted_iota(jnp.int32, (LANES, LANES), 0) // HD
    head_column = lax.broadcasted_iota(jnp.int32, (LANES, LANES), 1) // HD
    same_head = (head_row == head_column).astype(jnp.float32).astype(jnp.bfloat16)
    query_gain = query_gain_ref[...]
    key_gain = key_gain_ref[...]
    for source in range(sources):
        at, row = source * block, source * tile
        key = head_norm(recv_ref[at + tile : at + 2 * tile, :], key_gain, same_head)
        key_ref[row : row + tile, :] = key
        if row < window:
            window_ref[0, row : row + tile, :] = key
        value_ref[row : row + tile, :] = recv_ref[at + 2 * tile : at + 3 * tile, :]
        query = head_norm(recv_ref[at : at + tile, :], query_gain, same_head)
        query_ref[row : row + tile, :] = query * jnp.bfloat16(HD**-0.5)
        image, place = source // per_image, window + source % per_image * text_rows
        text = recv_ref[at + 3 * tile : at + 3 * tile + text_rows, :]
        window_ref[image, place : place + text_rows, :] = head_norm(text, key_gain, same_head)
    window_ref[1, :window, :] = key_ref[pl.ds(border, window), :]

    def weighed(values, used, image, start, rows):
        low = lax.broadcasted_iota(jnp.int32, (rows, LANES), 1) < HD
        kept = lax.broadcasted_iota(jnp.int32, (rows, LANES), 0) < used
        wide = jnp.where(kept, values.astype(jnp.float32), 0.0)
        ones = kept.astype(jnp.float32)
        weigh_ref[image, 0, start : start + rows, :] = jnp.where(low, wide, ones).astype(jnp.bfloat16)
        weigh_ref[image, 1, start : start + rows, :] = jnp.where(low, ones, wide).astype(jnp.bfloat16)

    for image in range(IMGS):
        used = counts_ref[0, image]
        for start in range(0, window, tile):
            begin = start if image == 0 else pl.multiple_of(border + start, tile)
            weighed(value_ref[pl.ds(begin, tile), :], used - start, image, start, tile)
        text = jnp.concatenate(
            [
                recv_ref[s * block + 3 * tile + text_rows : (s + 1) * block, :]
                for s in range(image * per_image, (image + 1) * per_image)
            ],
            axis=0,
        )
        weighed(text, lengths_ref[0, image], image, window, text_slots)

    low = lax.broadcasted_iota(jnp.int32, (Q_ROWS, LANES), 1) < HD

    def rows_of(image, start):
        query = query_ref[pl.ds(start, Q_ROWS), :].astype(jnp.float32)
        sums = []
        for head in range(2):
            own = jnp.where(low == (head == 0), query, 0.0).astype(jnp.bfloat16)
            scores = lax.dot_general(own, window_ref[image], NT, preferred_element_type=jnp.float32)
            weights = jnp.exp(scores).astype(jnp.bfloat16)
            sums.append(jnp.dot(weights, weigh_ref[image, head], preferred_element_type=jnp.float32))
        above = jnp.where(low, sums[0], sums[1])
        below = pltpu.roll(jnp.where(low, sums[1], sums[0]), HD, 1)
        result = (above / below).astype(jnp.bfloat16)
        for part in range(Q_ROWS // tile):
            at = start // tile + part
            place = (lax.rem(at, per_image) * IMGS + lax.div(at, per_image)) * tile
            out_ref[pl.ds(pl.multiple_of(place, tile), tile), :] = result[part * tile : (part + 1) * tile]

    @pl.loop(0, (border + Q_ROWS - 1) // Q_ROWS)
    def _(step):
        rows_of(0, pl.multiple_of(step * Q_ROWS, tile))

    @pl.loop(0, (rows_all - border + Q_ROWS - 1) // Q_ROWS)
    def _(step):
        rows_of(1, pl.multiple_of(jnp.minimum(border + step * Q_ROWS, rows_all - Q_ROWS), tile))


def attention(recv, counts, lengths, query_gain, key_gain, sources, tile, text_rows):
    rows_all = sources * tile
    keys = rows_all // IMGS + sources * text_rows // IMGS
    twice = lambda gain: jnp.concatenate([gain, gain]).reshape(1, LANES)
    return pl.pallas_call(
        functools.partial(attention_kernel, sources, tile, text_rows),
        out_shape=jax.ShapeDtypeStruct((rows_all, LANES), jnp.bfloat16),
        in_specs=[SMEM, SMEM, VMEM, VMEM, VMEM],
        out_specs=VMEM,
        scratch_shapes=[
            pltpu.VMEM((rows_all, LANES), jnp.bfloat16),
            pltpu.VMEM((rows_all, LANES), jnp.bfloat16),
            pltpu.VMEM((rows_all, LANES), jnp.bfloat16),
            pltpu.VMEM((IMGS, keys, LANES), jnp.bfloat16),
            pltpu.VMEM((IMGS, 2, keys, LANES), jnp.bfloat16),
        ],
        compiler_params=params(32),
        cost_estimate=pl.CostEstimate(
            flops=16 * rows_all * keys * LANES,
            bytes_accessed=4 * rows_all * LANES * 4,
            transcendentals=2 * rows_all * keys,
        ),
    )(counts, lengths, recv, twice(query_gain), twice(key_gain))


def thirds(number, row):
    high = number.astype(jnp.bfloat16).astype(jnp.float32)
    middle = (number - high).astype(jnp.bfloat16).astype(jnp.float32)
    low = number - high - middle
    rest = jnp.where(row == 1, middle, jnp.where(row == 2, low, 0.0))
    return jnp.where(row == 0, high, rest).astype(jnp.bfloat16)


def pick_rows(first, modulate_ref, at, width):
    columns = pl.ds(at * width, width)
    return jnp.where(first, modulate_ref[0:1, columns], modulate_ref[1:2, columns])


def row_mean(array):
    return jnp.sum(array, axis=-1, keepdims=True) * (1.0 / array.shape[1])


def layout(place_ref, counts_ref, tile):
    place = place_ref[0] * tile
    border = (counts_ref[0, 0] + tile - 1) // tile * tile
    first = place < border
    return first, jnp.where(first, counts_ref[0, 0], border + counts_ref[0, 1]) - place


def project_kernel(
    block, begin, half_ref, rows_ref, weight_ref, own_ref, other_ref, lined_ref, here_ref, semaphores
):
    tile, width = own_ref.shape
    whole = width // block

    def landing(at, size):
        there = pl.ds(pl.multiple_of(begin + at * block, LANES), size)
        here = pl.ds(pl.multiple_of(at * block, LANES), size)
        return pltpu.make_async_copy(weight_ref.at[:, there], here_ref.at[:, here], semaphores.at[at])

    sizes = [block] * whole + ([width % block] if width % block else [])
    for at, size in enumerate(sizes):
        landing(at, size).start()
    for at in range(lined_ref.shape[1] // LANES):
        rows = rows_ref[at * 2 * tile : (at + 1) * 2 * tile, :]
        lined_ref[:, at * LANES : (at + 1) * LANES] = rows
    first = half_ref[0] == 0

    def multiply(at, size):
        landing(at, size).wait()
        columns = pl.ds(pl.multiple_of(at * block, block), size)
        product = jnp.dot(lined_ref[...], here_ref[:, columns], preferred_element_type=jnp.float32)
        own_ref[:, columns] = jnp.where(first, product[:tile], product[tile:])
        other = jnp.where(first, product[tile:], product[:tile])
        other_ref[:, columns] = other.astype(jnp.bfloat16)

    @pl.loop(0, whole)
    def _(at):
        multiply(at, block)

    if width % block:
        multiply(whole, width % block)


def project(half, recv, weight, tile, begin, width):
    depth = weight.shape[0]
    block = 4 * LANES
    return pl.pallas_call(
        functools.partial(project_kernel, block, begin),
        out_shape=(
            jax.ShapeDtypeStruct((tile, width), jnp.float32),
            jax.ShapeDtypeStruct((tile, width), jnp.bfloat16),
        ),
        in_specs=[SMEM, VMEM, HBM],
        out_specs=(VMEM, VMEM),
        scratch_shapes=[
            pltpu.VMEM((2 * tile, depth), jnp.bfloat16),
            pltpu.VMEM((depth, width), jnp.bfloat16),
            pltpu.SemaphoreType.DMA((pl.cdiv(width, block),)),
        ],
        compiler_params=params(52),
        cost_estimate=pl.CostEstimate(
            flops=4 * tile * depth * width, bytes_accessed=2 * depth * width, transcendentals=0
        ),
    )(half, recv, weight)


def head_kernel(
    place_ref, counts_ref, own_left_ref, own_right_ref, other_left_ref, other_right_ref,
    residual_ref, modulate_ref, final_ref, noise_ref, near_ref, far_ref, velocity_ref, parts_ref, total_ref, normed_ref, inverse_ref, grad_ref,
    own_here, other_here, residual_here, semaphores,
):
    left = pl.ds(0, own_left_ref.shape[1])
    right = pl.ds(own_left_ref.shape[1], own_right_ref.shape[1])
    pairs = (
        (own_left_ref, own_here.at[:, left]),
        (own_right_ref, own_here.at[:, right]),
        (residual_ref, residual_here),
        (other_left_ref, other_here.at[:, left]),
        (other_right_ref, other_here.at[:, right]),
    )
    copies = [
        pltpu.make_async_copy(there, here, semaphores.at[at]) for at, (there, here) in enumerate(pairs)
    ]
    for copy in copies:
        copy.start()
    tile, width = residual_ref.shape
    lat = final_ref.shape[0]
    first, used_rows = layout(place_ref, counts_ref, tile)
    total = jnp.zeros((1, 1), jnp.float32)
    for ref in (near_ref, far_ref):
        note = ref[lat:, :].astype(jnp.float32)
        total += note[1:2, 0:1] * 128.0 + note[2:3, 0:1]
    total_ref[...] = jnp.broadcast_to(total, total_ref.shape)
    gate, shift, scale = (pick_rows(first, modulate_ref, at, width) for at in range(3))
    for copy in copies:
        copy.wait()
    projected = own_here[...] + other_here[...].astype(jnp.float32)
    hidden = residual_here[...].astype(jnp.float32) + gate * projected
    centered = hidden - row_mean(hidden)
    inverse = lax.rsqrt(row_mean(centered * centered) + EPSILON)
    normed = centered * inverse
    normed_ref[...] = normed
    inverse_ref[...] = jnp.broadcast_to(inverse, inverse_ref.shape)
    mixed = (normed * (1.0 + scale) + shift).astype(jnp.bfloat16)
    velocity = lax.dot_general(final_ref[...], mixed, NT, preferred_element_type=jnp.float32)
    velocity_ref[...] = velocity
    landed = near_ref[:lat, :].astype(jnp.float32) + far_ref[:lat, :].astype(jnp.float32)
    target = noise_ref[...].astype(jnp.float32) - landed
    used = lax.broadcasted_iota(jnp.int32, (lat, tile), 1) < used_rows
    error = jnp.where(used, velocity - target, 0.0)
    grad_wide = error * (2.0 / (total * lat))
    grad_columns = grad_wide.astype(jnp.bfloat16)
    grad_ref[...] = grad_wide
    final_part = jnp.dot(grad_columns, mixed, preferred_element_type=jnp.float32)
    for at in range(width // LANES):
        parts_ref[at] = final_part[:, at * LANES : (at + 1) * LANES].astype(jnp.bfloat16)
    squares = jnp.sum(error * error, axis=(0, 1), keepdims=True)
    parts_ref[width // LANES] = thirds(squares, lax.broadcasted_iota(jnp.int32, (lat, LANES), 0))


def head(place, counts, own, other, residual, modulate, final_columns, noise, near, far):
    tile, width = residual.shape
    lat = final_columns.shape[0]
    blocks = width // LANES + 1
    return pl.pallas_call(
        head_kernel,
        out_shape=(
            jax.ShapeDtypeStruct((lat, tile), jnp.float32),
            jax.ShapeDtypeStruct((blocks, lat, LANES), jnp.bfloat16),
            jax.ShapeDtypeStruct((8, LANES), jnp.float32),
            jax.ShapeDtypeStruct((tile, width), jnp.float32),
            jax.ShapeDtypeStruct((tile, LANES), jnp.float32),
            jax.ShapeDtypeStruct((lat, tile), jnp.float32),
        ),
        in_specs=[SMEM] * 2 + [pl.BlockSpec(memory_space=pl.ANY)] * 5 + [VMEM] * 5,
        out_specs=(VMEM,) * 6,
        scratch_shapes=[
            pltpu.VMEM(residual.shape, own[0].dtype),
            pltpu.VMEM(residual.shape, other[0].dtype),
            pltpu.VMEM(residual.shape, residual.dtype),
            pltpu.SemaphoreType.DMA((5,)),
        ],
        compiler_params=params(52),
    )(place, counts, *own, *other, residual, modulate, final_columns, noise, near, far)


def grad_kernel(
    place_ref, counts_ref, grad_columns_ref, normed_ref, inverse_ref, modulate_ref, final_ref, out_ref
):
    tile, width = normed_ref.shape
    first, _ = layout(place_ref, counts_ref, tile)
    gate, scale = (pick_rows(first, modulate_ref, at, width) for at in (0, 2))
    normed = normed_ref[...]
    grad_rows = grad_columns_ref[...].T.astype(jnp.bfloat16)
    grad_mixed = jnp.dot(grad_rows, final_ref[...], preferred_element_type=jnp.float32)
    grad_normed = grad_mixed * (1.0 + scale)
    across = normed * row_mean(grad_normed * normed)
    grad_hidden = inverse_ref[:, 0:1] * (grad_normed - row_mean(grad_normed) - across)
    out_ref[...] = (grad_hidden * gate).astype(jnp.bfloat16)


def grad_projected_of(place, counts, grad_columns, normed, inverse, modulate, final_columns):
    return pl.pallas_call(
        grad_kernel,
        out_shape=jax.ShapeDtypeStruct(normed.shape, jnp.bfloat16),
        in_specs=[SMEM] * 2 + [VMEM] * 5,
        out_specs=VMEM,
        compiler_params=params(20),
    )(place, counts, grad_columns, normed, inverse, modulate, final_columns)


def back_kernel(own_ref, other_ref, weight_ref, own_out_ref, other_out_ref, both_ref):
    tile = own_ref.shape[0]

    @pl.when(pl.program_id(0) == 0)
    def _():
        both_ref[:tile, :] = own_ref[...]
        both_ref[tile:, :] = other_ref[...]

    product = lax.dot_general(both_ref[...], weight_ref[...], NT, preferred_element_type=jnp.float32)
    own_out_ref[...] = product[:tile].astype(jnp.bfloat16)
    other_out_ref[...] = product[tile:].astype(jnp.bfloat16)


def back(own, other, weight):
    tile, width = own.shape
    depth = 2 * LANES
    out = jax.ShapeDtypeStruct((tile, weight.shape[0]), jnp.bfloat16)
    out_spec = pl.BlockSpec((tile, depth), lambda i: (0, i))
    return pl.pallas_call(
        back_kernel,
        grid=(weight.shape[0] // depth,),
        out_shape=(out, out),
        in_specs=[VMEM, VMEM, pl.BlockSpec((depth, width), lambda i: (i, 0))],
        out_specs=(out_spec, out_spec),
        scratch_shapes=[pltpu.VMEM((2 * tile, width), jnp.bfloat16)],
        compiler_params=params(24, ("arbitrary",)),
        cost_estimate=pl.CostEstimate(
            flops=4 * tile * width * weight.shape[0],
            bytes_accessed=2 * width * weight.shape[0],
            transcendentals=0,
        ),
    )(own, other, weight)


def join_kernel(half_ref, own_ref, other_ref, out_ref):
    depth = own_ref.shape[1]
    for half in range(2):

        @pl.when(half_ref[0] == half)
        def _():
            out_ref[:, half * depth : (half + 1) * depth] = own_ref[...]
            out_ref[:, (1 - half) * depth : (2 - half) * depth] = other_ref[...]


def join(half, own, other):
    return pl.pallas_call(
        join_kernel,
        out_shape=jax.ShapeDtypeStruct((own.shape[0], 2 * own.shape[1]), own.dtype),
        in_specs=[SMEM, VMEM, VMEM],
        out_specs=VMEM,
        compiler_params=params(16),
    )(half, own, other)


def sum_kernel(ranks, loss_row, last_ref, recv_ref, out_ref):
    rows = out_ref.shape[1]
    total = recv_ref[:rows, :].astype(jnp.float32)
    for rank in range(1, ranks):
        total += recv_ref[rank * rows : (rank + 1) * rows, :].astype(jnp.float32)
    loss = total[loss_row : loss_row + 1] + total[loss_row + 1 : loss_row + 2] + total[loss_row + 2 : loss_row + 3]
    row = lax.broadcasted_iota(jnp.int32, (rows, LANES), 0) - loss_row
    kept = thirds(loss, row)
    inside = jnp.logical_and(row >= 0, row < 3)
    changed = jnp.where(inside, kept.astype(jnp.float32), total)
    result = jnp.where(last_ref[0] == 1, changed, total).astype(jnp.bfloat16)
    for rank in range(out_ref.shape[0]):
        out_ref[rank] = result


def sum_out(recv, ranks, copies, loss_row, last):
    rows = recv.shape[0] // ranks
    result = pl.pallas_call(
        functools.partial(sum_kernel, ranks, loss_row),
        out_shape=jax.ShapeDtypeStruct((copies, rows, LANES), jnp.bfloat16),
        in_specs=[SMEM, VMEM],
        out_specs=VMEM,
        compiler_params=params(16),
    )(last, recv)
    return result.reshape(copies * rows, LANES)


def unpack_kernel(parts_ref, total_ref, out_ref, loss_ref):
    blocks, lat = parts_ref.shape[:2]
    for at in range(blocks - 1):
        out_ref[:, at * LANES : (at + 1) * LANES] = parts_ref[at].astype(jnp.float32)
    last = parts_ref[blocks - 1, :16, :].astype(jnp.float32)
    loss = last[0:1] + last[1:2] + last[2:3]
    loss_ref[...] = jnp.broadcast_to(loss, loss_ref.shape) / (total_ref[...] * lat)


def unpack(parts, total, width):
    return pl.pallas_call(
        unpack_kernel,
        out_shape=(
            jax.ShapeDtypeStruct((parts.shape[1], width), jnp.float32),
            jax.ShapeDtypeStruct((8, LANES), jnp.float32),
        ),
        in_specs=[VMEM, VMEM],
        out_specs=(VMEM, VMEM),
        compiler_params=params(16),
    )(parts, total)


def exchange(array, axis, groups=None):
    return lax.all_to_all(
        array, axis, split_axis=0, concat_axis=0, axis_index_groups=groups, tiled=True
    )


def per_device(
    near, latent_tiles, tile_route, image_tokens, text_lengths, queries, key_rows, values,
    text_keys, text_values, query_gain, key_gain, residual, out_weight, modulation, final_weight,
    noise_tiles,
):
    lat_width, tile = latent_tiles.shape[1:]
    rows_here, width = residual.shape
    text_rows = text_keys.shape[0]
    ranks, sources = lax.axis_size("dp"), lax.axis_size("seqt")
    far = ranks // near
    near_groups = [[row * near + at for at in range(near)] for row in range(far)]
    far_groups = [[row * near + at for row in range(far)] for at in range(near)]
    column_index = lax.axis_index("seqt").astype(jnp.int32)

    per_half = sources // 2
    halves = [[half * per_half + at for at in range(per_half)] for half in range(2)]
    place = column_index.reshape(1)
    half = (column_index // per_half).reshape(1)

    gathered = lax.all_gather(out_weight, "seqt", axis=0, axis_index_groups=halves, tiled=True)
    sent, tagged = pack(
        (queries, key_rows, values, text_keys, text_values), sources, latent_tiles, tile_route, image_tokens
    )
    recv = exchange(sent, "seqt")
    bits = [1 << at for at in range(ranks.bit_length() - 1)]
    held = gather(tagged, ranks, [bit for bit in reversed(bits) if bit < near])
    recv, _ = lax.optimization_barrier((recv, held))
    held = gather(held, ranks, [bit for bit in bits[:-1] if bit >= near])
    heads = attention(
        recv, image_tokens, text_lengths, query_gain, key_gain, sources, tile, text_rows
    )
    heads, held = lax.optimization_barrier((heads, held))
    attended = exchange(heads, "seqt", halves)
    mine, other = land(held, tagged.shape[0], ranks)
    attended, mine, other = lax.optimization_barrier((attended, mine, other))
    final_columns = final_weight.T
    left = pl.cdiv(width, 2 * LANES) * LANES
    own, across = [], []
    for begin, size in ((0, left), (left, width - left)):
        here, there = project(half, attended, gathered, tile, begin, size)
        own.append(here)
        across.append(swap(there, sources, per_half, "seqt"))
    velocity, parts, total, normed, inverse, grad_columns = head(
        place, image_tokens, own, across, residual, modulation, final_columns, noise_tiles[0],
        mine, other,
    )
    grad_projected = grad_projected_of(
        place, image_tokens, grad_columns, normed, inverse, modulation, final_columns
    )
    blocks = parts.shape[0]
    share = blocks * lat_width // sources
    loss_row = (blocks - 1) * lat_width - (sources - 1) * share
    last = (column_index == sources - 1).astype(jnp.int32).reshape(1)
    partner_grad = swap(grad_projected, sources, per_half, "seqt")
    own_grad, across_grad = back(grad_projected, partner_grad, gathered)
    swapped_grad = swap(across_grad, sources, per_half, "seqt")
    sums = exchange(parts.reshape(blocks * lat_width, LANES), "seqt")
    sums, _ = lax.optimization_barrier((sums, grad_projected))
    sums = exchange(sum_out(sums, sources, near, loss_row, last), "dp", near_groups)
    sums, _ = lax.optimization_barrier((sums, across_grad))
    sums = exchange(sum_out(sums, near, far, loss_row, last), "dp", far_groups)
    sums, _ = lax.optimization_barrier((sums, swapped_grad))
    sums = exchange(sum_out(sums, far, sources, loss_row, last), "seqt")
    attention_grad = join(half, own_grad, swapped_grad)
    final_sums, loss = unpack(sums.reshape(blocks, lat_width, LANES), total, width)
    return velocity[None], attention_grad, final_sums.T, loss[0, 0]


def solution(mesh):
    both = P(("dp", "seqt"), None)
    tiles = P(("dp", "seqt"), None, None)
    placed = (
        tiles, P(("dp", "seqt")), P("dp", None), P("dp", None), both, both, both, both, both,
        P(), P(), both, P("seqt", None), P("dp", None), P(), tiles,
    )
    near = 8 if mesh.shape["dp"] % 8 == 0 else mesh.shape["dp"]
    return jax.shard_map(
        functools.partial(per_device, near),
        mesh=mesh,
        in_specs=placed,
        out_specs=(tiles, both, P(), P()),
        check_vma=False,
    )
```

```python
import functools

import jax
import jax.numpy as jnp
from jax import lax
from jax.experimental import pallas as pl
from jax.experimental.pallas import tpu as pltpu
from jax.sharding import PartitionSpec as P

HD = 64
IMGS = 2
LANES = 128
Q_ROWS = 256
NOTES = 16
EPSILON = 1e-06
HBM = pl.BlockSpec(memory_space=pltpu.HBM)
VMEM = pl.BlockSpec(memory_space=pltpu.VMEM)
SMEM = pl.BlockSpec(memory_space=pltpu.SMEM)
NT = (((1,), (1,)), ((), ()))


def params(limit_mib, semantics=None):
    return pltpu.CompilerParams(
        vmem_limit_bytes=limit_mib * 2**20, dimension_semantics=semantics
    )


def pack_kernel(parts, count, route_ref, counts_ref, tile_ref, *refs):
    ins, (out_ref, tagged_ref, lined_ref, in_semaphores, out_semaphore) = refs[:count], refs[count:]
    block_rows = sum(ref.shape[0] for ref in ins)
    for part in range(parts):
        row = part * block_rows
        for ref in ins:
            rows = ref.shape[0]
            pltpu.make_async_copy(
                ref.at[:, pl.ds(part * LANES, LANES)],
                lined_ref.at[pl.ds(row, rows), :],
                in_semaphores.at[part],
            ).start()
            row += rows
    lat = tile_ref.shape[1]
    tokens = counts_ref[0, 0] + counts_ref[0, 1]
    tagged_ref[:lat, :] = tile_ref[0]
    tagged_ref[lat:, :] = notes(route_ref[0], tokens // 16, tokens % 16)
    for part in range(parts):
        here = lined_ref.at[pl.ds(part * block_rows, block_rows), :]
        pltpu.make_async_copy(here, here, in_semaphores.at[part]).wait()
        there = out_ref.at[pl.ds(part * block_rows, block_rows), :]
        pltpu.make_async_copy(here, there, out_semaphore).start()
    pltpu.make_async_copy(lined_ref, out_ref, out_semaphore).wait()


def notes(first, second, third):
    places = lax.broadcasted_iota(jnp.int32, (NOTES, LANES), 0)
    third_or_none = jnp.where(places == 2, third, 0)
    numbers = jnp.where(places == 0, first, jnp.where(places == 1, second, third_or_none))
    return numbers.astype(jnp.float32).astype(jnp.bfloat16)


def pack(arrays, parts, tile, route, counts):
    block_rows = sum(array.shape[0] for array in arrays)
    return pl.pallas_call(
        functools.partial(pack_kernel, parts, len(arrays)),
        out_shape=(
            jax.ShapeDtypeStruct((parts * block_rows, LANES), arrays[0].dtype),
            jax.ShapeDtypeStruct((tile.shape[1] + NOTES, LANES), tile.dtype),
        ),
        in_specs=[SMEM, SMEM, VMEM] + [HBM] * len(arrays),
        out_specs=(HBM, VMEM),
        scratch_shapes=[
            pltpu.VMEM((parts * block_rows, LANES), arrays[0].dtype),
            pltpu.SemaphoreType.DMA((parts,)),
            pltpu.SemaphoreType.DMA,
        ],
        compiler_params=params(60),
    )(route, counts, tile, *arrays)


def select_kernel(last, me_ref, *refs):
    ins, out_ref = refs[:-1], refs[-1]
    rows = out_ref.shape[1]
    lat = rows - NOTES
    tokens = jnp.zeros((1, 1), jnp.float32)
    mine = jnp.zeros((lat, LANES), jnp.float32)
    other = jnp.zeros((lat, LANES), jnp.float32)
    me = me_ref[0].astype(jnp.float32)
    beside = (me_ref[0] ^ last).astype(jnp.float32)
    for ref in ins:
        for at in range(0, ref.shape[0], rows):
            tile = ref[at : at + lat, :].astype(jnp.float32)
            note = ref[at + lat : at + rows, :].astype(jnp.float32)
            route = note[0:1, 0:1]
            mine += jnp.where(route == me, tile, 0.0)
            other += jnp.where(route == beside, tile, 0.0)
            tokens += note[1:2, 0:1] * 16.0 + note[2:3, 0:1]
    high = jnp.floor(tokens * (1.0 / 128.0))
    places = lax.broadcasted_iota(jnp.int32, (NOTES, LANES), 0)
    number = jnp.where(places == 1, high, jnp.where(places == 2, tokens - high * 128.0, 0.0))
    for half, tile in enumerate((mine, other)):
        out_ref[half, :lat, :] = tile.astype(jnp.bfloat16)
        out_ref[half, lat:, :] = number.astype(jnp.bfloat16)


def gather(held, ranks, bits):
    for bit in bits:
        held = jnp.concatenate([held, swap(held, ranks, bit)], axis=0)
    return held


def land(held, rows, ranks):
    bit = max(ranks // 2, 1)
    chosen = pl.pallas_call(
        functools.partial(select_kernel, bit),
        out_shape=jax.ShapeDtypeStruct((2, rows, LANES), held.dtype),
        in_specs=[SMEM, VMEM],
        out_specs=VMEM,
        compiler_params=params(16),
    )(lax.axis_index("dp").astype(jnp.int32).reshape(1), held)
    return chosen[0], swap(chosen[1], ranks, bit) if bit < ranks else jnp.zeros_like(chosen[1])


def swap(array, ranks, step, axis="dp"):
    return lax.ppermute(array, axis, [(rank, rank ^ step) for rank in range(ranks)])


def head_norm(rows, gain, same_head):
    wide = rows.astype(jnp.float32)
    square = wide * wide
    high = square.astype(jnp.bfloat16)
    low = (square - high.astype(jnp.float32)).astype(jnp.bfloat16)
    total = jnp.dot(high, same_head, preferred_element_type=jnp.float32) + jnp.dot(
        low, same_head, preferred_element_type=jnp.float32
    )
    return (wide * lax.rsqrt(total * (1.0 / HD) + EPSILON) * gain).astype(jnp.bfloat16)


def attention_kernel(
    sources, tile, text_rows, counts_ref, lengths_ref, recv_ref, query_gain_ref, key_gain_ref,
    out_ref, query_ref, key_ref, value_ref, window_ref, weigh_ref,
):
    rows_all = sources * tile
    text_slots = sources * text_rows // IMGS
    window = rows_all // IMGS
    block = 3 * tile + 2 * text_rows
    per_image = sources // IMGS
    first_count = counts_ref[0, 0]
    second_count = counts_ref[0, 1]
    border = pl.multiple_of((first_count + tile - 1) // tile * tile, tile)
    head_row = lax.broadcasted_iota(jnp.int32, (LANES, LANES), 0) // HD
    head_column = lax.broadcasted_iota(jnp.int32, (LANES, LANES), 1) // HD
    same_head = (head_row == head_column).astype(jnp.float32).astype(jnp.bfloat16)
    query_gain = query_gain_ref[...]
    key_gain = key_gain_ref[...]
    for source in range(sources):
        at, row = source * block, source * tile
        key = head_norm(recv_ref[at + tile : at + 2 * tile, :], key_gain, same_head)
        key_ref[row : row + tile, :] = key
        if row < window:
            window_ref[0, row : row + tile, :] = key
        value_ref[row : row + tile, :] = recv_ref[at + 2 * tile : at + 3 * tile, :]
        query = head_norm(recv_ref[at : at + tile, :], query_gain, same_head)
        query_ref[row : row + tile, :] = query * jnp.bfloat16(HD**-0.5)
        image, place = source // per_image, window + source % per_image * text_rows
        text = recv_ref[at + 3 * tile : at + 3 * tile + text_rows, :]
        window_ref[image, place : place + text_rows, :] = head_norm(text, key_gain, same_head)
    window_ref[1, :window, :] = key_ref[pl.ds(border, window), :]

    def weighed(values, used, image, start, rows):
        low = lax.broadcasted_iota(jnp.int32, (rows, LANES), 1) < HD
        kept = lax.broadcasted_iota(jnp.int32, (rows, LANES), 0) < used
        wide = jnp.where(kept, values.astype(jnp.float32), 0.0)
        ones = kept.astype(jnp.float32)
        weigh_ref[image, 0, start : start + rows, :] = jnp.where(low, wide, ones).astype(jnp.bfloat16)
        weigh_ref[image, 1, start : start + rows, :] = jnp.where(low, ones, wide).astype(jnp.bfloat16)

    for image in range(IMGS):
        used = counts_ref[0, image]
        for start in range(0, window, tile):
            begin = start if image == 0 else pl.multiple_of(border + start, tile)
            weighed(value_ref[pl.ds(begin, tile), :], used - start, image, start, tile)
        text = jnp.concatenate(
            [
                recv_ref[s * block + 3 * tile + text_rows : (s + 1) * block, :]
                for s in range(image * per_image, (image + 1) * per_image)
            ],
            axis=0,
        )
        weighed(text, lengths_ref[0, image], image, window, text_slots)

    low = lax.broadcasted_iota(jnp.int32, (Q_ROWS, LANES), 1) < HD

    def rows_of(image, start):
        query = query_ref[pl.ds(start, Q_ROWS), :].astype(jnp.float32)
        sums = []
        for head in range(2):
            own = jnp.where(low == (head == 0), query, 0.0).astype(jnp.bfloat16)
            scores = lax.dot_general(own, window_ref[image], NT, preferred_element_type=jnp.float32)
            weights = jnp.exp(scores).astype(jnp.bfloat16)
            sums.append(jnp.dot(weights, weigh_ref[image, head], preferred_element_type=jnp.float32))
        above = jnp.where(low, sums[0], sums[1])
        below = pltpu.roll(jnp.where(low, sums[1], sums[0]), HD, 1)
        result = (above / below).astype(jnp.bfloat16)
        for part in range(Q_ROWS // tile):
            at = start // tile + part
            place = (lax.rem(at, per_image) * IMGS + lax.div(at, per_image)) * tile
            out_ref[pl.ds(pl.multiple_of(place, tile), tile), :] = result[part * tile : (part + 1) * tile]

    @pl.loop(0, (border + Q_ROWS - 1) // Q_ROWS)
    def _(step):
        rows_of(0, pl.multiple_of(step * Q_ROWS, tile))

    @pl.loop(0, (rows_all - border + Q_ROWS - 1) // Q_ROWS)
    def _(step):
        rows_of(1, pl.multiple_of(jnp.minimum(border + step * Q_ROWS, rows_all - Q_ROWS), tile))


def attention(recv, counts, lengths, query_gain, key_gain, sources, tile, text_rows):
    rows_all = sources * tile
    keys = rows_all // IMGS + sources * text_rows // IMGS
    twice = lambda gain: jnp.concatenate([gain, gain]).reshape(1, LANES)
    return pl.pallas_call(
        functools.partial(attention_kernel, sources, tile, text_rows),
        out_shape=jax.ShapeDtypeStruct((rows_all, LANES), jnp.bfloat16),
        in_specs=[SMEM, SMEM, VMEM, VMEM, VMEM],
        out_specs=VMEM,
        scratch_shapes=[
            pltpu.VMEM((rows_all, LANES), jnp.bfloat16),
            pltpu.VMEM((rows_all, LANES), jnp.bfloat16),
            pltpu.VMEM((rows_all, LANES), jnp.bfloat16),
            pltpu.VMEM((IMGS, keys, LANES), jnp.bfloat16),
            pltpu.VMEM((IMGS, 2, keys, LANES), jnp.bfloat16),
        ],
        compiler_params=params(32),
        cost_estimate=pl.CostEstimate(
            flops=16 * rows_all * keys * LANES,
            bytes_accessed=4 * rows_all * LANES * 4,
            transcendentals=2 * rows_all * keys,
        ),
    )(counts, lengths, recv, twice(query_gain), twice(key_gain))


def thirds(number, row):
    high = number.astype(jnp.bfloat16).astype(jnp.float32)
    middle = (number - high).astype(jnp.bfloat16).astype(jnp.float32)
    low = number - high - middle
    rest = jnp.where(row == 1, middle, jnp.where(row == 2, low, 0.0))
    return jnp.where(row == 0, high, rest).astype(jnp.bfloat16)


def pick_rows(first, modulate_ref, at, width):
    columns = pl.ds(at * width, width)
    return jnp.where(first, modulate_ref[0:1, columns], modulate_ref[1:2, columns])


def row_mean(array):
    return jnp.sum(array, axis=-1, keepdims=True) * (1.0 / array.shape[1])


def layout(place_ref, counts_ref, tile):
    place = place_ref[0] * tile
    border = (counts_ref[0, 0] + tile - 1) // tile * tile
    first = place < border
    return first, jnp.where(first, counts_ref[0, 0], border + counts_ref[0, 1]) - place


def project_kernel(
    block, begin, half_ref, rows_ref, weight_ref, own_ref, other_ref, lined_ref, here_ref, semaphores
):
    tile, width = own_ref.shape
    whole = width // block

    def landing(at, size):
        there = pl.ds(pl.multiple_of(begin + at * block, LANES), size)
        here = pl.ds(pl.multiple_of(at * block, LANES), size)
        return pltpu.make_async_copy(weight_ref.at[:, there], here_ref.at[:, here], semaphores.at[at])

    sizes = [block] * whole + ([width % block] if width % block else [])
    for at, size in enumerate(sizes):
        landing(at, size).start()
    for at in range(lined_ref.shape[1] // LANES):
        rows = rows_ref[at * 2 * tile : (at + 1) * 2 * tile, :]
        lined_ref[:, at * LANES : (at + 1) * LANES] = rows
    first = half_ref[0] == 0

    def multiply(at, size):
        landing(at, size).wait()
        columns = pl.ds(pl.multiple_of(at * block, block), size)
        product = jnp.dot(lined_ref[...], here_ref[:, columns], preferred_element_type=jnp.float32)
        own_ref[:, columns] = jnp.where(first, product[:tile], product[tile:])
        other = jnp.where(first, product[tile:], product[:tile])
        other_ref[:, columns] = other.astype(jnp.bfloat16)

    @pl.loop(0, whole)
    def _(at):
        multiply(at, block)

    if width % block:
        multiply(whole, width % block)


def project(half, recv, weight, tile, begin, width):
    depth = weight.shape[0]
    block = 4 * LANES
    return pl.pallas_call(
        functools.partial(project_kernel, block, begin),
        out_shape=(
            jax.ShapeDtypeStruct((tile, width), jnp.float32),
            jax.ShapeDtypeStruct((tile, width), jnp.bfloat16),
        ),
        in_specs=[SMEM, VMEM, HBM],
        out_specs=(VMEM, VMEM),
        scratch_shapes=[
            pltpu.VMEM((2 * tile, depth), jnp.bfloat16),
            pltpu.VMEM((depth, width), jnp.bfloat16),
            pltpu.SemaphoreType.DMA((pl.cdiv(width, block),)),
        ],
        compiler_params=params(52),
        cost_estimate=pl.CostEstimate(
            flops=4 * tile * depth * width, bytes_accessed=2 * depth * width, transcendentals=0
        ),
    )(half, recv, weight)


def head_kernel(
    place_ref, counts_ref, own_left_ref, own_right_ref, other_left_ref, other_right_ref,
    residual_ref, modulate_ref, final_ref, noise_ref, near_ref, far_ref, velocity_ref, parts_ref, total_ref, normed_ref, inverse_ref, grad_ref,
    own_here, other_here, residual_here, semaphores,
):
    left = pl.ds(0, own_left_ref.shape[1])
    right = pl.ds(own_left_ref.shape[1], own_right_ref.shape[1])
    pairs = (
        (own_left_ref, own_here.at[:, left]),
        (own_right_ref, own_here.at[:, right]),
        (residual_ref, residual_here),
        (other_left_ref, other_here.at[:, left]),
        (other_right_ref, other_here.at[:, right]),
    )
    copies = [
        pltpu.make_async_copy(there, here, semaphores.at[at]) for at, (there, here) in enumerate(pairs)
    ]
    for copy in copies:
        copy.start()
    tile, width = residual_ref.shape
    lat = final_ref.shape[0]
    first, used_rows = layout(place_ref, counts_ref, tile)
    total = jnp.zeros((1, 1), jnp.float32)
    for ref in (near_ref, far_ref):
        note = ref[lat:, :].astype(jnp.float32)
        total += note[1:2, 0:1] * 128.0 + note[2:3, 0:1]
    total_ref[...] = jnp.broadcast_to(total, total_ref.shape)
    gate, shift, scale = (pick_rows(first, modulate_ref, at, width) for at in range(3))
    for copy in copies:
        copy.wait()
    projected = own_here[...] + other_here[...].astype(jnp.float32)
    hidden = residual_here[...].astype(jnp.float32) + gate * projected
    centered = hidden - row_mean(hidden)
    inverse = lax.rsqrt(row_mean(centered * centered) + EPSILON)
    normed = centered * inverse
    normed_ref[...] = normed
    inverse_ref[...] = jnp.broadcast_to(inverse, inverse_ref.shape)
    mixed = (normed * (1.0 + scale) + shift).astype(jnp.bfloat16)
    velocity = lax.dot_general(final_ref[...], mixed, NT, preferred_element_type=jnp.float32)
    velocity_ref[...] = velocity
    landed = near_ref[:lat, :].astype(jnp.float32) + far_ref[:lat, :].astype(jnp.float32)
    target = noise_ref[...].astype(jnp.float32) - landed
    used = lax.broadcasted_iota(jnp.int32, (lat, tile), 1) < used_rows
    error = jnp.where(used, velocity - target, 0.0)
    grad_wide = error * (2.0 / (total * lat))
    grad_columns = grad_wide.astype(jnp.bfloat16)
    grad_ref[...] = grad_wide
    final_part = jnp.dot(grad_columns, mixed, preferred_element_type=jnp.float32)
    for at in range(width // LANES):
        parts_ref[at] = final_part[:, at * LANES : (at + 1) * LANES].astype(jnp.bfloat16)
    squares = jnp.sum(error * error, axis=(0, 1), keepdims=True)
    parts_ref[width // LANES] = thirds(squares, lax.broadcasted_iota(jnp.int32, (lat, LANES), 0))


def head(place, counts, own, other, residual, modulate, final_columns, noise, near, far):
    tile, width = residual.shape
    lat = final_columns.shape[0]
    blocks = width // LANES + 1
    return pl.pallas_call(
        head_kernel,
        out_shape=(
            jax.ShapeDtypeStruct((lat, tile), jnp.float32),
            jax.ShapeDtypeStruct((blocks, lat, LANES), jnp.bfloat16),
            jax.ShapeDtypeStruct((8, LANES), jnp.float32),
            jax.ShapeDtypeStruct((tile, width), jnp.float32),
            jax.ShapeDtypeStruct((tile, LANES), jnp.float32),
            jax.ShapeDtypeStruct((lat, tile), jnp.float32),
        ),
        in_specs=[SMEM] * 2 + [pl.BlockSpec(memory_space=pl.ANY)] * 5 + [VMEM] * 5,
        out_specs=(VMEM,) * 6,
        scratch_shapes=[
            pltpu.VMEM(residual.shape, own[0].dtype),
            pltpu.VMEM(residual.shape, other[0].dtype),
            pltpu.VMEM(residual.shape, residual.dtype),
            pltpu.SemaphoreType.DMA((5,)),
        ],
        compiler_params=params(52),
    )(place, counts, *own, *other, residual, modulate, final_columns, noise, near, far)


def grad_kernel(
    place_ref, counts_ref, grad_columns_ref, normed_ref, inverse_ref, modulate_ref, final_ref, out_ref
):
    tile, width = normed_ref.shape
    first, _ = layout(place_ref, counts_ref, tile)
    gate, scale = (pick_rows(first, modulate_ref, at, width) for at in (0, 2))
    normed = normed_ref[...]
    grad_rows = grad_columns_ref[...].T.astype(jnp.bfloat16)
    grad_mixed = jnp.dot(grad_rows, final_ref[...], preferred_element_type=jnp.float32)
    grad_normed = grad_mixed * (1.0 + scale)
    across = normed * row_mean(grad_normed * normed)
    grad_hidden = inverse_ref[:, 0:1] * (grad_normed - row_mean(grad_normed) - across)
    out_ref[...] = (grad_hidden * gate).astype(jnp.bfloat16)


def grad_projected_of(place, counts, grad_columns, normed, inverse, modulate, final_columns):
    return pl.pallas_call(
        grad_kernel,
        out_shape=jax.ShapeDtypeStruct(normed.shape, jnp.bfloat16),
        in_specs=[SMEM] * 2 + [VMEM] * 5,
        out_specs=VMEM,
        compiler_params=params(20),
    )(place, counts, grad_columns, normed, inverse, modulate, final_columns)


def back_kernel(grad_ref, weight_ref, out_ref):
    product = lax.dot_general(grad_ref[...], weight_ref[...], NT, preferred_element_type=jnp.float32)
    out_ref[...] = product.astype(jnp.bfloat16)


def back(grad, weight):
    tile, width = grad.shape
    depth = 2 * LANES
    return pl.pallas_call(
        back_kernel,
        grid=(weight.shape[0] // depth,),
        out_shape=jax.ShapeDtypeStruct((tile, weight.shape[0]), jnp.bfloat16),
        in_specs=[VMEM, pl.BlockSpec((depth, width), lambda i: (i, 0))],
        out_specs=pl.BlockSpec((tile, depth), lambda i: (0, i)),
        compiler_params=params(24, ("arbitrary",)),
        cost_estimate=pl.CostEstimate(
            flops=2 * tile * width * weight.shape[0],
            bytes_accessed=2 * width * weight.shape[0],
            transcendentals=0,
        ),
    )(grad, weight)


def join_kernel(half_ref, own_ref, other_ref, out_ref):
    depth = own_ref.shape[1]
    for half in range(2):

        @pl.when(half_ref[0] == half)
        def _():
            out_ref[:, half * depth : (half + 1) * depth] = own_ref[...]
            out_ref[:, (1 - half) * depth : (2 - half) * depth] = other_ref[...]


def join(half, own, other):
    return pl.pallas_call(
        join_kernel,
        out_shape=jax.ShapeDtypeStruct((own.shape[0], 2 * own.shape[1]), own.dtype),
        in_specs=[SMEM, VMEM, VMEM],
        out_specs=VMEM,
        compiler_params=params(16),
    )(half, own, other)


def sum_kernel(ranks, loss_row, last_ref, recv_ref, out_ref):
    rows = out_ref.shape[1]
    total = recv_ref[:rows, :].astype(jnp.float32)
    for rank in range(1, ranks):
        total += recv_ref[rank * rows : (rank + 1) * rows, :].astype(jnp.float32)
    loss = total[loss_row : loss_row + 1] + total[loss_row + 1 : loss_row + 2] + total[loss_row + 2 : loss_row + 3]
    row = lax.broadcasted_iota(jnp.int32, (rows, LANES), 0) - loss_row
    kept = thirds(loss, row)
    inside = jnp.logical_and(row >= 0, row < 3)
    changed = jnp.where(inside, kept.astype(jnp.float32), total)
    result = jnp.where(last_ref[0] == 1, changed, total).astype(jnp.bfloat16)
    for rank in range(out_ref.shape[0]):
        out_ref[rank] = result


def sum_out(recv, ranks, copies, loss_row, last):
    rows = recv.shape[0] // ranks
    result = pl.pallas_call(
        functools.partial(sum_kernel, ranks, loss_row),
        out_shape=jax.ShapeDtypeStruct((copies, rows, LANES), jnp.bfloat16),
        in_specs=[SMEM, VMEM],
        out_specs=VMEM,
        compiler_params=params(16),
    )(last, recv)
    return result.reshape(copies * rows, LANES)


def unpack_kernel(parts_ref, total_ref, out_ref, loss_ref):
    blocks, lat = parts_ref.shape[:2]
    for at in range(blocks - 1):
        out_ref[:, at * LANES : (at + 1) * LANES] = parts_ref[at].astype(jnp.float32)
    last = parts_ref[blocks - 1, :16, :].astype(jnp.float32)
    loss = last[0:1] + last[1:2] + last[2:3]
    loss_ref[...] = jnp.broadcast_to(loss, loss_ref.shape) / (total_ref[...] * lat)


def unpack(parts, total, width):
    return pl.pallas_call(
        unpack_kernel,
        out_shape=(
            jax.ShapeDtypeStruct((parts.shape[1], width), jnp.float32),
            jax.ShapeDtypeStruct((8, LANES), jnp.float32),
        ),
        in_specs=[VMEM, VMEM],
        out_specs=(VMEM, VMEM),
        compiler_params=params(16),
    )(parts, total)


def exchange(array, axis, groups=None):
    return lax.all_to_all(
        array, axis, split_axis=0, concat_axis=0, axis_index_groups=groups, tiled=True
    )


def per_device(
    near, latent_tiles, tile_route, image_tokens, text_lengths, queries, key_rows, values,
    text_keys, text_values, query_gain, key_gain, residual, out_weight, modulation, final_weight,
    noise_tiles,
):
    lat_width, tile = latent_tiles.shape[1:]
    rows_here, width = residual.shape
    text_rows = text_keys.shape[0]
    ranks, sources = lax.axis_size("dp"), lax.axis_size("seqt")
    far = ranks // near
    near_groups = [[row * near + at for at in range(near)] for row in range(far)]
    far_groups = [[row * near + at for row in range(far)] for at in range(near)]
    column_index = lax.axis_index("seqt").astype(jnp.int32)

    per_half = sources // 2
    halves = [[half * per_half + at for at in range(per_half)] for half in range(2)]
    place = column_index.reshape(1)
    half = (column_index // per_half).reshape(1)

    gathered = lax.all_gather(out_weight, "seqt", axis=0, axis_index_groups=halves, tiled=True)
    sent, tagged = pack(
        (queries, key_rows, values, text_keys, text_values), sources, latent_tiles, tile_route, image_tokens
    )
    recv = exchange(sent, "seqt")
    bits = [1 << at for at in range(ranks.bit_length() - 1)]
    held = gather(tagged, ranks, [bit for bit in reversed(bits) if bit < near])
    recv, _ = lax.optimization_barrier((recv, held))
    held = gather(held, ranks, [bit for bit in bits[:-1] if bit >= near])
    heads = attention(
        recv, image_tokens, text_lengths, query_gain, key_gain, sources, tile, text_rows
    )
    heads, held = lax.optimization_barrier((heads, held))
    attended = exchange(heads, "seqt", halves)
    mine, other = land(held, tagged.shape[0], ranks)
    attended, mine, other = lax.optimization_barrier((attended, mine, other))
    final_columns = final_weight.T
    left = pl.cdiv(width, 2 * LANES) * LANES
    own, across = [], []
    for begin, size in ((0, left), (left, width - left)):
        here, there = project(half, attended, gathered, tile, begin, size)
        own.append(here)
        across.append(swap(there, sources, per_half, "seqt"))
    velocity, parts, total, normed, inverse, grad_columns = head(
        place, image_tokens, own, across, residual, modulation, final_columns, noise_tiles[0],
        mine, other,
    )
    grad_projected = grad_projected_of(
        place, image_tokens, grad_columns, normed, inverse, modulation, final_columns
    )
    blocks = parts.shape[0]
    share = blocks * lat_width // sources
    loss_row = (blocks - 1) * lat_width - (sources - 1) * share
    last = (column_index == sources - 1).astype(jnp.int32).reshape(1)
    partner_grad = swap(grad_projected, sources, per_half, "seqt")
    own_grad = back(grad_projected, gathered)
    own_grad, partner_grad = lax.optimization_barrier((own_grad, partner_grad))
    across_grad = back(partner_grad, gathered)
    swapped_grad = swap(across_grad, sources, per_half, "seqt")
    sums = exchange(parts.reshape(blocks * lat_width, LANES), "seqt")
    sums, _ = lax.optimization_barrier((sums, grad_projected))
    sums = exchange(sum_out(sums, sources, near, loss_row, last), "dp", near_groups)
    sums, _ = lax.optimization_barrier((sums, across_grad))
    sums = exchange(sum_out(sums, near, far, loss_row, last), "dp", far_groups)
    sums, _ = lax.optimization_barrier((sums, swapped_grad))
    sums = exchange(sum_out(sums, far, sources, loss_row, last), "seqt")
    attention_grad = join(half, own_grad, swapped_grad)
    final_sums, loss = unpack(sums.reshape(blocks, lat_width, LANES), total, width)
    return velocity[None], attention_grad, final_sums.T, loss[0, 0]


def solution(mesh):
    both = P(("dp", "seqt"), None)
    tiles = P(("dp", "seqt"), None, None)
    placed = (
        tiles, P(("dp", "seqt")), P("dp", None), P("dp", None), both, both, both, both, both,
        P(), P(), both, P("seqt", None), P("dp", None), P(), tiles,
    )
    near = 8 if mesh.shape["dp"] % 8 == 0 else mesh.shape["dp"]
    return jax.shard_map(
        functools.partial(per_device, near),
        mesh=mesh,
        in_specs=placed,
        out_specs=(tiles, both, P(), P()),
        check_vma=False,
    )
```
